32 devices in a mesh: dp: 2 (over y), row: 4 (over z), col: 4 (over x, core).
Axes of the slice: x: 2, y: 2, z: 4, core: 2. Of those that a mesh axis runs over, the one named last changes fastest.
Arguments:
- tokens: bfloat16 [32768, 1024], P(('dp', 'col'), 'row'), may hold values from -6 to 6
- w_query: bfloat16 [1024, 1024], P('row', 'col'), may hold values from -0.1875 to 0.1875
- w_key: bfloat16 [1024, 1024], P('row', 'col'), may hold values from -0.1875 to 0.1875
- w_value: bfloat16 [1024, 1024], P('row', 'col'), may hold values from -0.1875 to 0.1875
- w_out: bfloat16 [1024, 1024], P('col', 'row'), may hold values from -0.75 to 0.75
- w_act: bfloat16 [1024, 2624], P('row', 'col'), may hold values from -0.1875 to 0.1875
- w_gate: bfloat16 [1024, 2624], P('row', 'col'), may hold values from -0.1875 to 0.1875
- w_down: bfloat16 [2624, 1024], P('col', 'row'), may hold values from -0.125 to 0.125
- gain_attn: bfloat16 [1024], P('row'), may hold values from 0.5 to 1.5
- gain_ffn: bfloat16 [1024], P('row'), may hold values from 0.5 to 1.5
- cotangent: bfloat16 [32768, 1024], P(('dp', 'col'), 'row'), may hold values from -6 to 6
- segment_ids: int32 [8, 4096], P(('dp', 'row')), may hold values from 0 to 63, never falling along the last dimension, each value on 1 to 1024 neighbouring positions
- valid_mask: int32 [8, 4096], P(('dp', 'row')), may hold values from 0 to 1, as said below
Outputs:
- layer_out: bfloat16 [32768, 1024], P(('dp', 'col'), 'row')
- token_gradient: float32 [32768, 1024], P(('dp', 'col'), 'row')
- grad_query: float32 [1024, 1024], P('row', 'col')
- grad_key: float32 [1024, 1024], P('row', 'col')
- grad_value: float32 [1024, 1024], P('row', 'col')
- grad_out: float32 [1024, 1024], P('col', 'row')
- grad_act: float32 [1024, 2624], P('row', 'col')
- grad_gate: float32 [1024, 2624], P('row', 'col')
- grad_down: float32 [2624, 1024], P('col', 'row')
- grad_gain_attn: float32 [1024], P('row')
- grad_gain_ffn: float32 [1024], P('row')
The draws below stay inside these ranges and needn't reach their ends.
Inputs may be any that keep to these rules, and one draw needn't show every extreme that they name: `valid_mask`: in each sequence the ones come first, then 1 to 512 zeros of padding.
All inputs are finite; a program needn't handle non-finite values.
Results may differ from the reference program's by a relative error of at most 0.015.
Values may be sent and summed in bfloat16 or wider, within the bound.
No kernel may reach another device: no remote copies, remote signals or barrier semaphores. Data moves between devices by JAX's collectives and lax.ppermute only.
A program may use at most 384 MiB of HBM per device.

```python
import math
import jax
import jax.numpy as jnp
import numpy as np
from jax import lax

MODEL_WIDTH = 1024
HEADS = 16
HEAD = 64
FF = 2624
WINDOW = 128
LENGTH = 4096
TOKENS = 32768
SEQS = 8


def draw_valid_mask(key, part):
    padding = jax.random.randint(key, (SEQS, 1), 1, LENGTH // 8 + 1)
    position_index = lax.broadcasted_iota(jnp.int32, (SEQS, LENGTH), 1)
    return (position_index < LENGTH - padding).astype(jnp.int32)


def level_of(rng, shape, shards, least, high):
    loudness = 1.0
    for dim, shards_of in shards:
        steps = jax.random.uniform(jax.random.fold_in(jax.random.fold_in(rng, 6), dim), (shards_of,), jnp.float32, least / len(shards), high / len(shards))
        loudness = loudness * jnp.repeat(jnp.exp(steps), shape[dim] // shards_of).reshape((-1,) + (1,) * (len(shape) - 1 - dim))
    return loudness


def split_up(number_of, total, most, skew):
    loads = [(1 << 20) // math.isqrt(grade ** skew) + 1 for grade in range(2, number_of + 1)]
    surplus, counts = total - most - (number_of - 1), [1] * (number_of - 1)
    while surplus > 0:
        movable = [i for i in range(number_of - 1) if counts[i] < most]
        pool, left = sum([loads[i] for i in movable]), surplus
        for i in movable:
            more = min(most - counts[i], max(1, left * loads[i] // pool), surplus)
            counts[i] = counts[i] + more
            surplus = surplus - more
    return np.array([most] + counts)


def uneven(key, number_of, total, limit, skew):
    if number_of == 2:
        one = jax.random.randint(key, (), max(1, total - limit), min(limit, total - 1) + 1)
        return jnp.stack([one, total - one])
    lengths = jnp.asarray(split_up(number_of, total, limit, skew), jnp.int32)
    pairs = (number_of - 1) // 2
    donor, sink = lengths[1:1 + 2 * pairs:2], lengths[2:2 + 2 * pairs:2]
    room = jnp.minimum(donor - 1, limit - sink)
    moved = jax.random.randint(jax.random.fold_in(key, 1), (pairs,), 0, 1 << 20) % (room + 1)
    lengths = lengths.at[1:1 + 2 * pairs:2].set(donor - moved).at[2:2 + 2 * pairs:2].set(sink + moved)
    return lengths[jax.random.permutation(jax.random.fold_in(key, 2), number_of)]


def bell_draw(key, extent, scale, limit, pieces=(), held_as=jnp.bfloat16):
    loudness = level_of(key, extent, pieces, -0.22, 0.18) if pieces else 1.0
    entries = jax.random.normal(key, extent, jnp.float32) * scale * loudness
    return jnp.minimum(jnp.maximum(entries, -limit), limit).astype(held_as)


def setup_inputs(seed: int = 0) -> dict:
    streams_of = jax.random.split(jax.random.key(seed), 14)
    tokens = bell_draw(streams_of[0], (TOKENS, MODEL_WIDTH), 1.0, 6.0, ((0, 8), (1, 4)))
    w_query = bell_draw(streams_of[1], (MODEL_WIDTH, MODEL_WIDTH), MODEL_WIDTH ** -0.5, 0.1875, ((0, 4), (1, 4)))
    w_key = bell_draw(streams_of[2], (MODEL_WIDTH, MODEL_WIDTH), MODEL_WIDTH ** -0.5, 0.1875, ((0, 4), (1, 4)))
    w_value = bell_draw(streams_of[3], (MODEL_WIDTH, MODEL_WIDTH), MODEL_WIDTH ** -0.5, 0.1875, ((0, 4), (1, 4)))
    w_out = bell_draw(streams_of[4], (MODEL_WIDTH, MODEL_WIDTH), (MODEL_WIDTH // 16) ** -0.5, 0.75, ((0, 4), (1, 4)))
    w_act = bell_draw(streams_of[5], (MODEL_WIDTH, FF), MODEL_WIDTH ** -0.5, 0.1875, ((0, 4), (1, 4)))
    w_gate = bell_draw(streams_of[6], (MODEL_WIDTH, FF), MODEL_WIDTH ** -0.5, 0.1875, ((0, 4), (1, 4)))
    w_down = bell_draw(streams_of[7], (FF, MODEL_WIDTH), FF ** -0.5, 0.125, ((0, 4), (1, 4)))
    gain_attn = jnp.clip(1.0 + 0.1 * jax.random.normal(streams_of[8], (MODEL_WIDTH,), jnp.float32), 0.5, 1.5).astype(jnp.bfloat16)
    gain_ffn = jnp.clip(1.0 + 0.1 * jax.random.normal(streams_of[9], (MODEL_WIDTH,), jnp.float32), 0.5, 1.5).astype(jnp.bfloat16)
    cotangent = bell_draw(streams_of[10], (TOKENS, MODEL_WIDTH), 1.0, 6.0, ((0, 8), (1, 4)))
    segment_ids = jax.vmap(lambda own: jnp.searchsorted(jnp.cumsum(uneven(own, LENGTH // 64, LENGTH, LENGTH // 4, 3)), jnp.arange(LENGTH), side="right"))(jax.random.split(streams_of[11], SEQS)).reshape((SEQS, LENGTH)).astype(jnp.int32)
    valid_mask = draw_valid_mask(jax.random.fold_in(streams_of[13], 71), 0)
    return {"tokens": tokens, "w_query": w_query, "w_key": w_key, "w_value": w_value, "w_out": w_out, "w_act": w_act, "w_gate": w_gate, "w_down": w_down, "gain_attn": gain_attn, "gain_ffn": gain_ffn, "cotangent": cotangent, "segment_ids": segment_ids, "valid_mask": valid_mask}


EPSILON = 1e-05
ROPE_THETA = 10000.0
MASKED_SCORE = -1e+30
HIGHEST = lax.Precision.HIGHEST

@jax.custom_vjp
def low(v):
    return lax.optimization_barrier(v.astype(jnp.bfloat16)).astype(jnp.float32)

@jax.custom_vjp
def low_back(v):
    return v

def low_keep(v):
    return (low(v), None)

def low_pass(kept, grad):
    return (grad,)

def back_keep(v):
    return (v, None)

def back_low(kept, grad):
    return (low(grad),)
low.defvjp(low_keep, low_pass)
low_back.defvjp(back_keep, back_low)

def product(left, right):
    return jnp.dot(left, right, precision=HIGHEST)

def apply_norm(values):
    average = lax.optimization_barrier(jnp.mean(values, axis=-1, keepdims=True))
    centered = values - average
    variance = lax.optimization_barrier(jnp.mean(centered * centered, axis=-1, keepdims=True))
    return centered * lax.rsqrt(variance + EPSILON)

def rotary(segments):
    position_index = lax.broadcasted_iota(jnp.int32, segments.shape, 1)
    starts = jnp.concatenate([jnp.ones_like(segments[:, :1]), (segments[:, 1:] != segments[:, :-1]).astype(jnp.int32)], axis=1)
    first_index = lax.cummax(jnp.where(starts == 1, position_index, 0), axis=1)
    where_in = (position_index - first_index).astype(jnp.float32).reshape(-1)
    frequency = ROPE_THETA ** (-(jnp.arange(HEAD // 2, dtype=jnp.float32) * 2.0) / HEAD)
    angles = where_in[:, None] * frequency[None, :]
    return (jnp.cos(angles)[:, None, :], jnp.sin(angles)[:, None, :])

def rotate_half(values, cosine, sine_table):
    half_size = values.shape[-1] // 2
    first_half = values[..., :half_size]
    second = values[..., half_size:]
    return jnp.concatenate([first_half * cosine - second * sine_table, second * cosine + first_half * sine_table], axis=-1)

def attend_sequence(inputs):
    query_rows, key_rows, value_rows, segments, valid = inputs
    half_window = WINDOW // 2
    block_rows = min(512, LENGTH)
    blocks = LENGTH // block_rows
    span_rows = block_rows + 2 * half_window
    spread = ((half_window, half_window), (0, 0), (0, 0))
    key_pad = jnp.pad(key_rows, spread)
    value_pad = jnp.pad(value_rows, spread)
    seg_pad = jnp.pad(segments, (half_window, half_window), constant_values=-1)
    valid_pad = jnp.pad(valid, (half_window, half_window))

    def one_block(block_index):
        first_row = block_index * block_rows
        q_block = lax.dynamic_slice_in_dim(query_rows, first_row, block_rows, 0)
        k_block = lax.dynamic_slice_in_dim(key_pad, first_row, span_rows, 0)
        v_block = lax.dynamic_slice_in_dim(value_pad, first_row, span_rows, 0)
        seg_query = lax.dynamic_slice_in_dim(seg_pad, first_row + half_window, block_rows, 0)
        seg_key = lax.dynamic_slice_in_dim(seg_pad, first_row, span_rows, 0)
        valid_key = lax.dynamic_slice_in_dim(valid_pad, first_row, span_rows, 0)
        offset = lax.broadcasted_iota(jnp.int32, (block_rows, span_rows), 1) - half_window - lax.broadcasted_iota(jnp.int32, (block_rows, span_rows), 0)
        allowed = (jnp.abs(offset) <= half_window) & (seg_query[:, None] == seg_key[None, :]) & ((valid_key[None, :] == 1) | (offset == 0))
        raw_scores = low_back(jnp.einsum('qhe,khe->hqk', q_block, k_block, precision=HIGHEST) * HEAD ** (-0.5))
        masked = jnp.where(allowed[None], raw_scores, MASKED_SCORE)
        row_max = lax.optimization_barrier(jnp.max(masked, axis=-1, keepdims=True))
        exponent = jnp.exp(masked - row_max)
        row_sum_total = lax.optimization_barrier(jnp.sum(exponent, axis=-1, keepdims=True))
        probability = low(exponent / row_sum_total)
        return jnp.einsum('hqk,khe->qhe', probability, v_block, precision=HIGHEST)
    outputs = lax.map(jax.checkpoint(one_block), jnp.arange(blocks, dtype=jnp.int32))
    return outputs.reshape(LENGTH, HEADS, HEAD)

def layer_forward(tokens, w_query, w_key, w_value, w_out, w_act, w_gate, w_down, gain_attn, gain_ffn, segments, valid, cosine, sine_table):
    attention_normed_input = low(apply_norm(tokens) * gain_attn)
    queries = low_back(product(attention_normed_input, w_query)).reshape(TOKENS, HEADS, HEAD)
    key_rows = low_back(product(attention_normed_input, w_key)).reshape(TOKENS, HEADS, HEAD)
    value_rows = low(low_back(product(attention_normed_input, w_value)))
    queries = low(rotate_half(queries, cosine, sine_table)).reshape(SEQS, LENGTH, HEADS, HEAD)
    key_rows = low(rotate_half(key_rows, cosine, sine_table)).reshape(SEQS, LENGTH, HEADS, HEAD)
    value_rows = value_rows.reshape(SEQS, LENGTH, HEADS, HEAD)
    attended = lax.map(jax.checkpoint(attend_sequence), (queries, key_rows, value_rows, segments, valid))
    attended = low(low_back(attended.reshape(TOKENS, MODEL_WIDTH)))
    residual_mixed_state = tokens + low_back(product(attended, w_out))
    feedforward_normed_input = low(apply_norm(residual_mixed_state) * gain_ffn)
    act_value = low_back(product(feedforward_normed_input, w_act))
    gate_value = low_back(product(feedforward_normed_input, w_gate))
    hidden = low(jax.nn.gelu(act_value, approximate=False) * gate_value)
    return residual_mixed_state + low_back(product(hidden, w_down))

def reference(tokens, w_query, w_key, w_value, w_out, w_act, w_gate, w_down, gain_attn, gain_ffn, cotangent, segment_ids, valid_mask):
    floats = tuple((item.astype(jnp.float32) for item in (tokens, w_query, w_key, w_value, w_out, w_act, w_gate, w_down, gain_attn, gain_ffn)))
    cosine, sine_table = rotary(segment_ids)

    def forward_only(*weights):
        return layer_forward(*weights, segment_ids, valid_mask, cosine, sine_table)
    result, pullback = jax.vjp(forward_only, *floats)
    gradient = pullback(cotangent.astype(jnp.float32))
    return (result.astype(jnp.bfloat16), gradient[0], gradient[1], gradient[2], gradient[3], gradient[4], gradient[5], gradient[6], gradient[7], gradient[8], gradient[9])
```

```python
import functools
import math

import jax
import jax.numpy as jnp
from jax import lax
from jax.experimental import pallas as pl
from jax.experimental.pallas import tpu as pltpu
from jax.sharding import PartitionSpec as P

WIDTH = 1024
HEAD = 64
REACH = 64
EPSILON = 1e-05
ROPE_THETA = 10000.0
MASKED_SCORE = -1e30
LANES = 128
SLOTS = 4
GROUPS = 4
GROUP = 256
TILE = 256
QUERY = 128
VMEM = 60 * 1024 * 1024
F32 = jnp.float32
BF16 = jnp.bfloat16


def nt(left, right):
    return lax.dot_general(left, right, (((1,), (1,)), ((), ())), preferred_element_type=F32)


def nn(left, right):
    return lax.dot_general(left, right, (((1,), (0,)), ((), ())), preferred_element_type=F32)


def tn(left, right):
    return lax.dot_general(left, right, (((0,), (0,)), ((), ())), preferred_element_type=F32)


def call(kernel, grid, in_specs, out_specs, out_shape, scratch, flops, moved, name):
    return pl.pallas_call(
        kernel,
        grid=grid,
        in_specs=in_specs,
        out_specs=out_specs,
        out_shape=out_shape,
        scratch_shapes=scratch,
        compiler_params=pltpu.CompilerParams(
            vmem_limit_bytes=VMEM, dimension_semantics=("arbitrary",)
        ),
        cost_estimate=pl.CostEstimate(flops=flops, bytes_accessed=moved, transcendentals=0),
        name=name,
    )


def resident(shape):
    zeros = (0,) * len(shape)
    return pl.BlockSpec(shape, lambda i: zeros, pipeline_mode=pl.Buffered(1))


def rows_of(width, tile=TILE):
    return pl.BlockSpec((tile, width), lambda i: (i, 0))


def struct(shape, dtype):
    return jax.ShapeDtypeStruct(shape, dtype)


def lane_block(a, o):
    return pl.ds(a * SLOTS * LANES + o * LANES, LANES)


def whole_rows(slots):
    return jnp.concatenate(
        [slots[o][:, a * LANES : (a + 1) * LANES] for a in range(2) for o in range(SLOTS)], axis=1
    )


def place(pieces, target, first, rows, start):
    for p in range(GROUPS):
        for a in range(2):
            for o in range(SLOTS):
                target[pl.ds(start + p * rows, rows), lane_block(a, o)] = pieces[a * GROUPS + p][
                    o, pl.ds(first, rows), :
                ]


def norm(values):
    average = jnp.mean(values, axis=1, keepdims=True)
    centered = values - average
    variance = jnp.mean(centered * centered, axis=1, keepdims=True)
    inverse = lax.rsqrt(variance + EPSILON)
    return centered * inverse, inverse


def norm_back(gradient, unit, inverse, gain):
    scaled = gradient * gain
    average = jnp.mean(scaled, axis=1, keepdims=True)
    crossed = jnp.mean(scaled * unit, axis=1, keepdims=True)
    return inverse * (scaled - average - unit * crossed)


def add_gain(gain_part, products):
    @pl.when(pl.program_id(0) == 0)
    def _():
        gain_part[...] = jnp.zeros_like(gain_part)

    gain_part[...] += jnp.sum(products.reshape(-1, 8, WIDTH), axis=0)


def qkv_kernel(*refs):
    xs, (gain, cosine, sine), pieces = refs[:4], refs[4:7], refs[7:15]
    q, k, v, normed, held = refs[15:]

    @pl.when(pl.program_id(0) == 0)
    def _():
        for t in range(3):
            place(pieces, held, t * GROUP, GROUP, t * WIDTH)

    unit, _ = norm(whole_rows(xs).astype(F32))
    rows = (unit * gain[...]).astype(BF16)
    normed[...] = rows
    c, s = cosine[...], sine[...]
    for t, out in ((0, q), (1, k)):
        made = nt(rows, held[pl.ds(t * WIDTH, WIDTH), :])
        for p in range(GROUPS):
            first = made[:, p * GROUP : p * GROUP + LANES]
            second = made[:, p * GROUP + LANES : (p + 1) * GROUP]
            out[:, p * GROUP : p * GROUP + LANES] = (first * c - second * s).astype(BF16)
            out[:, p * GROUP + LANES : (p + 1) * GROUP] = (second * c + first * s).astype(BF16)
    v[...] = nt(rows, held[pl.ds(2 * WIDTH, WIDTH), :]).astype(BF16)


def project(xs, gain, cosine, sine, pieces):
    tokens = cosine.shape[0]
    return call(
        qkv_kernel,
        (tokens // TILE,),
        [rows_of(256)] * 4
        + [resident((1, WIDTH)), rows_of(LANES), rows_of(LANES)]
        + [resident((SLOTS, 3 * GROUP, LANES))] * 8,
        [rows_of(WIDTH)] * 4,
        [struct((tokens, WIDTH), BF16)] * 4,
        [pltpu.VMEM((3 * WIDTH, WIDTH), BF16)],
        2 * tokens * WIDTH * 3 * WIDTH,
        10 * tokens * WIDTH + 6 * WIDTH * WIDTH,
        "project",
    )(*xs, gain, cosine, sine, *pieces)


def head_masks():
    lane = lax.broadcasted_iota(jnp.int32, (1, GROUP), 1)
    halves = [((lane % LANES) // 32 == h) for h in range(4)]
    wholes = [(lane // HEAD == h) for h in range(4)]
    return halves, wholes


def spread(rows, masks):
    return jnp.concatenate([rows * m.astype(BF16) for m in masks], axis=0)


def collect(stacked, masks):
    total = jnp.where(masks[0], stacked[0:QUERY], 0.0)
    for h in range(1, 4):
        total = jnp.where(masks[h], stacked[h * QUERY : (h + 1) * QUERY], total)
    return total


def fill_span(span, low, own, high):
    count = own.shape[0]
    span[0:REACH, :] = low
    span[pl.ds(REACH, count), :] = own[...]
    span[pl.ds(REACH + count, REACH), :] = high


def attend_kernel(q, k, v, low, high, seg_query, seg_key, attended, probability, keys, values):
    step = pl.program_id(0)

    @pl.when(step == 0)
    def _():
        fill_span(keys, low[:, :WIDTH], k, high[:, :WIDTH])
        fill_span(values, low[:, WIDTH:], v, high[:, WIDTH:])

    span = pl.ds(pl.multiple_of(step * QUERY, QUERY), QUERY + 2 * REACH)
    shape = (QUERY, QUERY + 2 * REACH)
    offset = (
        lax.broadcasted_iota(jnp.int32, shape, 1)
        - lax.broadcasted_iota(jnp.int32, shape, 0)
        - REACH
    )
    allowed = (jnp.abs(offset) <= REACH) & ((seg_query[...] == seg_key[0]) | (offset == 0))
    halves, wholes = head_masks()
    for p in range(GROUPS):
        lanes = slice(p * GROUP, (p + 1) * GROUP)
        stacked = spread(q[:, lanes], halves)
        scores = nt(stacked, keys[span, lanes]) * HEAD**-0.5
        scores = jnp.concatenate(
            [
                jnp.where(allowed, scores[h * QUERY : (h + 1) * QUERY], MASKED_SCORE)
                for h in range(4)
            ],
            axis=0,
        )
        exponent = jnp.exp(scores - jnp.max(scores, axis=1, keepdims=True))
        weight = (exponent * (1.0 / jnp.sum(exponent, axis=1, keepdims=True))).astype(BF16)
        probability[0, p] = weight
        attended[:, lanes] = collect(nn(weight, values[span, lanes]), wholes).astype(BF16)


def attend(q, k, v, low, high, seg_query, seg_key):
    tokens = q.shape[0]
    blocks = tokens // QUERY
    span = QUERY + 2 * REACH
    full = resident((tokens, WIDTH))
    return call(
        attend_kernel,
        (blocks,),
        [
            rows_of(WIDTH, QUERY),
            full,
            full,
            resident((REACH, 2 * WIDTH)),
            resident((REACH, 2 * WIDTH)),
            rows_of(1, QUERY),
            pl.BlockSpec((1, 1, span), lambda i: (i, 0, 0)),
        ],
        [
            rows_of(WIDTH, QUERY),
            pl.BlockSpec((1, GROUPS, 4 * QUERY, span), lambda i: (i, 0, 0, 0)),
        ],
        [
            struct((tokens, WIDTH), BF16),
            struct((blocks, GROUPS, 4 * QUERY, span), BF16),
        ],
        [pltpu.VMEM((tokens + 2 * REACH, WIDTH), BF16)] * 2,
        blocks * GROUPS * 2 * 2 * 4 * QUERY * span * GROUP,
        8 * tokens * WIDTH + blocks * GROUPS * 8 * QUERY * span,
        "attend",
    )(q, k, v, low, high, seg_query, seg_key)


def attend_back_kernel(*refs):
    q, grad, weights, k, v, low, high, cosine, sine = refs[:9]
    gq, gk, gv, edge_k, edge_v, keys, values, sum_k, sum_v, every_c, every_s = refs[9:]
    step, steps = pl.program_id(0), pl.num_programs(0)
    tokens = k.shape[0]

    @pl.when(step == 0)
    def _():
        fill_span(keys, low[:, :WIDTH], k, high[:, :WIDTH])
        fill_span(values, low[:, WIDTH:], v, high[:, WIDTH:])
        sum_k[...] = jnp.zeros_like(sum_k)
        sum_v[...] = jnp.zeros_like(sum_v)

    start = pl.multiple_of(step * QUERY, QUERY)
    span = pl.ds(start, QUERY + 2 * REACH)
    halves, wholes = head_masks()
    c, s = cosine[...], sine[...]
    every_c[pl.ds(start, QUERY), :] = c
    every_s[pl.ds(start, QUERY), :] = s
    for p in range(GROUPS):
        lanes = slice(p * GROUP, (p + 1) * GROUP)
        queries = spread(q[:, lanes], halves)
        grads = spread(grad[:, lanes], wholes)
        block_k, block_v = keys[span, lanes], values[span, lanes]
        weight = weights[0, p]
        wide = weight.astype(F32)
        d_weight = nt(grads, block_v)
        mean = jnp.sum(wide * d_weight, axis=1, keepdims=True)
        g_score = (wide * (d_weight - mean)).astype(BF16)
        made = collect(nn(g_score, block_k), halves) * HEAD**-0.5
        first, second = made[:, :LANES], made[:, LANES:]
        gq[:, p * GROUP : p * GROUP + LANES] = (first * c + second * s).astype(BF16)
        gq[:, p * GROUP + LANES : (p + 1) * GROUP] = (second * c - first * s).astype(BF16)
        sum_k[span, lanes] += tn(g_score, queries) * HEAD**-0.5
        sum_v[span, lanes] += tn(weight, grads)

    @pl.when(step == steps - 1)
    def _():
        for edge, total in ((edge_k, sum_k), (edge_v, sum_v)):
            edge[0 : 2 * REACH, :] = total[0 : 2 * REACH, :]
            edge[2 * REACH :, :] = total[pl.ds(tokens, 2 * REACH), :]
        for at in range(0, tokens, QUERY):
            own = pl.ds(REACH + at, QUERY)
            c, s = every_c[pl.ds(at, QUERY), :], every_s[pl.ds(at, QUERY), :]
            for p in range(GROUPS):
                one, two = p * GROUP, p * GROUP + LANES
                first, second = sum_k[own, pl.ds(one, LANES)], sum_k[own, pl.ds(two, LANES)]
                gk[pl.ds(at, QUERY), pl.ds(one, LANES)] = (first * c + second * s).astype(BF16)
                gk[pl.ds(at, QUERY), pl.ds(two, LANES)] = (second * c - first * s).astype(BF16)
            gv[pl.ds(at, QUERY), :] = sum_v[own, :].astype(BF16)


def attend_back(q, grad, weights, k, v, low, high, cosine, sine):
    tokens = q.shape[0]
    blocks = tokens // QUERY
    span = QUERY + 2 * REACH
    full = resident((tokens, WIDTH))
    edge = resident((4 * REACH, WIDTH))
    return call(
        attend_back_kernel,
        (blocks,),
        [
            rows_of(WIDTH, QUERY),
            rows_of(WIDTH, QUERY),
            pl.BlockSpec((1, GROUPS, 4 * QUERY, span), lambda i: (i, 0, 0, 0)),
            full,
            full,
            resident((REACH, 2 * WIDTH)),
            resident((REACH, 2 * WIDTH)),
            rows_of(LANES, QUERY),
            rows_of(LANES, QUERY),
        ],
        [rows_of(WIDTH, QUERY), full, full, edge, edge],
        [struct((tokens, WIDTH), BF16)] * 3 + [struct((4 * REACH, WIDTH), F32)] * 2,
        [pltpu.VMEM((tokens + 2 * REACH, WIDTH), BF16)] * 2
        + [pltpu.VMEM((tokens + 2 * REACH, WIDTH), F32)] * 2
        + [pltpu.VMEM((tokens, LANES), F32)] * 2,
        blocks * GROUPS * 2 * 4 * 4 * QUERY * span * GROUP,
        14 * tokens * WIDTH + blocks * GROUPS * 8 * QUERY * span,
        "attend_back",
    )(q, grad, weights, k, v, low, high, cosine, sine)


def mix_kernel(*refs):
    xs, (attended, gain), pieces = refs[:4], refs[4:6], refs[6:14]
    mixed, normed, held = refs[14:]

    @pl.when(pl.program_id(0) == 0)
    def _():
        place(pieces, held, 0, GROUP, 0)

    total = whole_rows(xs).astype(F32) + nn(attended[...], held[...])
    mixed[...] = total
    normed[...] = (norm(total)[0] * gain[...]).astype(BF16)


def mix(xs, attended, gain, pieces):
    tokens = attended.shape[0]
    return call(
        mix_kernel,
        (tokens // TILE,),
        [rows_of(256)] * 4
        + [rows_of(WIDTH), resident((1, WIDTH))]
        + [resident((SLOTS, GROUP, LANES))] * 8,
        [rows_of(WIDTH)] * 2,
        [struct((tokens, WIDTH), F32), struct((tokens, WIDTH), BF16)],
        [pltpu.VMEM((WIDTH, WIDTH), BF16)],
        2 * tokens * WIDTH * WIDTH,
        10 * tokens * WIDTH + 2 * WIDTH * WIDTH,
        "mix",
    )(*xs, attended, gain, *pieces)


def feed_kernel(*refs):
    normed, mixed = refs[:2]
    up, down = refs[2:10], refs[10:18]
    outs = refs[18:22]
    hidden, slope, gelu, held_up, held_down = refs[22:]
    ff = hidden.shape[2]

    @pl.when(pl.program_id(0) == 0)
    def _():
        place(up, held_up, 0, ff, 0)
        place(up, held_up, ff, ff, GROUPS * ff)
        place(down, held_down, 0, ff, 0)

    rows = normed[...]
    total = mixed[...]
    for p in range(GROUPS):
        act = nt(rows, held_up[pl.ds(p * ff, ff), :])
        gate = nt(rows, held_up[pl.ds((GROUPS + p) * ff, ff), :])
        spread_to = 0.5 * (1.0 + lax.erf(act * math.sqrt(0.5)))
        curve = act * spread_to
        density = jnp.exp(act * act * -0.5) * (1.0 / math.sqrt(2.0 * math.pi))
        slope[p] = (gate * (spread_to + act * density)).astype(BF16)
        gelu[p] = curve.astype(BF16)
        unit = (curve * gate).astype(BF16)
        hidden[p] = unit
        total = total + nn(unit, held_down[pl.ds(p * ff, ff), :])
    for o in range(SLOTS):
        for a in range(2):
            at = (a * SLOTS + o) * LANES
            outs[o][:, a * LANES : (a + 1) * LANES] = total[:, at : at + LANES].astype(BF16)


def feed(normed, mixed, up, down):
    tokens, ff = normed.shape[0], down[0].shape[1]
    units = pl.BlockSpec((GROUPS, TILE, ff), lambda i: (0, i, 0))
    return call(
        feed_kernel,
        (tokens // TILE,),
        [rows_of(WIDTH), rows_of(WIDTH)]
        + [resident((SLOTS, 2 * ff, LANES))] * 8
        + [resident((SLOTS, ff, LANES))] * 8,
        [rows_of(256)] * 4 + [units] * 3,
        [struct((tokens, 256), BF16)] * 4 + [struct((GROUPS, tokens, ff), BF16)] * 3,
        [pltpu.VMEM((2 * GROUPS * ff, WIDTH), BF16), pltpu.VMEM((GROUPS * ff, WIDTH), BF16)],
        2 * tokens * WIDTH * 3 * GROUPS * ff,
        8 * tokens * WIDTH + 6 * GROUPS * ff * (tokens + WIDTH),
        "feed",
    )(normed, mixed, *up, *down)


def feed_back_kernel(*refs):
    cots, (slope, gelu, mixed, gain) = refs[:4], refs[4:8]
    up, down, outward = refs[8:16], refs[16:24], refs[24:32]
    g_act, g_gate, g_mixed, g_branch, g_attended, gain_part = refs[32:38]
    held_up, held_down, held_out = refs[38:]
    ff = g_act.shape[2]

    @pl.when(pl.program_id(0) == 0)
    def _():
        place(up, held_up, 0, ff, 0)
        place(up, held_up, ff, ff, GROUPS * ff)
        place(down, held_down, 0, ff, 0)
        place(outward, held_out, 0, GROUP, 0)

    cot = whole_rows(cots)
    gradient = jnp.zeros((TILE, WIDTH), F32)
    for p in range(GROUPS):
        g_hidden = nt(cot, held_down[pl.ds(p * ff, ff), :])
        to_act = (g_hidden * slope[p].astype(F32)).astype(BF16)
        to_gate = (g_hidden * gelu[p].astype(F32)).astype(BF16)
        g_act[p] = to_act
        g_gate[p] = to_gate
        gradient = gradient + nn(to_act, held_up[pl.ds(p * ff, ff), :])
        gradient = gradient + nn(to_gate, held_up[pl.ds((GROUPS + p) * ff, ff), :])
    unit, inverse = norm(mixed[...])
    add_gain(gain_part, gradient * unit)
    total = cot.astype(F32) + norm_back(gradient, unit, inverse, gain[...])
    g_mixed[...] = total
    branch = total.astype(BF16)
    g_branch[...] = branch
    g_attended[...] = nt(branch, held_out[...]).astype(BF16)


def feed_back(cots, slope, gelu, mixed, gain, up, down, outward):
    tokens, ff = mixed.shape[0], down[0].shape[1]
    units = pl.BlockSpec((GROUPS, TILE, ff), lambda i: (0, i, 0))
    return call(
        feed_back_kernel,
        (tokens // TILE,),
        [rows_of(256)] * 4
        + [units, units, rows_of(WIDTH), resident((1, WIDTH))]
        + [resident((SLOTS, 2 * ff, LANES))] * 8
        + [resident((SLOTS, ff, LANES))] * 8
        + [resident((SLOTS, GROUP, LANES))] * 8,
        [units, units] + [rows_of(WIDTH)] * 3 + [resident((8, WIDTH))],
        [struct((GROUPS, tokens, ff), BF16)] * 2
        + [
            struct((tokens, WIDTH), F32),
            struct((tokens, WIDTH), BF16),
            struct((tokens, WIDTH), BF16),
            struct((8, WIDTH), F32),
        ],
        [
            pltpu.VMEM((2 * GROUPS * ff, WIDTH), BF16),
            pltpu.VMEM((GROUPS * ff, WIDTH), BF16),
            pltpu.VMEM((WIDTH, WIDTH), BF16),
        ],
        2 * tokens * WIDTH * (3 * GROUPS * ff + WIDTH),
        14 * tokens * WIDTH + 8 * GROUPS * ff * (tokens + WIDTH),
        "feed_back",
    )(*cots, slope, gelu, mixed, gain, *up, *down, *outward)


def unproject_kernel(*refs):
    xs, (gq, gk, gv, g_mixed, gain), pieces = refs[:4], refs[4:9], refs[9:17]
    outs, gain_part, held = refs[17:21], refs[21], refs[22]

    @pl.when(pl.program_id(0) == 0)
    def _():
        for t in range(3):
            place(pieces, held, t * GROUP, GROUP, t * WIDTH)

    gradient = nn(gq[...], held[pl.ds(0, WIDTH), :])
    gradient = gradient + nn(gk[...], held[pl.ds(WIDTH, WIDTH), :])
    gradient = gradient + nn(gv[...], held[pl.ds(2 * WIDTH, WIDTH), :])
    unit, inverse = norm(whole_rows(xs).astype(F32))
    add_gain(gain_part, gradient * unit)
    total = g_mixed[...] + norm_back(gradient, unit, inverse, gain[...])
    for o in range(SLOTS):
        for a in range(2):
            at = (a * SLOTS + o) * LANES
            outs[o][:, a * LANES : (a + 1) * LANES] = total[:, at : at + LANES].astype(BF16)


def unproject(xs, gq, gk, gv, g_mixed, gain, pieces):
    tokens = gq.shape[0]
    return call(
        unproject_kernel,
        (tokens // TILE,),
        [rows_of(256)] * 4
        + [rows_of(WIDTH)] * 4
        + [resident((1, WIDTH))]
        + [resident((SLOTS, 3 * GROUP, LANES))] * 8,
        [rows_of(256)] * 4 + [resident((8, WIDTH))],
        [struct((tokens, 256), BF16)] * 4 + [struct((8, WIDTH), F32)],
        [pltpu.VMEM((3 * WIDTH, WIDTH), BF16)],
        2 * tokens * WIDTH * 3 * WIDTH,
        14 * tokens * WIDTH + 6 * WIDTH * WIDTH,
        "unproject",
    )(*xs, gq, gk, gv, g_mixed, gain, *pieces)


def outer_halves_kernel(count, slots, more, *refs):
    inner, outer = refs[: 2 * count], refs[2 * count : 2 * count + slots]
    rest = refs[2 * count + slots :]
    added, outs = (rest[:2], rest[2:]) if more else ((None, None), rest)
    if slots > 1:
        right = jnp.concatenate([ref[...] for ref in outer], axis=1)
    else:
        right = outer[0][...]
    for b in range(2):
        for t in range(count):
            left = inner[2 * t + b]
            left = left[0] if len(left.shape) == 3 else left[...]
            made = tn(left, right)
            rows = slice(t * made.shape[0], (t + 1) * made.shape[0])
            for o in range(SLOTS):
                part = made[:, o * LANES : (o + 1) * LANES]
                if more:
                    part = part + added[b][0, o, rows, :].astype(F32)
                outs[b][0, o, rows, :] = part.astype(BF16)


def outer_groups_kernel(count, more, *refs):
    inner, outer, rest = refs[:count], refs[count], refs[count + 1 :]
    added, outs = (rest[:2], rest[2:]) if more else ((None, None), rest)
    right = outer[...]
    for t in range(count):
        left = inner[t]
        left = left[0] if len(left.shape) == 3 else left[...]
        made = tn(left, right)
        rows = slice(t * made.shape[0], (t + 1) * made.shape[0])
        for a in range(2):
            for o in range(SLOTS):
                at = (a * SLOTS + o) * LANES
                part = made[:, at : at + LANES]
                if more:
                    part = part + added[a][0, o, rows, :].astype(F32)
                outs[a][0, o, rows, :] = part.astype(BF16)


def inner_block(value, group):
    if value.ndim == 3:
        return pl.BlockSpec((1,) + value.shape[1:], lambda i: (group(i), 0, 0))
    return pl.BlockSpec((value.shape[0], GROUP), lambda i: (0, group(i)))


def outer_product(kind, inner, outer, d, added=None):
    tokens = outer[0].shape[0]
    width = inner[0].shape[2] if inner[0].ndim == 3 else GROUP
    rows = len(inner) * width
    block = pl.BlockSpec((1, SLOTS, rows, LANES), lambda i: (i, 0, 0, 0))
    if kind == "halves":
        kernel = functools.partial(
            outer_halves_kernel, len(inner), len(outer), added is not None
        )
        operands = [value for value in inner for _ in range(2)]
        specs = [inner_block(v, lambda i, b=b: 2 * b + d) for v in inner for b in range(2)]
        step = LANES if len(outer) > 1 else SLOTS * LANES
        specs += [pl.BlockSpec((tokens, step), lambda i: (0, i)) for _ in outer]
    else:
        kernel = functools.partial(outer_groups_kernel, len(inner), added is not None)
        operands = list(inner)
        specs = [inner_block(v, lambda i: 2 * i + d) for v in inner]
        specs += [resident((tokens, WIDTH))]
    operands += list(outer)
    if added is not None:
        operands += list(added)
        specs += [block] * 2
    return call(
        kernel,
        (2,),
        specs,
        [block] * 2,
        [struct((2, SLOTS, rows, LANES), BF16)] * 2,
        [],
        2 * tokens * 2 * rows * WIDTH,
        4 * rows * (tokens + WIDTH) + 2 * tokens * WIDTH,
        "outer_product",
    )(*operands)


ROTATE = 4


def over_dp(value):
    return lax.ppermute(value, "dp", [(0, 1), (1, 0)])


def over_chip(value):
    return lax.ppermute(value, "col", [(i, i ^ 2) for i in range(4)])


def over_core(value):
    return lax.ppermute(value, "col", [(i, i ^ 1) for i in range(4)])


def from_row(value, o):
    return lax.ppermute(value, "row", [((i + o) % ROTATE, i) for i in range(ROTATE)])


def to_row(value, o):
    return lax.ppermute(value, "row", [(i, (i + o) % ROTATE) for i in range(ROTATE)])


def gather_pieces(shard, chips_last):
    half = lax.dynamic_slice_in_dim(shard, lax.axis_index("dp") * LANES, LANES, 1)
    own = jnp.stack([half] + [from_row(half, o) for o in range(1, SLOTS)])
    if chips_last:
        other = over_dp(own)
        held = {(0, 0): own, (1, 0): other, (0, 1): over_chip(own), (1, 1): over_chip(other)}
    else:
        other = over_chip(own)
        held = {(0, 0): own, (0, 1): other, (1, 0): over_dp(own), (1, 1): over_dp(other)}
    pieces = {}
    for (a, b), value in held.items():
        pieces[a, b, 0] = value
        pieces[a, b, 1] = over_core(value)
    return [pieces[a, b, d] for a in range(2) for b in range(2) for d in range(2)]


def plus(left, right):
    return (left.astype(F32) + right.astype(F32)).astype(BF16)


def reduce_pieces(kind, parts):
    near, far = parts
    cross, turn = (over_chip, over_dp) if kind == "halves" else (over_dp, over_chip)
    came = cross(far)
    came_too = turn(plus(near[1], came[1]))
    total = plus(plus(near[0], came[0]), came_too)
    half = total[0].astype(F32)
    for o in range(1, SLOTS):
        half = half + to_row(total[o], o).astype(F32)
    half = half.astype(BF16)
    other = over_dp(half)
    first = lax.axis_index("dp") == 0
    return jnp.where(
        first,
        jnp.concatenate([half, other], axis=1),
        jnp.concatenate([other, half], axis=1),
    ).astype(F32)


def own_half_first(value):
    return jnp.where(lax.axis_index("dp") == 0, value, jnp.roll(value, LANES, axis=-1))


def slots_of(value):
    me = lax.axis_index("row")
    blocks = value.reshape(ROTATE, -1, 256)
    outs = [lax.dynamic_index_in_dim(blocks, me, 0, False)]
    for o in range(1, ROTATE):
        mine = lax.dynamic_index_in_dim(blocks, (me + ROTATE - o) % ROTATE, 0, False)
        outs.append(from_row(own_half_first(mine), o))
    outs[0] = own_half_first(outs[0])
    return outs


def from_slots(slots, dtype):
    me = lax.axis_index("row")
    tokens = slots[0].shape[0]
    whole = jnp.zeros((ROTATE * tokens, 256), dtype)
    for o in range(ROTATE):
        came = slots[0] if o == 0 else to_row(slots[o], o)
        at = ((me + ROTATE - o) % ROTATE) * tokens
        whole = lax.dynamic_update_slice(whole, own_half_first(came).astype(dtype), (at, 0))
    return whole


def sum_gains(parts):
    total = parts.reshape(2, 2, SLOTS, LANES)
    both = total + over_dp(total)[:, ::-1]
    both = both + over_chip(both)
    both = both + over_core(both)
    mine = both[:, :, 0]
    for o in range(1, SLOTS):
        mine = mine + to_row(both[:, :, o], o)
    return own_half_first(mine.reshape(2, 2 * LANES))


def pieces_of(whole):
    rows = whole.shape[0] // GROUPS
    cut = whole.reshape(GROUPS, rows, SLOTS, 2, LANES).transpose(3, 0, 2, 1, 4)
    return [cut[a, p] for a in range(2) for p in range(GROUPS)]


def whole_of(kind, near_far_by_d, types):
    cut = jnp.stack([jnp.stack(pair) for pair in near_far_by_d])
    cut = cut.transpose((1, 0, 4, 3, 2, 5) if kind == "halves" else (2, 0, 4, 3, 1, 5))
    b, d, rows, o, a, lanes = cut.shape
    cut = cut.reshape(b * d, types, rows // types, WIDTH)
    return [cut[:, t].reshape(-1, WIDTH) for t in range(types)]


def split_heads(rows):
    return rows.reshape(-1, 4, 2, 32, rows.shape[1]).swapaxes(1, 2).reshape(rows.shape)


def join_heads(rows):
    return rows.reshape(-1, 2, 4, 32, rows.shape[1]).swapaxes(1, 2).reshape(rows.shape)


def positions_and_masks(segment_ids, valid_mask, tokens, rows, cols):
    length = segment_ids.shape[1]
    both = lax.all_gather(jnp.stack([segment_ids, valid_mask]), "row", axis=1, tiled=True)
    at = (lax.axis_index("col") * rows + lax.axis_index("row")) * tokens
    sequence, first = at // length, at % length
    segments, valid = lax.dynamic_index_in_dim(both, sequence, 1, False)
    own = lax.dynamic_slice_in_dim(segments, first, tokens, 0)
    ids = jnp.arange(64, dtype=jnp.int32)
    before = jnp.sum((segments[None, :] < ids[:, None]).astype(jnp.int32), axis=1)
    begin = jnp.sum(jnp.where(own[:, None] == ids[None, :], before[None, :], 0), axis=1)
    where_in = (first + jnp.arange(tokens, dtype=jnp.int32) - begin).astype(F32)
    frequency = ROPE_THETA ** (-(jnp.arange(32, dtype=F32) * 2.0) / HEAD)
    angles = where_in[:, None] * frequency[None, :]
    cosine, sine = jnp.tile(jnp.cos(angles), (1, 4)), jnp.tile(jnp.sin(angles), (1, 4))
    code = jnp.pad(jnp.where(valid == 1, segments, -1), (REACH, REACH), constant_values=-1)
    code = lax.dynamic_slice_in_dim(code, first, tokens + 2 * REACH, 0)
    span = QUERY + 2 * REACH
    keys = jnp.stack([code[i : i + span] for i in range(0, tokens, QUERY)])[:, None, :]
    return cosine, sine, own[:, None], keys


def body(
    dp,
    rows,
    cols,
    tokens_in,
    w_query,
    w_key,
    w_value,
    w_out,
    w_act,
    w_gate,
    w_down,
    gain_attn,
    gain_ffn,
    cotangent,
    segment_ids,
    valid_mask,
):
    own_slice = (dp, rows, cols) == (2, 4, 4)
    tokens = tokens_in.shape[0] // rows
    length = segment_ids.shape[1]
    gains = jnp.stack([gain_attn, gain_ffn])
    if own_slice:
        xs = slots_of(tokens_in)
        cots = slots_of(cotangent)
        gain_slots = own_half_first(gains)
        gain_slots = jnp.stack([gain_slots] + [from_row(gain_slots, o) for o in range(1, SLOTS)])
        gather = gather_pieces
        project_rows = jnp.concatenate(
            [split_heads(w_query.T), split_heads(w_key.T), w_value.T], axis=0
        )
        project_w = gather(project_rows, True)
        out_w = gather(w_out, False)
        up_w = gather(jnp.concatenate([w_act.T, w_gate.T], axis=0), False)
        down_w = gather(w_down, True)
    else:

        def exchange(value):
            return lax.all_to_all(value.reshape(rows, tokens, 256), "row", 0, 0)

        def full(value, inner_first):
            first, second = ("col", "row") if inner_first else ("row", "col")
            value = lax.all_gather(value, first, axis=0, tiled=True)
            value = lax.all_gather(value, second, axis=1, tiled=True)
            return value if inner_first else value.T

        xs = list(exchange(tokens_in))
        cots = list(exchange(cotangent))
        gain_slots = lax.all_gather(gains, "row", axis=0)

        def joined(*parts):
            lists = [pieces_of(part) for part in parts]
            return [jnp.concatenate(same, axis=1) for same in zip(*lists)]

        project_w = joined(
            split_heads(full(w_query, False)),
            split_heads(full(w_key, False)),
            full(w_value, False),
        )
        out_w = joined(full(w_out, True))
        up_w = joined(full(w_act, False), full(w_gate, False))
        down_w = joined(full(w_down, True))
    gain_rows = (
        gain_slots.reshape(SLOTS, 2, 2, LANES).transpose(1, 2, 0, 3).reshape(2, 1, WIDTH)
    ).astype(F32)

    cosine, sine, seg_query, seg_key = positions_and_masks(
        segment_ids, valid_mask, tokens, rows, cols
    )
    q, k, v, normed_attn = project(xs, gain_rows[0], cosine, sine, project_w)

    count = rows * cols
    joins = [i for i in range(count - 1) if ((i + 1) * tokens) % length]
    upward, downward = [(i, i + 1) for i in joins], [(i + 1, i) for i in joins]

    def shift(value, perm):
        place_of = [(i % rows) * cols + i // rows for i in range(count)]
        return lax.ppermute(value, ("row", "col"), [(place_of[i], place_of[j]) for i, j in perm])

    low = shift(jnp.concatenate([k[-REACH:], v[-REACH:]], axis=1), upward)
    high = shift(jnp.concatenate([k[:REACH], v[:REACH]], axis=1), downward)
    attended, weights = attend(q, k, v, low, high, seg_query, seg_key)
    mixed, normed_ffn = mix(xs, attended, gain_rows[1], out_w)
    *out_slots, hidden, slope, gelu = feed(normed_ffn, mixed, up_w, down_w)

    def outer_sum(kind, inner, outer):
        far = outer_product(kind, inner, outer, 1)
        if own_slice:
            came = [over_core(value) for value in far]
            return outer_product(kind, inner, outer, 0, came)
        return [outer_product(kind, inner, outer, 0), far]

    down_parts = outer_sum("halves", [hidden], cots)
    g_act, g_gate, g_mixed, g_branch, g_attended, gain_part_ffn = feed_back(
        cots, slope, gelu, mixed, gain_rows[1], up_w, down_w, out_w
    )
    up_parts = outer_sum("groups", [g_act, g_gate], [normed_ffn])
    out_parts = outer_sum("groups", [attended], [g_branch])
    gq, gk, gv, edge_k, edge_v = attend_back(
        q, g_attended, weights, k, v, low, high, cosine, sine
    )
    to_low = jnp.concatenate([edge_k[:REACH], edge_v[:REACH]], axis=1).astype(BF16)
    to_high = jnp.concatenate([edge_k[-REACH:], edge_v[-REACH:]], axis=1).astype(BF16)
    from_high = shift(to_low, downward).astype(F32)
    from_low = shift(to_high, upward).astype(F32)

    def turned(value, c, s):
        cut = value.reshape(-1, GROUPS, 2, LANES)
        first, second = cut[:, :, 0], cut[:, :, 1]
        c, s = c[:, None], s[:, None]
        back = jnp.stack([first * c + second * s, second * c - first * s], axis=2)
        return back.reshape(value.shape).astype(BF16)

    near_k = edge_k[REACH : 2 * REACH] + from_low[:, :WIDTH]
    near_v = edge_v[REACH : 2 * REACH] + from_low[:, WIDTH:]
    last_k = edge_k[2 * REACH : 3 * REACH] + from_high[:, :WIDTH]
    last_v = edge_v[2 * REACH : 3 * REACH] + from_high[:, WIDTH:]
    gk = gk.at[:REACH].set(turned(near_k, cosine[:REACH], sine[:REACH]))
    gk = gk.at[-REACH:].set(turned(last_k, cosine[-REACH:], sine[-REACH:]))
    gv = gv.at[:REACH].set(near_v.astype(BF16))
    gv = gv.at[-REACH:].set(last_v.astype(BF16))

    *grad_slots, gain_part_attn = unproject(xs, gq, gk, gv, g_mixed, gain_rows[0], project_w)
    project_parts = outer_sum("halves", [gq, gk, gv], [normed_attn])

    gain_parts = jnp.stack([jnp.sum(gain_part_attn, axis=0), jnp.sum(gain_part_ffn, axis=0)])
    if own_slice:
        layer_out = from_slots(out_slots, BF16)
        token_gradient = from_slots(grad_slots, F32)
        down_sum = reduce_pieces("halves", down_parts)
        up_sum = reduce_pieces("groups", up_parts)
        out_sum = reduce_pieces("groups", out_parts)
        project_sum = reduce_pieces("halves", project_parts)
        ff = w_act.shape[1]
        grads = (
            join_heads(project_sum[:GROUP]).T,
            join_heads(project_sum[GROUP : 2 * GROUP]).T,
            project_sum[2 * GROUP :].T,
            out_sum,
            up_sum[:ff].T,
            up_sum[ff:].T,
            down_sum,
        )
        gain_grads = sum_gains(gain_parts)
    else:

        def back(slots):
            return lax.all_to_all(jnp.stack(slots), "row", 0, 0).reshape(-1, 256)

        def share(value, inner_first):
            first, second = ("col", "row") if inner_first else ("row", "col")
            value = value if inner_first else value.T
            value = lax.psum_scatter(value, first, scatter_dimension=0, tiled=True)
            value = lax.psum_scatter(value, second, scatter_dimension=1, tiled=True)
            return lax.psum(value, "dp").astype(F32)

        layer_out = back(out_slots)
        token_gradient = back(grad_slots).astype(F32)
        (down_whole,) = whole_of("halves", down_parts, 1)
        act_whole, gate_whole = whole_of("groups", up_parts, 2)
        (out_whole,) = whole_of("groups", out_parts, 1)
        query_whole, key_whole, value_whole = whole_of("halves", project_parts, 3)
        grads = (
            share(join_heads(query_whole), False),
            share(join_heads(key_whole), False),
            share(value_whole, False),
            share(out_whole, True),
            share(act_whole, False),
            share(gate_whole, False),
            share(down_whole, True),
        )
        totals = lax.psum(gain_parts, ("dp", "row", "col"))
        totals = totals.reshape(2, 2, SLOTS, LANES).swapaxes(1, 2).reshape(2, SLOTS, 256)
        gain_grads = lax.dynamic_index_in_dim(totals, lax.axis_index("row"), 1, False)
    return (layer_out, token_gradient) + grads + (gain_grads[0], gain_grads[1])


def solution(mesh):
    sizes = tuple(mesh.shape[axis] for axis in ("dp", "row", "col"))
    in_specs = (
        P(("dp", "col"), "row"),
        P("row", "col"),
        P("row", "col"),
        P("row", "col"),
        P("col", "row"),
        P("row", "col"),
        P("row", "col"),
        P("col", "row"),
        P("row"),
        P("row"),
        P(("dp", "col"), "row"),
        P(("dp", "row"), None),
        P(("dp", "row"), None),
    )
    out_specs = (
        P(("dp", "col"), "row"),
        P(("dp", "col"), "row"),
        P("row", "col"),
        P("row", "col"),
        P("row", "col"),
        P("col", "row"),
        P("row", "col"),
        P("row", "col"),
        P("col", "row"),
        P("row"),
        P("row"),
    )
    return jax.shard_map(
        functools.partial(body, *sizes),
        mesh=mesh,
        in_specs=in_specs,
        out_specs=out_specs,
        check_vma=False,
    )
```

```python
import functools
import math

import jax
import jax.numpy as jnp
from jax import lax
from jax.experimental import pallas as pl
from jax.experimental.pallas import tpu as pltpu
from jax.sharding import PartitionSpec as P

WIDTH = 1024
HEAD = 64
REACH = 64
EPSILON = 1e-05
ROPE_THETA = 10000.0
MASKED_SCORE = -1e30
LANES = 128
SLOTS = 4
GROUPS = 4
GROUP = 256
TILE = 256
QUERY = 128
VMEM = 60 * 1024 * 1024
F32 = jnp.float32
BF16 = jnp.bfloat16


def nt(left, right):
    return lax.dot_general(left, right, (((1,), (1,)), ((), ())), preferred_element_type=F32)


def nn(left, right):
    return lax.dot_general(left, right, (((1,), (0,)), ((), ())), preferred_element_type=F32)


def tn(left, right):
    return lax.dot_general(left, right, (((0,), (0,)), ((), ())), preferred_element_type=F32)


def call(kernel, grid, in_specs, out_specs, out_shape, scratch, flops, moved, name):
    return pl.pallas_call(
        kernel,
        grid=grid,
        in_specs=in_specs,
        out_specs=out_specs,
        out_shape=out_shape,
        scratch_shapes=scratch,
        compiler_params=pltpu.CompilerParams(
            vmem_limit_bytes=VMEM, dimension_semantics=("arbitrary",)
        ),
        cost_estimate=pl.CostEstimate(flops=flops, bytes_accessed=moved, transcendentals=0),
        name=name,
    )


def resident(shape):
    zeros = (0,) * len(shape)
    return pl.BlockSpec(shape, lambda i: zeros, pipeline_mode=pl.Buffered(1))


def rows_of(width, tile=TILE):
    return pl.BlockSpec((tile, width), lambda i: (i, 0))


BLOCKS = pl.BlockSpec((SLOTS, TILE, 256), lambda i: (0, i, 0))


def later_rows(width):
    return pl.BlockSpec((TILE, width), lambda i: (jnp.maximum(i - GROUPS, 0), 0))


LATER_BLOCKS = pl.BlockSpec((SLOTS, TILE, 256), lambda i: (0, jnp.maximum(i - GROUPS, 0), 0))


def group_of(i):
    return jnp.minimum(i, GROUPS - 1)


def weight_rows(rows, at=0):
    return [
        pl.BlockSpec(
            (1, SLOTS, rows, LANES), lambda i, a=a: (a * GROUPS + group_of(i), 0, at, 0)
        )
        for a in range(2)
    ]


def joined_rows(halves, rows=slice(None)):
    return jnp.concatenate([w[0, o, rows, :] for o in range(SLOTS) for w in halves], axis=1)


def at_first(run):
    pl.when(pl.program_id(0) == 0)(run)


def add_up(total, part):
    @at_first
    def _():
        total[...] = part

    @pl.when((pl.program_id(0) > 0) & (pl.program_id(0) < GROUPS))
    def _():
        total[...] += part


def struct(shape, dtype):
    return jax.ShapeDtypeStruct(shape, dtype)


def whole_rows(slots, rows=slice(None)):
    return jnp.concatenate([slots[o, rows, :] for o in range(SLOTS)], axis=1)


def inner_rows(tile):
    return pl.ds(pl.multiple_of(pl.program_id(0) * tile + REACH, REACH), tile)


def put_rows(slots, total):
    for o in range(SLOTS):
        slots[o] = total[:, o * 256 : (o + 1) * 256].astype(slots.dtype)


def norm(values):
    average = jnp.mean(values, axis=1, keepdims=True)
    centered = values - average
    variance = jnp.mean(centered * centered, axis=1, keepdims=True)
    inverse = lax.rsqrt(variance + EPSILON)
    return centered * inverse, inverse


def norm_back(gradient, unit, inverse, gain):
    scaled = gradient * gain
    average = jnp.mean(scaled, axis=1, keepdims=True)
    crossed = jnp.mean(scaled * unit, axis=1, keepdims=True)
    return inverse * (scaled - average - unit * crossed)


def add_gain(gain_part, products):
    @pl.when(pl.program_id(0) == GROUPS)
    def _():
        gain_part[...] = jnp.zeros_like(gain_part)

    gain_part[...] += jnp.sum(products.reshape(-1, 8, WIDTH), axis=0)


def project_kernel(xs, gain, cosine, sine, low, high, q, k, v, normed, rows):
    @at_first
    def _():
        for at in range(0, rows.shape[0], QUERY):
            cut = slice(at, at + QUERY)
            values = jnp.concatenate([xs[o, cut, :] for o in range(SLOTS)], axis=1)
            made = (norm(values.astype(F32))[0] * gain[...]).astype(BF16)
            rows[cut, :] = made
            normed[cut, :] = made

    made = nt(rows[...], joined_rows((low, high)))
    c, s = cosine[...], sine[...]
    for t, out in ((0, q), (1, k)):
        first = made[:, t * GROUP : t * GROUP + LANES]
        second = made[:, t * GROUP + LANES : (t + 1) * GROUP]
        out[:, :LANES] = (first * c - second * s).astype(BF16)
        out[:, LANES:] = (second * c + first * s).astype(BF16)
    v[...] = made[:, 2 * GROUP :].astype(BF16)


def project(xs, gain, cosine, sine, weight):
    tokens = cosine.shape[0]
    return call(
        project_kernel,
        (GROUPS,),
        [resident(xs.shape), resident((1, WIDTH))]
        + [resident((tokens, LANES))] * 2
        + weight_rows(3 * GROUP),
        [pl.BlockSpec((tokens, GROUP), lambda i: (0, i))] * 3 + [resident((tokens, WIDTH))],
        [struct((tokens, WIDTH), BF16)] * 4,
        [pltpu.VMEM((tokens, WIDTH), BF16)],
        2 * tokens * WIDTH * 3 * WIDTH,
        10 * tokens * WIDTH + 6 * WIDTH * WIDTH,
        "project",
    )(xs, gain, cosine, sine, weight, weight)


def head_masks():
    lane = lax.broadcasted_iota(jnp.int32, (1, GROUP), 1)
    halves = [((lane % LANES) // 32 == h) for h in range(4)]
    wholes = [(lane // HEAD == h) for h in range(4)]
    return halves, wholes


def spread(rows, masks):
    return jnp.concatenate([rows * m.astype(BF16) for m in masks], axis=0)


def collect(stacked, masks):
    total = jnp.where(masks[0], stacked[0:QUERY], 0.0)
    for h in range(1, 4):
        total = jnp.where(masks[h], stacked[h * QUERY : (h + 1) * QUERY], total)
    return total


def attend_kernel(q, k, v, seg_query, seg_key, attended, probability):
    span = pl.ds(pl.multiple_of(pl.program_id(0) * QUERY, QUERY), QUERY + 2 * REACH)
    own = inner_rows(QUERY)
    shape = (QUERY, QUERY + 2 * REACH)
    offset = (
        lax.broadcasted_iota(jnp.int32, shape, 1)
        - lax.broadcasted_iota(jnp.int32, shape, 0)
        - REACH
    )
    allowed = (jnp.abs(offset) <= REACH) & ((seg_query[...] == seg_key[0]) | (offset == 0))
    halves, wholes = head_masks()
    for p in range(GROUPS):
        lanes = slice(p * GROUP, (p + 1) * GROUP)
        stacked = spread(q[own, lanes], halves)
        scores = nt(stacked, k[span, lanes]) * HEAD**-0.5
        scores = jnp.concatenate(
            [
                jnp.where(allowed, scores[h * QUERY : (h + 1) * QUERY], MASKED_SCORE)
                for h in range(4)
            ],
            axis=0,
        )
        exponent = jnp.exp(scores - jnp.max(scores, axis=1, keepdims=True))
        weight = (exponent * (1.0 / jnp.sum(exponent, axis=1, keepdims=True))).astype(BF16)
        probability[0, p] = weight
        attended[:, lanes] = collect(nn(weight, v[span, lanes]), wholes).astype(BF16)


def attend(q, k, v, seg_query, seg_key):
    tokens = seg_query.shape[0]
    blocks = tokens // QUERY
    span = QUERY + 2 * REACH
    return call(
        attend_kernel,
        (blocks,),
        [resident(q.shape)] * 3
        + [rows_of(1, QUERY), pl.BlockSpec((1, 1, span), lambda i: (i, 0, 0))],
        [
            rows_of(WIDTH, QUERY),
            pl.BlockSpec((1, GROUPS, 4 * QUERY, span), lambda i: (i, 0, 0, 0)),
        ],
        [
            struct((tokens, WIDTH), BF16),
            struct((blocks, GROUPS, 4 * QUERY, span), BF16),
        ],
        [],
        blocks * GROUPS * 2 * 2 * 4 * QUERY * span * GROUP,
        8 * tokens * WIDTH + blocks * GROUPS * 8 * QUERY * span,
        "attend",
    )(q, k, v, seg_query, seg_key)


def attend_back_kernel(*refs):
    q, grad, weights, k, v, cosine, sine = refs[:7]
    gq, gk, gv, edge_k, edge_v, sum_k, sum_v = refs[7:]
    step, steps = pl.program_id(0), pl.num_programs(0)
    tokens = gk.shape[0]

    @at_first
    def _():
        sum_k[...] = jnp.zeros_like(sum_k)
        sum_v[...] = jnp.zeros_like(sum_v)

    start = pl.multiple_of(step * QUERY, QUERY)
    span = pl.ds(start, QUERY + 2 * REACH)
    halves, wholes = head_masks()
    own = inner_rows(QUERY)
    c, s = cosine[own, :], sine[own, :]
    for p in range(GROUPS):
        lanes = slice(p * GROUP, (p + 1) * GROUP)
        queries = spread(q[own, lanes], halves)
        grads = spread(grad[:, lanes], wholes)
        block_k, block_v = k[span, lanes], v[span, lanes]
        weight = weights[0, p]
        wide = weight.astype(F32)
        d_weight = nt(grads, block_v)
        mean = jnp.sum(wide * d_weight, axis=1, keepdims=True)
        g_score = (wide * (d_weight - mean)).astype(BF16)
        made = collect(nn(g_score, block_k), halves) * HEAD**-0.5
        first, second = made[:, :LANES], made[:, LANES:]
        gq[:, p * GROUP : p * GROUP + LANES] = (first * c + second * s).astype(BF16)
        gq[:, p * GROUP + LANES : (p + 1) * GROUP] = (second * c - first * s).astype(BF16)
        sum_k[span, lanes] += tn(g_score, queries) * HEAD**-0.5
        sum_v[span, lanes] += tn(weight, grads)

    @pl.when(step == steps - 1)
    def _():
        for edge, total in ((edge_k, sum_k), (edge_v, sum_v)):
            edge[0 : 2 * REACH, :] = total[0 : 2 * REACH, :]
            edge[2 * REACH :, :] = total[pl.ds(tokens, 2 * REACH), :]
        for at in range(0, tokens, QUERY):
            own = pl.ds(REACH + at, QUERY)
            c, s = cosine[own, :], sine[own, :]
            for p in range(GROUPS):
                one, two = p * GROUP, p * GROUP + LANES
                first, second = sum_k[own, pl.ds(one, LANES)], sum_k[own, pl.ds(two, LANES)]
                gk[pl.ds(at, QUERY), pl.ds(one, LANES)] = (first * c + second * s).astype(BF16)
                gk[pl.ds(at, QUERY), pl.ds(two, LANES)] = (second * c - first * s).astype(BF16)
            gv[pl.ds(at, QUERY), :] = sum_v[own, :].astype(BF16)


def attend_back(q, grad, weights, k, v, cosine, sine):
    tokens = grad.shape[0]
    blocks = tokens // QUERY
    span = QUERY + 2 * REACH
    full = resident((tokens, WIDTH))
    edge = resident((4 * REACH, WIDTH))
    return call(
        attend_back_kernel,
        (blocks,),
        [
            resident(q.shape),
            rows_of(WIDTH, QUERY),
            pl.BlockSpec((1, GROUPS, 4 * QUERY, span), lambda i: (i, 0, 0, 0)),
            resident(q.shape),
            resident(q.shape),
            resident(cosine.shape),
            resident(cosine.shape),
        ],
        [rows_of(WIDTH, QUERY), full, full, edge, edge],
        [struct((tokens, WIDTH), BF16)] * 3 + [struct((4 * REACH, WIDTH), F32)] * 2,
        [pltpu.VMEM(q.shape, F32)] * 2,
        blocks * GROUPS * 2 * 4 * 4 * QUERY * span * GROUP,
        14 * tokens * WIDTH + blocks * GROUPS * 8 * QUERY * span,
        "attend_back",
    )(q, grad, weights, k, v, cosine, sine)


def mix_kernel(xs, attended, gain, low, high, mixed, normed, total):
    @pl.when(pl.program_id(0) < GROUPS)
    def _():
        add_up(total, nn(attended[...], joined_rows((low, high))))

    @pl.when(pl.program_id(0) >= GROUPS)
    def _():
        rows = step_rows()
        made = whole_rows(xs, between_rows()).astype(F32) + total[rows, :]
        mixed[...] = made.astype(mixed.dtype)
        normed[...] = (norm(made)[0] * gain[...]).astype(BF16)


def step_rows():
    return pl.ds(pl.multiple_of((pl.program_id(0) - GROUPS) * TILE, TILE), TILE)


def between_rows():
    at = (pl.program_id(0) - GROUPS) * TILE + REACH
    return pl.ds(pl.multiple_of(at, REACH), TILE)


def mix(xs, attended, gain, weight):
    tokens = attended.shape[0]
    return call(
        mix_kernel,
        (GROUPS + tokens // TILE,),
        [
            resident(xs.shape),
            pl.BlockSpec((tokens, GROUP), lambda i: (0, group_of(i))),
            resident((1, WIDTH)),
        ]
        + weight_rows(GROUP, 3),
        [later_rows(WIDTH)] * 2,
        [struct((tokens, WIDTH), BF16)] * 2,
        [pltpu.VMEM((tokens, WIDTH), F32)],
        2 * tokens * WIDTH * WIDTH,
        8 * tokens * WIDTH + 2 * WIDTH * WIDTH,
        "mix",
    )(xs, attended, gain, weight, weight)


def up_kernel(normed, low, high, hidden, slope, gelu):
    ff = hidden.shape[2]
    act = nt(normed[...], joined_rows((low, high), slice(0, ff)))
    gate = nt(normed[...], joined_rows((low, high), slice(ff, 2 * ff)))
    spread_to = 0.5 * (1.0 + lax.erf(act * math.sqrt(0.5)))
    curve = act * spread_to
    density = jnp.exp(act * act * -0.5) * (1.0 / math.sqrt(2.0 * math.pi))
    slope[0] = (gate * (spread_to + act * density)).astype(BF16)
    gelu[0] = curve.astype(BF16)
    hidden[0] = (curve * gate).astype(BF16)


def units_of(tokens, ff):
    return pl.BlockSpec((1, tokens, ff), lambda i: (group_of(i), 0, 0))


def feed_up(normed, weight):
    tokens, ff = normed.shape[0], weight.shape[2] // 2
    return call(
        up_kernel,
        (GROUPS,),
        [resident((tokens, WIDTH))] + weight_rows(2 * ff),
        [units_of(tokens, ff)] * 3,
        [struct((GROUPS, tokens, ff), BF16)] * 3,
        [],
        2 * tokens * WIDTH * 2 * GROUPS * ff,
        2 * tokens * WIDTH + 2 * GROUPS * ff * (3 * tokens + 2 * WIDTH),
        "feed_up",
    )(normed, weight, weight)


def down_kernel(hidden, mixed, low, high, early, late, total):
    @pl.when(pl.program_id(0) < GROUPS)
    def _():
        add_up(total, nn(hidden[0], joined_rows((low, high))))

    half = GROUPS + total.shape[0] // TILE // 2

    @pl.when((pl.program_id(0) >= GROUPS) & (pl.program_id(0) < half))
    def _():
        put_rows(early, mixed[...].astype(F32) + total[step_rows(), :])

    @pl.when(pl.program_id(0) >= half)
    def _():
        put_rows(late, mixed[...].astype(F32) + total[step_rows(), :])


def feed_down(hidden, mixed, weight):
    _, tokens, ff = hidden.shape
    steps = tokens // TILE // 2
    return call(
        down_kernel,
        (GROUPS + tokens // TILE,),
        [units_of(tokens, ff), later_rows(WIDTH)] + weight_rows(ff),
        [
            pl.BlockSpec(
                (SLOTS, TILE, 256),
                lambda i, first=first: (0, jnp.clip(i - GROUPS - first, 0, steps - 1), 0),
            )
            for first in (0, steps)
        ],
        [struct((SLOTS, tokens // 2, 256), BF16)] * 2,
        [pltpu.VMEM((tokens, WIDTH), F32)],
        2 * tokens * WIDTH * GROUPS * ff,
        4 * tokens * WIDTH + 2 * GROUPS * ff * (tokens + WIDTH),
        "feed_down",
    )(hidden, mixed, weight, weight)


def down_back_kernel(cots, slope, gelu, low, high, g_act, g_gate):
    g_hidden = nt(whole_rows(cots), joined_rows((low, high)))
    g_act[0] = (g_hidden * slope[0].astype(F32)).astype(BF16)
    g_gate[0] = (g_hidden * gelu[0].astype(F32)).astype(BF16)


def down_back(cots, slope, gelu, weight):
    _, tokens, ff = slope.shape
    return call(
        down_back_kernel,
        (GROUPS,),
        [resident(cots.shape)] + [units_of(tokens, ff)] * 2 + weight_rows(ff),
        [units_of(tokens, ff)] * 2,
        [struct((GROUPS, tokens, ff), BF16)] * 2,
        [],
        2 * tokens * WIDTH * GROUPS * ff,
        2 * tokens * WIDTH + 2 * GROUPS * ff * (4 * tokens + WIDTH),
        "down_back",
    )(cots, slope, gelu, weight, weight)


def up_back_kernel(*refs):
    cots, g_act, g_gate, mixed, gain, low, high, out_low, out_high = refs[:9]
    g_branch, g_attended, gain_part, total = refs[9:]
    ff = g_act.shape[2]

    @pl.when(pl.program_id(0) < GROUPS)
    def _():
        part = nn(g_act[0], joined_rows((low, high), slice(0, ff)))
        add_up(total, part + nn(g_gate[0], joined_rows((low, high), slice(ff, 2 * ff))))

    @pl.when(pl.program_id(0) >= GROUPS)
    def _():
        gradient = total[step_rows(), :]
        unit, inverse = norm(mixed[...].astype(F32))
        add_gain(gain_part, gradient * unit)
        made = whole_rows(cots).astype(F32) + norm_back(gradient, unit, inverse, gain[...])
        branch = made.astype(BF16)
        g_branch[...] = branch
        for p in range(GROUPS):
            parts = [ref[p, o] for o in range(SLOTS) for ref in (out_low, out_high)]
            held = jnp.concatenate(parts, axis=1)
            g_attended[:, p * GROUP : (p + 1) * GROUP] = nt(branch, held).astype(BF16)


def up_back(cots, g_act, g_gate, mixed, gain, up, heads):
    _, tokens, ff = g_act.shape
    out_shape = (GROUPS, SLOTS, GROUP, LANES)
    return call(
        up_back_kernel,
        (GROUPS + tokens // TILE,),
        [LATER_BLOCKS]
        + [units_of(tokens, ff)] * 2
        + [later_rows(WIDTH), resident((1, WIDTH))]
        + weight_rows(2 * ff)
        + [
            pl.BlockSpec(out_shape, lambda i, a=a: (a, 0, 3, 0), pipeline_mode=pl.Buffered(1))
            for a in range(2)
        ],
        [later_rows(WIDTH)] * 2 + [resident((8, WIDTH))],
        [struct((tokens, WIDTH), BF16)] * 2 + [struct((8, WIDTH), F32)],
        [pltpu.VMEM((tokens, WIDTH), F32)],
        2 * tokens * WIDTH * (2 * GROUPS * ff + WIDTH),
        8 * tokens * WIDTH + 4 * GROUPS * ff * (tokens + WIDTH),
        "up_back",
    )(cots, g_act, g_gate, mixed, gain, up, up, heads, heads)


def unproject_kernel(xs, gq, gk, gv, g_branch, gain, low, high, outs, gain_part, total):
    @pl.when(pl.program_id(0) < GROUPS)
    def _():
        inner = jnp.concatenate([gq[...], gk[...], gv[...]], axis=1)
        add_up(total, nn(inner, joined_rows((low, high))))

    @pl.when(pl.program_id(0) >= GROUPS)
    def _():
        gradient = total[step_rows(), :]
        unit, inverse = norm(whole_rows(xs, between_rows()).astype(F32))
        add_gain(gain_part, gradient * unit)
        back = norm_back(gradient, unit, inverse, gain[...])
        put_rows(outs, g_branch[...].astype(F32) + back)


def unproject(xs, gq, gk, gv, g_branch, gain, weight):
    tokens = gq.shape[0]
    return call(
        unproject_kernel,
        (GROUPS + tokens // TILE,),
        [resident(xs.shape)]
        + [pl.BlockSpec((tokens, GROUP), lambda i: (0, group_of(i)))] * 3
        + [later_rows(WIDTH), resident((1, WIDTH))]
        + weight_rows(3 * GROUP),
        [LATER_BLOCKS, resident((8, WIDTH))],
        [struct((SLOTS, tokens, 256), BF16), struct((8, WIDTH), F32)],
        [pltpu.VMEM((tokens, WIDTH), F32)],
        2 * tokens * WIDTH * 3 * WIDTH,
        12 * tokens * WIDTH + 6 * WIDTH * WIDTH,
        "unproject",
    )(xs, gq, gk, gv, g_branch, gain, weight, weight)


def outer_kernel(pairs, count, *refs):
    inner, outer, out = refs[: len(pairs)], refs[len(pairs) : -1], refs[-1]
    tokens = inner[0].shape[-2]

    def make(left, right):
        left = left[0] if len(left.shape) == 3 else left[...]
        if len(right.shape) == 3:
            right = whole_rows(right)
        else:
            right = right[pl.ds((right.shape[0] - tokens) // 2, tokens), :]
        made = tn(left, right)
        for a in range(2):
            for o in range(SLOTS):
                at = o * 256 + a * LANES
                out[a, 0, o] = made[:, at : at + LANES].astype(BF16)

    for t, j in enumerate(pairs):
        pl.when(pl.program_id(0) % count == t)(functools.partial(make, inner[t], outer[j]))


def outer_product(pairs, inner, outer):
    count = len(inner)
    tokens = inner[0].shape[-2]
    width = inner[0].shape[2] if inner[0].ndim == 3 else GROUP
    rows = count * width

    def inner_block(value):
        if value.ndim == 3:
            return pl.BlockSpec((1, tokens, width), lambda i: (i // count, 0, 0))
        return pl.BlockSpec((tokens, GROUP), lambda i: (0, i // count))

    return call(
        functools.partial(outer_kernel, pairs, count),
        (GROUPS * count,),
        [inner_block(value) for value in inner] + [resident(value.shape) for value in outer],
        [
            pl.BlockSpec(
                (2, 1, SLOTS, width, LANES), lambda i: (0, i // count, 0, i % count, 0)
            )
        ],
        [struct((2, GROUPS, SLOTS, rows, LANES), BF16)],
        [],
        2 * tokens * GROUPS * rows * WIDTH,
        8 * rows * (tokens + WIDTH) + 2 * tokens * WIDTH,
        "outer_product",
    )(*inner, *outer)[0]


def over_dp(value):
    return lax.ppermute(value, "dp", [(0, 1), (1, 0)])


def over_chip(value):
    return lax.ppermute(value, "col", [(i, i ^ 2) for i in range(4)])


def over_core(value):
    return lax.ppermute(value, "col", [(i, i ^ 1) for i in range(4)])


def exchange(value):
    return lax.all_to_all(value, "row", 0, 0)


def after(value, *earlier):
    return lax.optimization_barrier((value,) + earlier)[0]


def own_half(shard):
    return lax.dynamic_slice_in_dim(shard, lax.axis_index("dp") * LANES, LANES, 1)


def gather_rows(half):
    return exchange(jnp.broadcast_to(half, (SLOTS,) + half.shape))


def gather_groups(own):
    return lax.all_gather(own, ("dp", "col"), axis=0, tiled=False)


def reduce_groups(parts):
    parts = parts.reshape((2 * GROUPS,) + parts.shape[2:])
    return lax.psum_scatter(parts, ("dp", "col"), scatter_dimension=0, tiled=False)


def sum_rows(parts):
    half = jnp.sum(parts.astype(F32), axis=0).astype(BF16)
    other = over_dp(half)
    first = lax.axis_index("dp") == 0
    return jnp.where(
        first,
        jnp.concatenate([half, other], axis=1),
        jnp.concatenate([other, half], axis=1),
    ).astype(F32)


def sum_gains(parts):
    both = parts + over_dp(parts)
    both = both + over_chip(both)
    both = both + over_core(both)
    for bit in (1, 2):
        both = both + lax.ppermute(both, "row", [(i, i ^ bit) for i in range(SLOTS)])
    return lax.dynamic_slice_in_dim(both, lax.axis_index("row") * 256, 256, 1)


def groups_of(whole):
    rows = whole.shape[0] // GROUPS
    cut = whole.reshape(GROUPS, rows, SLOTS, 2, LANES).transpose(3, 0, 2, 1, 4)
    return cut.reshape(2 * GROUPS, SLOTS, rows, LANES)


def whole_of(parts, types):
    cut = parts.transpose(1, 3, 2, 0, 4).reshape(GROUPS, types, -1, WIDTH)
    return [cut[:, t].reshape(-1, WIDTH) for t in range(types)]


def split_heads(rows):
    return rows.reshape(-1, 4, 2, 32, rows.shape[1]).swapaxes(1, 2).reshape(rows.shape)


def join_heads(rows):
    return rows.reshape(-1, 2, 4, 32, rows.shape[1]).swapaxes(1, 2).reshape(rows.shape)


def positions_and_masks(segments, valid, first, tokens):
    length = segments.shape[0]
    index = first - REACH + jnp.arange(tokens + 2 * REACH, dtype=jnp.int32)
    pads = (REACH, REACH)
    near = lax.dynamic_slice_in_dim(jnp.pad(segments, pads), first, tokens + 2 * REACH, 0)
    ids = jnp.arange(64, dtype=jnp.int32)
    before = jnp.sum((segments[None, :] < ids[:, None]).astype(jnp.int32), axis=1)
    begin = jnp.sum(jnp.where(near[:, None] == ids[None, :], before[None, :], 0), axis=1)
    where_in = (index - begin).astype(F32)
    frequency = ROPE_THETA ** (-(jnp.arange(32, dtype=F32) * 2.0) / HEAD)
    angles = where_in[:, None] * frequency[None, :]
    cosine, sine = jnp.tile(jnp.cos(angles), (1, 4)), jnp.tile(jnp.sin(angles), (1, 4))
    code = jnp.pad(jnp.where(valid == 1, segments, -1), pads, constant_values=-1)
    code = lax.dynamic_slice_in_dim(code, first, tokens + 2 * REACH, 0)
    span = QUERY + 2 * REACH
    keys = jnp.stack([code[i : i + span] for i in range(0, tokens, QUERY)])[:, None, :]
    return cosine, sine, near[REACH:-REACH, None], keys


def body(
    dp,
    rows,
    cols,
    tokens_in,
    w_query,
    w_key,
    w_value,
    w_out,
    w_act,
    w_gate,
    w_down,
    gain_attn,
    gain_ffn,
    cotangent,
    segment_ids,
    valid_mask,
):
    tokens = tokens_in.shape[0] // rows
    length = segment_ids.shape[1]
    own_slice = (dp, rows, cols) == (2, 4, 4) and rows * tokens == length
    gains = jnp.stack([gain_attn, gain_ffn])
    at = (lax.axis_index("col") * rows + lax.axis_index("row")) * tokens
    sequence, first = at // length, at % length
    count = rows * cols
    joins = [i for i in range(count - 1) if ((i + 1) * tokens) % length]
    upward, downward = [(i, i + 1) for i in joins], [(i + 1, i) for i in joins]

    def shift(value, perm):
        place_of = [(i % rows) * cols + i // rows for i in range(count)]
        return lax.ppermute(value, ("row", "col"), [(place_of[i], place_of[j]) for i, j in perm])

    if own_slice:
        marks = jnp.concatenate([segment_ids, valid_mask]).astype(BF16).reshape(-1, LANES)
        heads_half = jnp.concatenate(
            [
                split_heads(own_half(w_query.T)),
                split_heads(own_half(w_key.T)),
                own_half(w_value.T),
                own_half(w_out),
                marks,
                gains.reshape(4, LANES),
                jnp.zeros((12, LANES), BF16),
            ],
            axis=0,
        )
        up_half = jnp.concatenate([own_half(w_act.T), own_half(w_gate.T)], axis=0)
        padded = jnp.pad(tokens_in, ((REACH, REACH), (0, 0)))
        spans = [padded[j * tokens : (j + 1) * tokens + 2 * REACH] for j in range(rows)]
        heads_own = gather_rows(heads_half)
        heads_w = gather_groups(heads_own[:, :WIDTH])
        up_own = gather_rows(after(up_half, heads_own))
        up_w = gather_groups(up_own)
        last = WIDTH + marks.shape[0]
        marks = heads_own[:, WIDTH:last].reshape(rows, 2, length)
        marks = lax.dynamic_index_in_dim(marks, sequence, 0, False).astype(jnp.int32)
        gain_slots = heads_own[:, last : last + 4].reshape(SLOTS, 2, 256)
        tables = positions_and_masks(*marks, first, tokens)
        xs = exchange(after(jnp.stack(spans), up_own, *tables))
        down_own = gather_rows(after(own_half(w_down), xs))
    else:
        xs = exchange(tokens_in.reshape(rows, tokens, 256))
        below, above = shift(xs[:, -REACH:], upward), shift(xs[:, :REACH], downward)
        xs = jnp.concatenate([below, xs, above], axis=1)
        cots = exchange(cotangent.reshape(rows, tokens, 256))
        gain_slots = exchange(jnp.broadcast_to(gains, (rows, 2, 256)))
        marks = lax.all_gather(jnp.stack([segment_ids, valid_mask]), "row", axis=1, tiled=True)
        marks = lax.dynamic_index_in_dim(marks, sequence, 1, False)
        tables = positions_and_masks(*marks, first, tokens)

        def full(value, inner_first):
            first, second = ("col", "row") if inner_first else ("row", "col")
            value = lax.all_gather(value, first, axis=0, tiled=True)
            value = lax.all_gather(value, second, axis=1, tiled=True)
            return value if inner_first else value.T

        def joined(*parts):
            return jnp.concatenate([groups_of(part) for part in parts], axis=2)

        heads_w = joined(
            split_heads(full(w_query, False)),
            split_heads(full(w_key, False)),
            full(w_value, False),
            full(w_out, True),
        )
        up_w = joined(full(w_act, False), full(w_gate, False))
        down_w = joined(full(w_down, True))
    gain_rows = gain_slots.swapaxes(0, 1).reshape(2, 1, WIDTH).astype(F32)
    cosine, sine, seg_query, seg_key = tables

    q, k, v, normed_attn = project(xs, gain_rows[0], cosine, sine, heads_w)
    if own_slice:
        down_own = after(down_own, q)
        down_w = gather_groups(down_own)
        cots = exchange(after(cotangent.reshape(rows, tokens, 256), down_own))
    attended, weights = attend(q, k, v, seg_query, seg_key)
    mixed, normed_ffn = mix(xs, attended, gain_rows[1], heads_w)
    hidden, slope, gelu = feed_up(normed_ffn, up_w)
    early, late = feed_down(hidden, mixed, down_w)
    hidden = after(hidden, early)
    early = exchange(after(early, cots))
    late = exchange(after(late, early))
    layer_out = jnp.concatenate([early, late], axis=1)
    down_parts = outer_product((0,), [hidden], [cots])
    g_act, g_gate = down_back(cots, after(slope, down_parts), gelu, down_w)
    up_parts = outer_product((0, 0), [after(g_act, early), g_gate], [normed_ffn])
    g_branch, g_attended, gain_part_ffn = up_back(
        cots, after(g_act, up_parts), g_gate, mixed, gain_rows[1], up_w, heads_w
    )
    if own_slice:
        down_own, up_own = reduce_groups(down_parts), reduce_groups(up_parts)
        down_sum = exchange(after(down_own, late))
        g_attended = after(g_attended, late, down_own)
    gq, gk, gv, edge_k, edge_v = attend_back(q, g_attended, weights, k, v, cosine, sine)
    to_low = jnp.concatenate([edge_k[:REACH], edge_v[:REACH]], axis=1).astype(BF16)
    to_high = jnp.concatenate([edge_k[-REACH:], edge_v[-REACH:]], axis=1).astype(BF16)
    from_high = shift(to_low, downward).astype(F32)
    from_low = shift(to_high, upward).astype(F32)

    def turned(value, c, s):
        cut = value.reshape(-1, GROUPS, 2, LANES)
        first, second = cut[:, :, 0], cut[:, :, 1]
        c, s = c[:, None], s[:, None]
        back = jnp.stack([first * c + second * s, second * c - first * s], axis=2)
        return back.reshape(value.shape).astype(BF16)

    near_k = edge_k[REACH : 2 * REACH] + from_low[:, :WIDTH]
    near_v = edge_v[REACH : 2 * REACH] + from_low[:, WIDTH:]
    last_k = edge_k[2 * REACH : 3 * REACH] + from_high[:, :WIDTH]
    last_v = edge_v[2 * REACH : 3 * REACH] + from_high[:, WIDTH:]
    gk = gk.at[:REACH].set(turned(near_k, cosine[REACH : 2 * REACH], sine[REACH : 2 * REACH]))
    gk = gk.at[-REACH:].set(
        turned(last_k, cosine[-2 * REACH : -REACH], sine[-2 * REACH : -REACH])
    )
    gv = gv.at[:REACH].set(near_v.astype(BF16))
    gv = gv.at[-REACH:].set(last_v.astype(BF16))

    if own_slice:
        gq = after(gq, down_sum, up_own)
    heads_parts = outer_product(
        (0, 0, 0, 1), [gq, gk, gv, attended], [normed_attn, g_branch]
    )
    grad_slots, gain_part_attn = unproject(
        xs, after(gq, heads_parts), gk, gv, g_branch, gain_rows[0], heads_w
    )

    gain_parts = jnp.stack([jnp.sum(gain_part_attn, axis=0), jnp.sum(gain_part_ffn, axis=0)])
    if own_slice:
        up_sum = exchange(after(up_own, down_sum))
        token_gradient = exchange(after(grad_slots, up_sum))
        gain_grads = sum_gains(gain_parts)
        heads_sum = exchange(after(reduce_groups(heads_parts), token_gradient, gain_grads))
        down_sum, up_sum, heads_sum = (sum_rows(v) for v in (down_sum, up_sum, heads_sum))
        ff = w_act.shape[1]
        grads = (
            join_heads(heads_sum[:GROUP]).T,
            join_heads(heads_sum[GROUP : 2 * GROUP]).T,
            heads_sum[2 * GROUP : 3 * GROUP].T,
            heads_sum[3 * GROUP :],
            up_sum[:ff].T,
            up_sum[ff:].T,
            down_sum,
        )
    else:

        def share(value, inner_first):
            first, second = ("col", "row") if inner_first else ("row", "col")
            value = value if inner_first else value.T
            value = lax.psum_scatter(value, first, scatter_dimension=0, tiled=True)
            value = lax.psum_scatter(value, second, scatter_dimension=1, tiled=True)
            return lax.psum(value, "dp").astype(F32)

        token_gradient = exchange(grad_slots)
        (down_whole,) = whole_of(down_parts, 1)
        act_whole, gate_whole = whole_of(up_parts, 2)
        query_whole, key_whole, value_whole, out_whole = whole_of(heads_parts, 4)
        grads = (
            share(join_heads(query_whole), False),
            share(join_heads(key_whole), False),
            share(value_whole, False),
            share(out_whole, True),
            share(act_whole, False),
            share(gate_whole, False),
            share(down_whole, True),
        )
        totals = lax.psum(gain_parts, ("dp", "row", "col")).reshape(2, SLOTS, 256)
        gain_grads = lax.dynamic_index_in_dim(totals, lax.axis_index("row"), 1, False)
    layer_out = layer_out.reshape(-1, 256)
    token_gradient = token_gradient.reshape(-1, 256).astype(F32)
    return (layer_out, token_gradient) + grads + (gain_grads[0], gain_grads[1])


def solution(mesh):
    sizes = tuple(mesh.shape[axis] for axis in ("dp", "row", "col"))
    in_specs = (
        P(("dp", "col"), "row"),
        P("row", "col"),
        P("row", "col"),
        P("row", "col"),
        P("col", "row"),
        P("row", "col"),
        P("row", "col"),
        P("col", "row"),
        P("row"),
        P("row"),
        P(("dp", "col"), "row"),
        P(("dp", "row"), None),
        P(("dp", "row"), None),
    )
    out_specs = (
        P(("dp", "col"), "row"),
        P(("dp", "col"), "row"),
        P("row", "col"),
        P("row", "col"),
        P("row", "col"),
        P("col", "row"),
        P("row", "col"),
        P("row", "col"),
        P("col", "row"),
        P("row"),
        P("row"),
    )
    return jax.shard_map(
        functools.partial(body, *sizes),
        mesh=mesh,
        in_specs=in_specs,
        out_specs=out_specs,
        check_vma=False,
    )
```

```python
import functools
import math

import jax
import jax.numpy as jnp
from jax import lax
from jax.experimental import pallas as pl
from jax.experimental.pallas import tpu as pltpu
from jax.sharding import PartitionSpec as P

WIDTH = 1024
HEAD = 64
REACH = 64
EPSILON = 1e-05
ROPE_THETA = 10000.0
MASKED_SCORE = -1e30
LANES = 128
SLOTS = 4
GROUPS = 4
GROUP = 256
TILE = 256
QUERY = 128
VMEM = 60 * 1024 * 1024
F32 = jnp.float32
BF16 = jnp.bfloat16


def nt(left, right):
    return lax.dot_general(left, right, (((1,), (1,)), ((), ())), preferred_element_type=F32)


def nn(left, right):
    return lax.dot_general(left, right, (((1,), (0,)), ((), ())), preferred_element_type=F32)


def tn(left, right):
    return lax.dot_general(left, right, (((0,), (0,)), ((), ())), preferred_element_type=F32)


def call(kernel, grid, in_specs, out_specs, out_shape, scratch, flops, moved, name):
    return pl.pallas_call(
        kernel,
        grid=grid,
        in_specs=in_specs,
        out_specs=out_specs,
        out_shape=out_shape,
        scratch_shapes=scratch,
        compiler_params=pltpu.CompilerParams(
            vmem_limit_bytes=VMEM, dimension_semantics=("arbitrary",)
        ),
        cost_estimate=pl.CostEstimate(flops=flops, bytes_accessed=moved, transcendentals=0),
        name=name,
    )


def resident(shape):
    zeros = (0,) * len(shape)
    return pl.BlockSpec(shape, lambda i: zeros, pipeline_mode=pl.Buffered(1))


def rows_of(width, tile=TILE):
    return pl.BlockSpec((tile, width), lambda i: (i, 0))


BLOCKS = pl.BlockSpec((SLOTS, TILE, 256), lambda i: (0, i, 0))


def later_rows(width):
    return pl.BlockSpec((TILE, width), lambda i: (jnp.maximum(i - GROUPS, 0), 0))


LATER_BLOCKS = pl.BlockSpec((SLOTS, TILE, 256), lambda i: (0, jnp.maximum(i - GROUPS, 0), 0))


def group_of(i):
    return jnp.minimum(i, GROUPS - 1)


def weight_rows(rows, at=0):
    return [
        pl.BlockSpec(
            (1, SLOTS, rows, LANES), lambda i, a=a: (a * GROUPS + group_of(i), 0, at, 0)
        )
        for a in range(2)
    ]


def joined_rows(halves, p=0, rows=slice(None)):
    return jnp.concatenate([w[p, o, rows, :] for o in range(SLOTS) for w in halves], axis=1)


def at_first(run):
    pl.when(pl.program_id(0) == 0)(run)


def add_up(total, inner, weight, rows=slice(None)):
    @at_first
    def _():
        total[...] = nn(inner[0], joined_rows(weight, 0, rows))

    @pl.when(pl.program_id(0) > 0)
    def _():
        total[...] += nn(inner[0], joined_rows(weight, 0, rows))


def struct(shape, dtype):
    return jax.ShapeDtypeStruct(shape, dtype)


def whole_rows(slots, rows=slice(None)):
    return jnp.concatenate([slots[o, rows, :] for o in range(SLOTS)], axis=1)


def inner_rows(tile):
    return pl.ds(pl.multiple_of(pl.program_id(0) * tile + REACH, REACH), tile)


def put_rows(slots, total):
    for o in range(SLOTS):
        slots[o] = total[:, o * 256 : (o + 1) * 256].astype(slots.dtype)


def norm(values):
    average = jnp.mean(values, axis=1, keepdims=True)
    centered = values - average
    variance = jnp.mean(centered * centered, axis=1, keepdims=True)
    inverse = lax.rsqrt(variance + EPSILON)
    return centered * inverse, inverse


def norm_back(gradient, unit, inverse, gain):
    scaled = gradient * gain
    average = jnp.mean(scaled, axis=1, keepdims=True)
    crossed = jnp.mean(scaled * unit, axis=1, keepdims=True)
    return inverse * (scaled - average - unit * crossed)


def add_gain(gain_part, products):
    @pl.when(pl.program_id(0) == GROUPS)
    def _():
        gain_part[...] = jnp.zeros_like(gain_part)

    gain_part[...] += jnp.sum(products.reshape(-1, 8, WIDTH), axis=0)


def project_kernel(xs, gain, cosine, sine, low, high, q, k, v, normed, rows):
    @at_first
    def _():
        for at in range(0, rows.shape[0], QUERY):
            cut = slice(at, at + QUERY)
            values = jnp.concatenate([xs[o, cut, :] for o in range(SLOTS)], axis=1)
            made = (norm(values.astype(F32))[0] * gain[...]).astype(BF16)
            rows[cut, :] = made
            normed[cut, :] = made

    made = nt(rows[...], joined_rows((low, high)))
    c, s = cosine[...], sine[...]
    for t, out in ((0, q), (1, k)):
        first = made[:, t * GROUP : t * GROUP + LANES]
        second = made[:, t * GROUP + LANES : (t + 1) * GROUP]
        out[:, :LANES] = (first * c - second * s).astype(BF16)
        out[:, LANES:] = (second * c + first * s).astype(BF16)
    v[...] = made[:, 2 * GROUP :].astype(BF16)


def project(xs, gain, cosine, sine, weight):
    tokens = cosine.shape[0]
    return call(
        project_kernel,
        (GROUPS,),
        [resident(xs.shape), resident((1, WIDTH))]
        + [resident((tokens, LANES))] * 2
        + weight_rows(3 * GROUP),
        [pl.BlockSpec((tokens, GROUP), lambda i: (0, i))] * 3 + [resident((tokens, WIDTH))],
        [struct((tokens, WIDTH), BF16)] * 4,
        [pltpu.VMEM((tokens, WIDTH), BF16)],
        2 * tokens * WIDTH * 3 * WIDTH,
        10 * tokens * WIDTH + 6 * WIDTH * WIDTH,
        "project",
    )(xs, gain, cosine, sine, weight, weight)


def head_masks():
    lane = lax.broadcasted_iota(jnp.int32, (1, GROUP), 1)
    halves = [((lane % LANES) // 32 == h) for h in range(4)]
    wholes = [(lane // HEAD == h) for h in range(4)]
    return halves, wholes


def spread(rows, masks):
    return jnp.concatenate([rows * m.astype(BF16) for m in masks], axis=0)


def collect(stacked, masks):
    total = jnp.where(masks[0], stacked[0:QUERY], 0.0)
    for h in range(1, 4):
        total = jnp.where(masks[h], stacked[h * QUERY : (h + 1) * QUERY], total)
    return total


def attend_kernel(*refs):
    q, k, v, bias, xs, gain, low, high = refs[:8]
    attended, probability, mixed, normed, held = refs[8:]

    @at_first
    def _():
        for p in range(GROUPS):
            held[pl.ds(p * GROUP, GROUP), :] = joined_rows((low, high), p)

    span = pl.ds(pl.multiple_of(pl.program_id(0) * QUERY, QUERY), QUERY + 2 * REACH)
    own = inner_rows(QUERY)
    halves, wholes = head_masks()
    masked = bias[0]
    for p in range(GROUPS):
        lanes = slice(p * GROUP, (p + 1) * GROUP)
        scores = nt(spread(q[own, lanes], halves), k[span, lanes]) * HEAD**-0.5
        scores = jnp.concatenate(
            [scores[h * QUERY : (h + 1) * QUERY] + masked for h in range(4)], axis=0
        )
        exponent = jnp.exp(scores - jnp.max(scores, axis=1, keepdims=True))
        weight = (exponent * (1.0 / jnp.sum(exponent, axis=1, keepdims=True))).astype(BF16)
        probability[0, p] = weight
        attended[:, lanes] = collect(nn(weight, v[span, lanes]), wholes).astype(BF16)
    total = whole_rows(xs, own).astype(F32) + nn(attended[...], held[...])
    mixed[...] = total.astype(BF16)
    normed[...] = (norm(total)[0] * gain[...]).astype(BF16)


def out_weight():
    return [
        pl.BlockSpec(
            (GROUPS, SLOTS, GROUP, LANES), lambda i, a=a: (a, 0, 3, 0), pipeline_mode=pl.Buffered(1)
        )
        for a in range(2)
    ]


def attend(q, k, v, bias, xs, gain, heads):
    blocks, _, span = bias.shape
    tokens = blocks * QUERY
    return call(
        attend_kernel,
        (blocks,),
        [resident(q.shape)] * 3
        + [pl.BlockSpec((1, QUERY, span), lambda i: (i, 0, 0))]
        + [resident(xs.shape), resident((1, WIDTH))]
        + out_weight(),
        [
            rows_of(WIDTH, QUERY),
            pl.BlockSpec((1, GROUPS, 4 * QUERY, span), lambda i: (i, 0, 0, 0)),
            rows_of(WIDTH, QUERY),
            rows_of(WIDTH, QUERY),
        ],
        [
            struct((tokens, WIDTH), BF16),
            struct((blocks, GROUPS, 4 * QUERY, span), BF16),
            struct((tokens, WIDTH), BF16),
            struct((tokens, WIDTH), BF16),
        ],
        [pltpu.VMEM((WIDTH, WIDTH), BF16)],
        blocks * GROUPS * 2 * 2 * 4 * QUERY * span * GROUP + 2 * tokens * WIDTH * WIDTH,
        14 * tokens * WIDTH + blocks * GROUPS * 8 * QUERY * span,
        "attend",
    )(q, k, v, bias, xs, gain, heads, heads)


def attend_back_kernel(*refs):
    q, grad, weights, k, v, cosine, sine = refs[:7]
    gq, gk, gv, to_low, to_high, edges, sum_k, sum_v = refs[7:]
    step, steps = pl.program_id(0), pl.num_programs(0)
    tokens = gk.shape[0]

    @at_first
    def _():
        sum_k[...] = jnp.zeros_like(sum_k)
        sum_v[...] = jnp.zeros_like(sum_v)

    start = pl.multiple_of(step * QUERY, QUERY)
    span = pl.ds(start, QUERY + 2 * REACH)
    halves, wholes = head_masks()
    own = inner_rows(QUERY)
    c, s = cosine[own, :], sine[own, :]
    for p in range(GROUPS):
        lanes = slice(p * GROUP, (p + 1) * GROUP)
        queries = spread(q[own, lanes], halves)
        grads = spread(grad[:, lanes], wholes)
        block_k, block_v = k[span, lanes], v[span, lanes]
        weight = weights[0, p]
        wide = weight.astype(F32)
        d_weight = nt(grads, block_v)
        mean = jnp.sum(wide * d_weight, axis=1, keepdims=True)
        g_score = (wide * (d_weight - mean)).astype(BF16)
        made = collect(nn(g_score, block_k), halves) * HEAD**-0.5
        first, second = made[:, :LANES], made[:, LANES:]
        gq[:, p * GROUP : p * GROUP + LANES] = (first * c + second * s).astype(BF16)
        gq[:, p * GROUP + LANES : (p + 1) * GROUP] = (second * c - first * s).astype(BF16)
        sum_k[span, lanes] += tn(g_score, queries) * HEAD**-0.5
        sum_v[span, lanes] += tn(weight, grads)

    @pl.when(step == steps - 1)
    def _():
        for t, total in ((0, sum_k), (1, sum_v)):
            lanes = slice(t * WIDTH, (t + 1) * WIDTH)
            to_low[:, lanes] = total[0:REACH, :].astype(BF16)
            edges[0, :, lanes] = total[REACH : 2 * REACH, :]
            edges[1, :, lanes] = total[pl.ds(tokens, REACH), :]
            to_high[:, lanes] = total[pl.ds(tokens + REACH, REACH), :].astype(BF16)
        for at in range(0, tokens, QUERY):
            own = pl.ds(REACH + at, QUERY)
            c, s = cosine[own, :], sine[own, :]
            for p in range(GROUPS):
                one, two = p * GROUP, p * GROUP + LANES
                first, second = sum_k[own, pl.ds(one, LANES)], sum_k[own, pl.ds(two, LANES)]
                gk[pl.ds(at, QUERY), pl.ds(one, LANES)] = (first * c + second * s).astype(BF16)
                gk[pl.ds(at, QUERY), pl.ds(two, LANES)] = (second * c - first * s).astype(BF16)
            gv[pl.ds(at, QUERY), :] = sum_v[own, :].astype(BF16)


def attend_back(q, grad, weights, k, v, cosine, sine):
    tokens = grad.shape[0]
    blocks = tokens // QUERY
    span = QUERY + 2 * REACH
    full = resident((tokens, WIDTH))
    edge = (REACH, 2 * WIDTH)
    return call(
        attend_back_kernel,
        (blocks,),
        [
            resident(q.shape),
            rows_of(WIDTH, QUERY),
            pl.BlockSpec((1, GROUPS, 4 * QUERY, span), lambda i: (i, 0, 0, 0)),
            resident(q.shape),
            resident(q.shape),
            resident(cosine.shape),
            resident(cosine.shape),
        ],
        [rows_of(WIDTH, QUERY), full, full, resident(edge), resident(edge), resident((2,) + edge)],
        [struct((tokens, WIDTH), BF16)] * 3 + [struct(edge, BF16)] * 2 + [struct((2,) + edge, F32)],
        [pltpu.VMEM(q.shape, F32)] * 2,
        blocks * GROUPS * 2 * 4 * 4 * QUERY * span * GROUP,
        14 * tokens * WIDTH + blocks * GROUPS * 8 * QUERY * span,
        "attend_back",
    )(q, grad, weights, k, v, cosine, sine)


def edge_kernel(*refs):
    edges, from_low, from_high, cosine, sine = refs[2:7]
    gk, gv = refs[7:]

    def finish(came):
        c, s = cosine[...], sine[...]
        for p in range(GROUPS):
            one = slice(p * GROUP, p * GROUP + LANES)
            two = slice(p * GROUP + LANES, (p + 1) * GROUP)
            first = edges[0, :, one] + came[:, one].astype(F32)
            second = edges[0, :, two] + came[:, two].astype(F32)
            gk[:, one] = (first * c + second * s).astype(BF16)
            gk[:, two] = (second * c - first * s).astype(BF16)
        gv[...] = (edges[0, :, WIDTH:] + came[:, WIDTH:].astype(F32)).astype(BF16)

    pl.when(pl.program_id(0) == 0)(lambda: finish(from_low))
    pl.when(pl.program_id(0) == 1)(lambda: finish(from_high))


def add_edges(gk, gv, edges, from_low, from_high, cosine, sine):
    tokens = gk.shape[0]
    far = tokens // REACH - 1
    rows = pl.BlockSpec((REACH, WIDTH), lambda i: (i * far, 0))
    table = pl.BlockSpec((REACH, LANES), lambda i: (1 + i * far, 0))
    came = resident(from_low.shape)
    return pl.pallas_call(
        edge_kernel,
        grid=(2,),
        in_specs=[pl.BlockSpec(memory_space=pl.ANY)] * 2
        + [pl.BlockSpec((1, REACH, 2 * WIDTH), lambda i: (i, 0, 0)), came, came, table, table],
        out_specs=[rows] * 2,
        out_shape=[struct(gk.shape, BF16)] * 2,
        input_output_aliases={0: 0, 1: 1},
        compiler_params=pltpu.CompilerParams(
            vmem_limit_bytes=VMEM, dimension_semantics=("arbitrary",)
        ),
        cost_estimate=pl.CostEstimate(flops=1, bytes_accessed=2**21, transcendentals=0),
        name="add_edges",
    )(gk, gv, edges, from_low, from_high, cosine, sine)


def step_rows():
    return pl.ds(pl.multiple_of((pl.program_id(0) - GROUPS) * TILE, TILE), TILE)


def between_rows():
    at = (pl.program_id(0) - GROUPS) * TILE + REACH
    return pl.ds(pl.multiple_of(at, REACH), TILE)


def feed_kernel(*refs):
    normed, mixed, weight = refs[0], refs[1], refs[2:4]
    hidden, slope, gelu, early, late, total = refs[4:]
    ff = hidden.shape[2]
    half = GROUPS + total.shape[0] // TILE // 2
    step = pl.program_id(0)

    @pl.when(step < GROUPS)
    def _():
        act = nt(normed[...], joined_rows(weight, 0, slice(0, ff)))
        gate = nt(normed[...], joined_rows(weight, 0, slice(ff, 2 * ff)))
        spread_to = 0.5 * (1.0 + lax.erf(act * math.sqrt(0.5)))
        curve = act * spread_to
        density = jnp.exp(act * act * -0.5) * (1.0 / math.sqrt(2.0 * math.pi))
        slope[0] = (gate * (spread_to + act * density)).astype(BF16)
        gelu[0] = curve.astype(BF16)
        hidden[0] = (curve * gate).astype(BF16)
        add_up(total, hidden, weight, slice(2 * ff, 3 * ff))

    @pl.when((step >= GROUPS) & (step < half))
    def _():
        put_rows(early, mixed[...].astype(F32) + total[step_rows(), :])

    @pl.when(step >= half)
    def _():
        put_rows(late, mixed[...].astype(F32) + total[step_rows(), :])


def units_of(tokens, ff):
    return pl.BlockSpec((1, tokens, ff), lambda i: (group_of(i), 0, 0))


def feed(normed, mixed, weight):
    tokens, ff = normed.shape[0], weight.shape[2] // 3
    steps = tokens // TILE // 2
    return call(
        feed_kernel,
        (GROUPS + tokens // TILE,),
        [resident((tokens, WIDTH)), later_rows(WIDTH)] + weight_rows(3 * ff),
        [units_of(tokens, ff)] * 3
        + [
            pl.BlockSpec(
                (SLOTS, TILE, 256),
                lambda i, first=first: (0, jnp.clip(i - GROUPS - first, 0, steps - 1), 0),
            )
            for first in (0, steps)
        ],
        [struct((GROUPS, tokens, ff), BF16)] * 3
        + [struct((SLOTS, tokens // 2, 256), BF16)] * 2,
        [pltpu.VMEM((tokens, WIDTH), F32)],
        2 * tokens * WIDTH * 3 * GROUPS * ff,
        6 * tokens * WIDTH + 6 * GROUPS * ff * (tokens + WIDTH),
        "feed",
    )(normed, mixed, weight, weight)


def feed_back_kernel(*refs):
    cots, slope, gelu, mixed, gain = refs[:5]
    weight, outward = refs[5:7], refs[7:9]
    g_act, g_gate, g_branch, g_attended, gain_part, cot, total = refs[9:]
    ff = g_act.shape[2]

    @at_first
    def _():
        cot[...] = whole_rows(cots)

    @pl.when(pl.program_id(0) < GROUPS)
    def _():
        g_hidden = nt(cot[...], joined_rows(weight, 0, slice(2 * ff, 3 * ff)))
        g_act[0] = (g_hidden * slope[0].astype(F32)).astype(BF16)
        g_gate[0] = (g_hidden * gelu[0].astype(F32)).astype(BF16)
        add_up(total, g_act, weight, slice(0, ff))
        total[...] += nn(g_gate[0], joined_rows(weight, 0, slice(ff, 2 * ff)))

    @pl.when(pl.program_id(0) >= GROUPS)
    def _():
        gradient = total[step_rows(), :]
        unit, inverse = norm(mixed[...].astype(F32))
        add_gain(gain_part, gradient * unit)
        made = cot[step_rows(), :].astype(F32) + norm_back(gradient, unit, inverse, gain[...])
        branch = made.astype(BF16)
        g_branch[...] = branch
        for p in range(GROUPS):
            lanes = slice(p * GROUP, (p + 1) * GROUP)
            g_attended[:, lanes] = nt(branch, joined_rows(outward, p)).astype(BF16)


def feed_back(cots, slope, gelu, mixed, gain, weight, heads):
    _, tokens, ff = slope.shape
    return call(
        feed_back_kernel,
        (GROUPS + tokens // TILE,),
        [resident(cots.shape)]
        + [units_of(tokens, ff)] * 2
        + [later_rows(WIDTH), resident((1, WIDTH))]
        + weight_rows(3 * ff)
        + out_weight(),
        [units_of(tokens, ff)] * 2 + [later_rows(WIDTH)] * 2 + [resident((8, WIDTH))],
        [struct((GROUPS, tokens, ff), BF16)] * 2
        + [struct((tokens, WIDTH), BF16)] * 2
        + [struct((8, WIDTH), F32)],
        [pltpu.VMEM((tokens, WIDTH), BF16), pltpu.VMEM((tokens, WIDTH), F32)],
        2 * tokens * WIDTH * (3 * GROUPS * ff + WIDTH),
        8 * tokens * WIDTH + 6 * GROUPS * ff * (tokens + WIDTH),
        "feed_back",
    )(cots, slope, gelu, mixed, gain, weight, weight, heads, heads)


def unproject_kernel(xs, gq, gk, gv, g_branch, gain, low, high, outs, gain_part, held, total):
    @pl.when(pl.program_id(0) < GROUPS)
    def _():
        held[0] = jnp.concatenate([gq[...], gk[...], gv[...]], axis=1)
        add_up(total, held, (low, high))

    @pl.when(pl.program_id(0) >= GROUPS)
    def _():
        gradient = total[step_rows(), :]
        unit, inverse = norm(whole_rows(xs, between_rows()).astype(F32))
        add_gain(gain_part, gradient * unit)
        back = norm_back(gradient, unit, inverse, gain[...])
        put_rows(outs, g_branch[...].astype(F32) + back)


def unproject(xs, gq, gk, gv, g_branch, gain, weight):
    tokens = gq.shape[0]
    return call(
        unproject_kernel,
        (GROUPS + tokens // TILE,),
        [resident(xs.shape)]
        + [pl.BlockSpec((tokens, GROUP), lambda i: (0, group_of(i)))] * 3
        + [later_rows(WIDTH), resident((1, WIDTH))]
        + weight_rows(3 * GROUP),
        [LATER_BLOCKS, resident((8, WIDTH))],
        [struct((SLOTS, tokens, 256), BF16), struct((8, WIDTH), F32)],
        [pltpu.VMEM((1, tokens, 3 * GROUP), BF16), pltpu.VMEM((tokens, WIDTH), F32)],
        2 * tokens * WIDTH * 3 * WIDTH,
        12 * tokens * WIDTH + 6 * WIDTH * WIDTH,
        "unproject",
    )(xs, gq, gk, gv, g_branch, gain, weight, weight)


def outer_kernel(count, *refs):
    inner, outer, out = refs[:count], refs[count : 2 * count], refs[-1]
    tokens = inner[0].shape[-2]

    def make(left, right):
        left = left[0] if len(left.shape) == 3 else left[...]
        if len(right.shape) == 3:
            right = whole_rows(right)
        else:
            right = right[pl.ds((right.shape[0] - tokens) // 2, tokens), :]
        made = tn(left, right)
        for a in range(2):
            for o in range(SLOTS):
                at = o * 256 + a * LANES
                out[a, 0, o] = made[:, at : at + LANES].astype(BF16)

    for t in range(count):
        pl.when(pl.program_id(0) % count == t)(functools.partial(make, inner[t], outer[t]))


def outer_product(inner, outer, places, kinds, base=None):
    count = len(inner)
    tokens = inner[0].shape[-2]
    width = inner[0].shape[2] if inner[0].ndim == 3 else GROUP
    stride = places[-1] - places[0]

    def inner_block(value):
        if value.ndim == 3:
            return pl.BlockSpec((1, tokens, width), lambda i: (i // count, 0, 0))
        return pl.BlockSpec((tokens, GROUP), lambda i: (0, i // count))

    more = [] if base is None else [base]
    moved = 8 * count * width * (tokens + WIDTH) + 2 * tokens * WIDTH
    return pl.pallas_call(
        functools.partial(outer_kernel, count),
        grid=(GROUPS * count,),
        in_specs=[inner_block(value) for value in inner]
        + [resident(value.shape) for value in outer]
        + [pl.BlockSpec(memory_space=pl.ANY) for _ in more],
        out_specs=pl.BlockSpec(
            (2, 1, SLOTS, width, LANES),
            lambda i: (0, i // count, 0, places[0] + i % count * stride, 0),
        ),
        out_shape=struct((2, GROUPS, SLOTS, kinds * width, LANES), BF16),
        input_output_aliases={2 * count: 0} if more else {},
        compiler_params=pltpu.CompilerParams(
            vmem_limit_bytes=VMEM, dimension_semantics=("arbitrary",)
        ),
        cost_estimate=pl.CostEstimate(
            flops=2 * tokens * GROUPS * count * width * WIDTH,
            bytes_accessed=moved,
            transcendentals=0,
        ),
        name="outer_product",
    )(*inner, *outer, *more)


def over_dp(value):
    return lax.ppermute(value, "dp", [(0, 1), (1, 0)])


def over_chip(value):
    return lax.ppermute(value, "col", [(i, i ^ 2) for i in range(4)])


def over_core(value):
    return lax.ppermute(value, "col", [(i, i ^ 1) for i in range(4)])


def exchange(value):
    return lax.all_to_all(value, "row", 0, 0)


def after(value, *earlier):
    return lax.optimization_barrier((value,) + earlier)[0]


def own_half(shard):
    return lax.dynamic_slice_in_dim(shard, lax.axis_index("dp") * LANES, LANES, 1)


def gather_rows(half):
    return exchange(jnp.broadcast_to(half, (SLOTS,) + half.shape))


def gather_groups(own):
    return lax.all_gather(own, ("dp", "col"), axis=0, tiled=False)


def reduce_groups(parts):
    parts = parts.reshape((2 * GROUPS,) + parts.shape[2:])
    return lax.psum_scatter(parts, ("dp", "col"), scatter_dimension=0, tiled=False)


def sum_rows(parts):
    half = jnp.sum(parts.astype(F32), axis=0).astype(BF16)
    other = over_dp(half)
    first = lax.axis_index("dp") == 0
    return jnp.where(first, half, other), jnp.where(first, other, half)


def finish_kernel(kinds, width, low, high, *outs):
    for t, (kind, out) in enumerate(zip(kinds, outs, strict=True)):
        rows = slice(t * width, (t + 1) * width)
        value = jnp.concatenate([low[rows, :], high[rows, :]], axis=1).astype(F32)
        if kind not in "qkv":
            out[...] = value
            continue
        if kind in "qk":
            cuts = [value[at * 32 : (at + 1) * 32] for at in (0, 4, 1, 5, 2, 6, 3, 7)]
            value = jnp.concatenate(cuts, axis=0)
        out[...] = value.T


def finish(halves, kinds, width):
    return pl.pallas_call(
        functools.partial(finish_kernel, kinds, width),
        out_shape=[struct((256, width) if kind in "qkv" else (width, 256), F32) for kind in kinds],
        compiler_params=pltpu.CompilerParams(vmem_limit_bytes=VMEM),
        cost_estimate=pl.CostEstimate(flops=1, bytes_accessed=2**21, transcendentals=0),
        name="finish",
    )(*halves)


def sum_gains(parts):
    both = parts + over_dp(parts)
    both = both + over_chip(both)
    both = both + over_core(both)
    for bit in (1, 2):
        both = both + lax.ppermute(both, "row", [(i, i ^ bit) for i in range(SLOTS)])
    return lax.dynamic_slice_in_dim(both, lax.axis_index("row") * 256, 256, 1)


def groups_of(whole):
    rows = whole.shape[0] // GROUPS
    cut = whole.reshape(GROUPS, rows, SLOTS, 2, LANES).transpose(3, 0, 2, 1, 4)
    return cut.reshape(2 * GROUPS, SLOTS, rows, LANES)


def whole_of(parts, types):
    cut = parts.transpose(1, 3, 2, 0, 4).reshape(GROUPS, types, -1, WIDTH)
    return [cut[:, t].reshape(-1, WIDTH) for t in range(types)]


def split_heads(rows):
    return rows.reshape(-1, 4, 2, 32, rows.shape[1]).swapaxes(1, 2).reshape(rows.shape)


def join_heads(rows):
    return rows.reshape(-1, 2, 4, 32, rows.shape[1]).swapaxes(1, 2).reshape(rows.shape)


def positions_and_masks(segments, valid, first, tokens):
    length = segments.shape[0]
    index = first - REACH + jnp.arange(tokens + 2 * REACH, dtype=jnp.int32)
    pads = (REACH, REACH)
    near = lax.dynamic_slice_in_dim(jnp.pad(segments, pads), first, tokens + 2 * REACH, 0)
    ids = jnp.arange(64, dtype=jnp.int32)
    before = jnp.sum((segments[None, :] < ids[:, None]).astype(jnp.int32), axis=1)
    begin = jnp.sum(jnp.where(near[:, None] == ids[None, :], before[None, :], 0), axis=1)
    where_in = (index - begin).astype(F32)
    frequency = ROPE_THETA ** (-((jnp.arange(LANES) % 32).astype(F32) * 2.0) / HEAD)
    angles = where_in[:, None] * frequency[None, :]
    code = jnp.pad(jnp.where(valid == 1, segments, -1), pads, constant_values=-1)
    code = lax.dynamic_slice_in_dim(code, first, tokens + 2 * REACH, 0)
    span = QUERY + 2 * REACH
    keys = jnp.stack([code[i : i + span] for i in range(0, tokens, QUERY)])[:, None, :]
    queries = near[REACH:-REACH].reshape(-1, QUERY, 1)
    shape = (tokens // QUERY, QUERY, span)
    offset = (
        lax.broadcasted_iota(jnp.int32, shape, 2)
        - lax.broadcasted_iota(jnp.int32, shape, 1)
        - REACH
    )
    allowed = (jnp.abs(offset) <= REACH) & ((queries == keys) | (offset == 0))
    return jnp.cos(angles), jnp.sin(angles), jnp.where(allowed, 0.0, MASKED_SCORE).astype(F32)


def body(
    dp,
    rows,
    cols,
    tokens_in,
    w_query,
    w_key,
    w_value,
    w_out,
    w_act,
    w_gate,
    w_down,
    gain_attn,
    gain_ffn,
    cotangent,
    segment_ids,
    valid_mask,
):
    tokens = tokens_in.shape[0] // rows
    length = segment_ids.shape[1]
    own_slice = (dp, rows, cols) == (2, 4, 4) and rows * tokens == length
    gains = jnp.stack([gain_attn, gain_ffn])
    at = (lax.axis_index("col") * rows + lax.axis_index("row")) * tokens
    sequence, first = at // length, at % length
    count = rows * cols
    joins = [i for i in range(count - 1) if ((i + 1) * tokens) % length]
    upward, downward = [(i, i + 1) for i in joins], [(i + 1, i) for i in joins]

    def shift(value, perm):
        place_of = [(i % rows) * cols + i // rows for i in range(count)]
        return lax.ppermute(value, ("row", "col"), [(place_of[i], place_of[j]) for i, j in perm])

    if own_slice:
        marks = jnp.concatenate([segment_ids, valid_mask]).astype(BF16).reshape(-1, LANES)
        heads_half = jnp.concatenate(
            [
                split_heads(own_half(w_query.T)),
                split_heads(own_half(w_key.T)),
                own_half(w_value.T),
                own_half(w_out),
                marks,
                gains.reshape(4, LANES),
                jnp.zeros((12, LANES), BF16),
            ],
            axis=0,
        )
        feed_half = jnp.concatenate(
            [own_half(w_act.T), own_half(w_gate.T), own_half(w_down)], axis=0
        )
        padded = jnp.pad(tokens_in, ((REACH, REACH), (0, 0)))
        spans = [padded[j * tokens : (j + 1) * tokens + 2 * REACH] for j in range(rows)]
        heads_own = gather_rows(heads_half)
        heads_w = gather_groups(heads_own[:, :WIDTH])
        feed_own = gather_rows(after(feed_half, heads_own))
        feed_w = gather_groups(feed_own)
        last = WIDTH + marks.shape[0]
        marks = heads_own[:, WIDTH:last].reshape(rows, 2, length)
        marks = lax.dynamic_index_in_dim(marks, sequence, 0, False).astype(jnp.int32)
        gain_slots = heads_own[:, last : last + 4].reshape(SLOTS, 2, 256)
        tables = positions_and_masks(*marks, first, tokens)
        xs = exchange(after(jnp.stack(spans), feed_own))
        cots = exchange(after(cotangent.reshape(rows, tokens, 256), xs))
    else:
        xs = exchange(tokens_in.reshape(rows, tokens, 256))
        below, above = shift(xs[:, -REACH:], upward), shift(xs[:, :REACH], downward)
        xs = jnp.concatenate([below, xs, above], axis=1)
        cots = exchange(cotangent.reshape(rows, tokens, 256))
        gain_slots = exchange(jnp.broadcast_to(gains, (rows, 2, 256)))
        marks = lax.all_gather(jnp.stack([segment_ids, valid_mask]), "row", axis=1, tiled=True)
        marks = lax.dynamic_index_in_dim(marks, sequence, 1, False)
        tables = positions_and_masks(*marks, first, tokens)

        def full(value, inner_first):
            first, second = ("col", "row") if inner_first else ("row", "col")
            value = lax.all_gather(value, first, axis=0, tiled=True)
            value = lax.all_gather(value, second, axis=1, tiled=True)
            return value if inner_first else value.T

        def joined(*parts):
            return jnp.concatenate([groups_of(part) for part in parts], axis=2)

        heads_w = joined(
            split_heads(full(w_query, False)),
            split_heads(full(w_key, False)),
            full(w_value, False),
            full(w_out, True),
        )
        feed_w = joined(full(w_act, False), full(w_gate, False), full(w_down, True))
    gain_rows = gain_slots.swapaxes(0, 1).reshape(2, 1, WIDTH).astype(F32)
    cosine, sine, bias = tables

    q, k, v, normed_attn = project(xs, gain_rows[0], cosine, sine, heads_w)
    attended, weights, mixed, normed_ffn = attend(q, k, v, bias, xs, gain_rows[1], heads_w)
    hidden, slope, gelu, early, late = feed(normed_ffn, mixed, feed_w)
    early = exchange(after(early, cots))
    down_parts = outer_product([hidden], [cots], (0,), 1)
    g_act, g_gate, g_branch, g_attended, gain_part_ffn = feed_back(
        cots, after(slope, down_parts), gelu, mixed, gain_rows[1], feed_w, heads_w
    )
    up_parts = outer_product([after(g_act, early), g_gate], [normed_ffn] * 2, (0, 1), 2)
    if own_slice:
        down_own, up_own = reduce_groups(down_parts), reduce_groups(up_parts)
        g_attended = after(g_attended, up_parts, down_own)
    gq, gk, gv, to_low, to_high, edges = attend_back(
        q, g_attended, weights, k, v, cosine, sine
    )
    from_low, from_high = shift(to_high, upward), shift(to_low, downward)
    if own_slice:
        rest = down_own.reshape(rows, -1, 256)
        late, rest = jnp.split(
            exchange(jnp.concatenate([after(late, early), rest], axis=1)), [tokens // 2], axis=1
        )
        down_sum = rest.reshape(down_own.shape)
        gq = after(gq, late, down_sum)
    else:
        late = exchange(late)
    layer_out = jnp.concatenate([early, late], axis=1)
    heads_parts = outer_product([gq, attended], [normed_attn, g_branch], (0, 3), 4)
    from_low = after(from_low, heads_parts)
    gk, gv = add_edges(gk, gv, edges, from_low, from_high, cosine, sine)
    heads_parts = outer_product([gk, gv], [normed_attn] * 2, (1, 2), 4, heads_parts)
    grad_slots, gain_part_attn = unproject(
        xs, after(gq, heads_parts), gk, gv, g_branch, gain_rows[0], heads_w
    )

    gain_parts = jnp.stack([jnp.sum(gain_part_attn, axis=0), jnp.sum(gain_part_ffn, axis=0)])
    if own_slice:
        token_gradient = exchange(after(grad_slots, down_sum))
        up_sum = exchange(after(up_own, token_gradient))
        gain_grads = sum_gains(gain_parts)
        heads_sum = exchange(after(reduce_groups(heads_parts), up_sum, gain_grads))
        ff = w_act.shape[1]
        grads = (
            *finish(sum_rows(heads_sum), "qkvo", GROUP),
            *(value.T for value in finish(sum_rows(up_sum), "ag", ff)),
            *finish(sum_rows(down_sum), "d", ff),
        )
    else:

        def share(value, inner_first):
            first, second = ("col", "row") if inner_first else ("row", "col")
            value = value if inner_first else value.T
            value = lax.psum_scatter(value, first, scatter_dimension=0, tiled=True)
            value = lax.psum_scatter(value, second, scatter_dimension=1, tiled=True)
            return lax.psum(value, "dp").astype(F32)

        token_gradient = exchange(grad_slots)
        (down_whole,) = whole_of(down_parts, 1)
        act_whole, gate_whole = whole_of(up_parts, 2)
        query_whole, key_whole, value_whole, out_whole = whole_of(heads_parts, 4)
        grads = (
            share(join_heads(query_whole), False),
            share(join_heads(key_whole), False),
            share(value_whole, False),
            share(out_whole, True),
            share(act_whole, False),
            share(gate_whole, False),
            share(down_whole, True),
        )
        totals = lax.psum(gain_parts, ("dp", "row", "col")).reshape(2, SLOTS, 256)
        gain_grads = lax.dynamic_index_in_dim(totals, lax.axis_index("row"), 1, False)
    layer_out = layer_out.reshape(-1, 256)
    token_gradient = token_gradient.reshape(-1, 256).astype(F32)
    return (layer_out, token_gradient) + grads + (gain_grads[0], gain_grads[1])


def solution(mesh):
    sizes = tuple(mesh.shape[axis] for axis in ("dp", "row", "col"))
    in_specs = (
        P(("dp", "col"), "row"),
        P("row", "col"),
        P("row", "col"),
        P("row", "col"),
        P("col", "row"),
        P("row", "col"),
        P("row", "col"),
        P("col", "row"),
        P("row"),
        P("row"),
        P(("dp", "col"), "row"),
        P(("dp", "row"), None),
        P(("dp", "row"), None),
    )
    out_specs = (
        P(("dp", "col"), "row"),
        P(("dp", "col"), "row"),
        P("row", "col"),
        P("row", "col"),
        P("row", "col"),
        P("col", "row"),
        P("row", "col"),
        P("row", "col"),
        P("col", "row"),
        P("row"),
        P("row"),
    )
    return jax.shard_map(
        functools.partial(body, *sizes),
        mesh=mesh,
        in_specs=in_specs,
        out_specs=out_specs,
        check_vma=False,
    )
```

```python
import functools
import math

import jax
import jax.numpy as jnp
from jax import lax
from jax.experimental import pallas as pl
from jax.experimental.pallas import tpu as pltpu
from jax.sharding import PartitionSpec as P

WIDTH = 1024
HEAD = 64
REACH = 64
EPSILON = 1e-05
ROPE_THETA = 10000.0
MASKED_SCORE = -1e30
LANES = 128
SLOTS = 4
GROUPS = 4
GROUP = 256
TILE = 256
QUERY = 128
VMEM = 60 * 1024 * 1024
F32 = jnp.float32
BF16 = jnp.bfloat16


def nt(left, right):
    return lax.dot_general(left, right, (((1,), (1,)), ((), ())), preferred_element_type=F32)


def nn(left, right):
    return lax.dot_general(left, right, (((1,), (0,)), ((), ())), preferred_element_type=F32)


def tn(left, right):
    return lax.dot_general(left, right, (((0,), (0,)), ((), ())), preferred_element_type=F32)


def call(kernel, grid, in_specs, out_specs, out_shape, scratch, flops, moved, name):
    return pl.pallas_call(
        kernel,
        grid=grid,
        in_specs=in_specs,
        out_specs=out_specs,
        out_shape=out_shape,
        scratch_shapes=scratch,
        compiler_params=pltpu.CompilerParams(
            vmem_limit_bytes=VMEM, dimension_semantics=("arbitrary",)
        ),
        cost_estimate=pl.CostEstimate(flops=flops, bytes_accessed=moved, transcendentals=0),
        name=name,
    )


def resident(shape):
    zeros = (0,) * len(shape)
    return pl.BlockSpec(shape, lambda i: zeros, pipeline_mode=pl.Buffered(1))


def rows_of(width, tile=TILE):
    return pl.BlockSpec((tile, width), lambda i: (i, 0))


BLOCKS = pl.BlockSpec((SLOTS, TILE, 256), lambda i: (0, i, 0))


def later_rows(width):
    return pl.BlockSpec((TILE, width), lambda i: (jnp.maximum(i - GROUPS, 0), 0))


LATER_BLOCKS = pl.BlockSpec((SLOTS, TILE, 256), lambda i: (0, jnp.maximum(i - GROUPS, 0), 0))


def group_of(i):
    return jnp.minimum(i, GROUPS - 1)


def weight_rows(rows, at=0):
    return [
        pl.BlockSpec(
            (1, SLOTS, rows, LANES), lambda i, a=a: (a * GROUPS + group_of(i), 0, at, 0)
        )
        for a in range(2)
    ]


def joined_rows(halves, p=0, rows=slice(None)):
    return jnp.concatenate([w[p, o, rows, :] for o in range(SLOTS) for w in halves], axis=1)


def at_first(run):
    pl.when(pl.program_id(0) == 0)(run)


def add_up(total, inner, weight, rows=slice(None)):
    @at_first
    def _():
        total[...] = nn(inner[0], joined_rows(weight, 0, rows))

    @pl.when(pl.program_id(0) > 0)
    def _():
        total[...] += nn(inner[0], joined_rows(weight, 0, rows))


def struct(shape, dtype):
    return jax.ShapeDtypeStruct(shape, dtype)


def whole_rows(slots, rows=slice(None)):
    return jnp.concatenate([slots[o, rows, :] for o in range(SLOTS)], axis=1)


def put_rows(slots, total):
    for o in range(SLOTS):
        slots[o] = total[:, o * 256 : (o + 1) * 256].astype(slots.dtype)


def norm(values):
    average = jnp.mean(values, axis=1, keepdims=True)
    centered = values - average
    variance = jnp.mean(centered * centered, axis=1, keepdims=True)
    inverse = lax.rsqrt(variance + EPSILON)
    return centered * inverse, inverse


def norm_back(gradient, unit, inverse, gain):
    scaled = gradient * gain
    average = jnp.mean(scaled, axis=1, keepdims=True)
    crossed = jnp.mean(scaled * unit, axis=1, keepdims=True)
    return inverse * (scaled - average - unit * crossed)


def add_gain(gain_part, products):
    @pl.when(pl.program_id(0) == GROUPS)
    def _():
        gain_part[...] = jnp.zeros_like(gain_part)

    gain_part[...] += jnp.sum(products.reshape(-1, 8, WIDTH), axis=0)


def project_kernel(xs, gain, cosine, sine, low, high, q, k, v, normed, rows):
    @at_first
    def _():
        for at in range(0, rows.shape[0], QUERY):
            cut = slice(at, at + QUERY)
            values = jnp.concatenate([xs[o, cut, :] for o in range(SLOTS)], axis=1)
            made = (norm(values.astype(F32))[0] * gain[...]).astype(BF16)
            rows[cut, :] = made
            normed[cut, :] = made

    made = nt(rows[...], joined_rows((low, high)))
    c, s = cosine[...], sine[...]
    for t, out, scale in ((0, q, HEAD**-0.5), (1, k, 1.0)):
        first = made[:, t * GROUP : t * GROUP + LANES] * scale
        second = made[:, t * GROUP + LANES : (t + 1) * GROUP] * scale
        out[:, :LANES] = (first * c - second * s).astype(BF16)
        out[:, LANES:] = (second * c + first * s).astype(BF16)
    v[...] = made[:, 2 * GROUP :].astype(BF16)


def project(xs, gain, cosine, sine, weight):
    tokens = cosine.shape[0]
    return call(
        project_kernel,
        (GROUPS,),
        [resident(xs.shape), resident((1, WIDTH))]
        + [resident((tokens, LANES))] * 2
        + weight_rows(3 * GROUP),
        [pl.BlockSpec((tokens, GROUP), lambda i: (0, i))] * 3 + [resident((tokens, WIDTH))],
        [struct((tokens, WIDTH), BF16)] * 4,
        [pltpu.VMEM((tokens, WIDTH), BF16)],
        2 * tokens * WIDTH * 3 * WIDTH,
        10 * tokens * WIDTH + 6 * WIDTH * WIDTH,
        "project",
    )(xs, gain, cosine, sine, weight, weight)


def head_masks():
    lane = lax.broadcasted_iota(jnp.int32, (1, GROUP), 1)
    halves = [((lane % LANES) // 32 == h) for h in range(4)]
    wholes = [(lane // HEAD == h) for h in range(4)]
    return halves, wholes


def spread(rows, masks):
    return jnp.concatenate([rows * m.astype(BF16) for m in masks], axis=0)


def collect(stacked, masks):
    total = jnp.where(masks[0], stacked[0:QUERY], 0.0)
    for h in range(1, 4):
        total = jnp.where(masks[h], stacked[h * QUERY : (h + 1) * QUERY], total)
    return total


def pair(refs, lanes=slice(None)):
    return jnp.concatenate([ref[:, lanes] for ref in refs], axis=0)


def pair_of(shape):
    lead = len(shape) - 2
    return [
        pl.BlockSpec(
            shape[:lead] + (QUERY, shape[-1]),
            lambda i, more=more: (0,) * lead + (i + more, 0),
        )
        for more in range(2)
    ]


MIDDLE = slice(REACH, REACH + QUERY)


def attend_kernel(*refs):
    q, k, v, xs = (refs[2 * t : 2 * t + 2] for t in range(4))
    bias, gain, low, high = refs[8:12]
    attended, probability, mixed, normed, held = refs[12:]

    @at_first
    def _():
        for p in range(GROUPS):
            held[pl.ds(p * GROUP, GROUP), :] = joined_rows((low, high), p)

    halves, wholes = head_masks()
    masked = bias[0]
    for p in range(GROUPS):
        lanes = slice(p * GROUP, (p + 1) * GROUP)
        scores = nt(spread(pair(q, lanes)[MIDDLE], halves), pair(k, lanes))
        for h in range(4):
            rows = slice(h * QUERY, (h + 1) * QUERY)
            score = scores[rows] + masked
            exponent = jnp.exp(score - jnp.max(score, axis=1, keepdims=True))
            share = 1.0 / jnp.sum(exponent, axis=1, keepdims=True)
            probability[0, p, rows, :] = (exponent * share).astype(BF16)
        made = collect(nn(probability[0, p], pair(v, lanes)), wholes)
        attended[:, lanes] = made.astype(BF16)
    values = [jnp.concatenate([ref[o] for ref in xs], axis=0)[MIDDLE] for o in range(SLOTS)]
    total = jnp.concatenate(values, axis=1).astype(F32) + nn(attended[...], held[...])
    mixed[...] = total.astype(BF16)
    normed[...] = (norm(total)[0] * gain[...]).astype(BF16)


def out_weight():
    return [
        pl.BlockSpec(
            (GROUPS, SLOTS, GROUP, LANES), lambda i, a=a: (a, 0, 3, 0), pipeline_mode=pl.Buffered(1)
        )
        for a in range(2)
    ]


def attend(q, k, v, bias, xs, gain, heads):
    blocks, _, span = bias.shape
    tokens = blocks * QUERY
    return call(
        attend_kernel,
        (blocks,),
        pair_of((QUERY, WIDTH)) * 3
        + pair_of((SLOTS, QUERY, 256))
        + [pl.BlockSpec((1, QUERY, span), lambda i: (i, 0, 0)), resident((1, WIDTH))]
        + out_weight(),
        [
            rows_of(WIDTH, QUERY),
            pl.BlockSpec((1, GROUPS, 4 * QUERY, span), lambda i: (i, 0, 0, 0)),
            rows_of(WIDTH, QUERY),
            rows_of(WIDTH, QUERY),
        ],
        [
            struct((tokens, WIDTH), BF16),
            struct((blocks, GROUPS, 4 * QUERY, span), BF16),
            struct((tokens, WIDTH), BF16),
            struct((tokens, WIDTH), BF16),
        ],
        [pltpu.VMEM((WIDTH, WIDTH), BF16)],
        blocks * GROUPS * 2 * 2 * 4 * QUERY * span * GROUP + 2 * tokens * WIDTH * WIDTH,
        14 * tokens * WIDTH + blocks * GROUPS * 8 * QUERY * span,
        "attend",
    )(q, q, k, k, v, v, xs, xs, bias, gain, heads, heads)


def attend_back_kernel(*refs):
    q, k, v, table_c, table_s = (refs[2 * t : 2 * t + 2] for t in range(5))
    grad, weights = refs[10:12]
    gq, gk, gv, to_low, to_high, edges, sum_k, sum_v = refs[12:]
    step, last = pl.program_id(0), pl.num_programs(0) - 1

    @at_first
    def _():
        sum_k[...] = jnp.zeros_like(sum_k)
        sum_v[...] = jnp.zeros_like(sum_v)

    @pl.when(step < last)
    def _():
        halves, wholes = head_masks()
        c, s = pair(table_c)[MIDDLE], pair(table_s)[MIDDLE]
        for p in range(GROUPS):
            lanes = slice(p * GROUP, (p + 1) * GROUP)
            queries = spread(pair(q, lanes)[MIDDLE], halves)
            grads = spread(grad[:, lanes], wholes)
            d_weights = nt(grads, pair(v, lanes))
            parts = []
            for h in range(4):
                rows = slice(h * QUERY, (h + 1) * QUERY)
                wide, d_weight = weights[0, p, rows, :].astype(F32), d_weights[rows]
                mean = jnp.sum(wide * d_weight, axis=1, keepdims=True)
                parts.append((wide * (d_weight - mean)).astype(BF16))
            g_score = jnp.concatenate(parts, axis=0)
            made = collect(nn(g_score, pair(k, lanes)), halves) * HEAD**-0.5
            first, second = made[:, :LANES], made[:, LANES:]
            gq[:, p * GROUP : p * GROUP + LANES] = (first * c + second * s).astype(BF16)
            gq[:, p * GROUP + LANES : (p + 1) * GROUP] = (second * c - first * s).astype(BF16)
            for total, made in (
                (sum_k, tn(g_score, queries)),
                (sum_v, tn(weights[0, p], grads)),
            ):
                total[0:QUERY, lanes] = total[QUERY:, lanes] + made[0:QUERY]
                total[QUERY:, lanes] = made[QUERY:]

    @pl.when(step == last)
    def _():
        for total in (sum_k, sum_v):
            total[0:QUERY, :] = total[QUERY:, :]

    c, s = table_c[0][...], table_s[0][...]
    for p in range(GROUPS):
        one, two = slice(p * GROUP, p * GROUP + LANES), slice(p * GROUP + LANES, (p + 1) * GROUP)
        first, second = sum_k[0:QUERY, one], sum_k[0:QUERY, two]
        gk[:, one] = (first * c + second * s).astype(BF16)
        gk[:, two] = (second * c - first * s).astype(BF16)
    gv[...] = sum_v[0:QUERY, :].astype(BF16)

    @at_first
    def _():
        for t, total in ((0, sum_k), (1, sum_v)):
            lanes = slice(t * WIDTH, (t + 1) * WIDTH)
            to_low[:, lanes] = total[0:REACH, :].astype(BF16)
            edges[0, :, lanes] = total[REACH:QUERY, :]

    @pl.when(step == last)
    def _():
        for t, total in ((0, sum_k), (1, sum_v)):
            lanes = slice(t * WIDTH, (t + 1) * WIDTH)
            edges[1, :, lanes] = total[0:REACH, :]
            to_high[:, lanes] = total[REACH:QUERY, :].astype(BF16)


def attend_back(q, grad, weights, k, v, cosine, sine):
    tokens = grad.shape[0]
    blocks = tokens // QUERY
    span = QUERY + 2 * REACH
    edge = (REACH, 2 * WIDTH)

    def own(i):
        return jnp.minimum(i, blocks - 1)

    def pairs(width):
        return [
            pl.BlockSpec((QUERY, width), lambda i: (i, 0)),
            pl.BlockSpec((QUERY, width), lambda i: (own(i) + 1, 0)),
        ]

    return call(
        attend_back_kernel,
        (blocks + 1,),
        pairs(WIDTH) * 3
        + pairs(LANES) * 2
        + [
            pl.BlockSpec((QUERY, WIDTH), lambda i: (own(i), 0)),
            pl.BlockSpec((1, GROUPS, 4 * QUERY, span), lambda i: (own(i), 0, 0, 0)),
        ],
        [pl.BlockSpec((QUERY, WIDTH), lambda i: (own(i), 0))]
        + [rows_of(WIDTH, QUERY)] * 2
        + [resident(edge), resident(edge), resident((2,) + edge)],
        [struct((tokens, WIDTH), BF16)]
        + [struct(q.shape, BF16)] * 2
        + [struct(edge, BF16)] * 2
        + [struct((2,) + edge, F32)],
        [pltpu.VMEM((span, WIDTH), F32)] * 2,
        blocks * GROUPS * 2 * 4 * 4 * QUERY * span * GROUP,
        14 * tokens * WIDTH + blocks * GROUPS * 8 * QUERY * span,
        "attend_back",
    )(q, q, k, k, v, v, cosine, cosine, sine, sine, grad, weights)


def edge_kernel(*refs):
    edges, from_low, from_high, cosine, sine = refs[2:7]
    gk, gv = refs[7:]

    def finish(came):
        c, s = cosine[...], sine[...]
        for p in range(GROUPS):
            one = slice(p * GROUP, p * GROUP + LANES)
            two = slice(p * GROUP + LANES, (p + 1) * GROUP)
            first = edges[0, :, one] + came[:, one].astype(F32)
            second = edges[0, :, two] + came[:, two].astype(F32)
            gk[:, one] = (first * c + second * s).astype(BF16)
            gk[:, two] = (second * c - first * s).astype(BF16)
        gv[...] = (edges[0, :, WIDTH:] + came[:, WIDTH:].astype(F32)).astype(BF16)

    pl.when(pl.program_id(0) == 0)(lambda: finish(from_low))
    pl.when(pl.program_id(0) == 1)(lambda: finish(from_high))


def add_edges(gk, gv, edges, from_low, from_high, cosine, sine):
    far = gk.shape[0] // REACH - 3
    rows = pl.BlockSpec((REACH, WIDTH), lambda i: (1 + i * far, 0))
    table = pl.BlockSpec((REACH, LANES), lambda i: (1 + i * far, 0))
    came = resident(from_low.shape)
    return pl.pallas_call(
        edge_kernel,
        grid=(2,),
        in_specs=[pl.BlockSpec(memory_space=pl.ANY)] * 2
        + [pl.BlockSpec((1, REACH, 2 * WIDTH), lambda i: (i, 0, 0)), came, came, table, table],
        out_specs=[rows] * 2,
        out_shape=[struct(gk.shape, BF16)] * 2,
        input_output_aliases={0: 0, 1: 1},
        compiler_params=pltpu.CompilerParams(
            vmem_limit_bytes=VMEM, dimension_semantics=("arbitrary",)
        ),
        cost_estimate=pl.CostEstimate(flops=1, bytes_accessed=2**21, transcendentals=0),
        name="add_edges",
    )(gk, gv, edges, from_low, from_high, cosine, sine)


def step_rows():
    return pl.ds(pl.multiple_of((pl.program_id(0) - GROUPS) * TILE, TILE), TILE)


def between_rows():
    at = (pl.program_id(0) - GROUPS) * TILE + REACH
    return pl.ds(pl.multiple_of(at, REACH), TILE)


def feed_kernel(*refs):
    normed, mixed, weight = refs[0], refs[1], refs[2:4]
    hidden, slope, gelu, early, late, total = refs[4:]
    ff = hidden.shape[2]
    half = GROUPS + total.shape[0] // TILE - 1
    step = pl.program_id(0)

    @pl.when(step < GROUPS)
    def _():
        act = nt(normed[...], joined_rows(weight, 0, slice(0, ff)))
        gate = nt(normed[...], joined_rows(weight, 0, slice(ff, 2 * ff)))
        spread_to = 0.5 * (1.0 + lax.erf(act * math.sqrt(0.5)))
        curve = act * spread_to
        density = jnp.exp(act * act * -0.5) * (1.0 / math.sqrt(2.0 * math.pi))
        slope[0] = (gate * (spread_to + act * density)).astype(BF16)
        gelu[0] = curve.astype(BF16)
        hidden[0] = (curve * gate).astype(BF16)
        add_up(total, hidden, weight, slice(2 * ff, 3 * ff))

    @pl.when((step >= GROUPS) & (step < half))
    def _():
        put_rows(early, mixed[...].astype(F32) + total[step_rows(), :])

    @pl.when(step >= half)
    def _():
        put_rows(late, mixed[...].astype(F32) + total[step_rows(), :])


def units_of(tokens, ff):
    return pl.BlockSpec((1, tokens, ff), lambda i: (group_of(i), 0, 0))


def feed(normed, mixed, weight):
    tokens, ff = normed.shape[0], weight.shape[2] // 3
    last = tokens // TILE - 1
    return call(
        feed_kernel,
        (GROUPS + tokens // TILE,),
        [resident((tokens, WIDTH)), later_rows(WIDTH)] + weight_rows(3 * ff),
        [units_of(tokens, ff)] * 3
        + [
            pl.BlockSpec(
                (SLOTS, TILE, 256), lambda i: (0, jnp.clip(i - GROUPS, 0, last - 1), 0)
            ),
            resident((SLOTS, TILE, 256)),
        ],
        [struct((GROUPS, tokens, ff), BF16)] * 3
        + [struct((SLOTS, tokens - TILE, 256), BF16), struct((SLOTS, TILE, 256), BF16)],
        [pltpu.VMEM((tokens, WIDTH), F32)],
        2 * tokens * WIDTH * 3 * GROUPS * ff,
        6 * tokens * WIDTH + 6 * GROUPS * ff * (tokens + WIDTH),
        "feed",
    )(normed, mixed, weight, weight)


def feed_back_kernel(*refs):
    cots, slope, gelu, mixed, gain = refs[:5]
    weight, outward = refs[5:7], refs[7:9]
    g_act, g_gate, g_branch, g_attended, gain_part, cot, total = refs[9:]
    ff = g_act.shape[2]

    @at_first
    def _():
        cot[...] = whole_rows(cots)

    @pl.when(pl.program_id(0) < GROUPS)
    def _():
        g_hidden = nt(cot[...], joined_rows(weight, 0, slice(2 * ff, 3 * ff)))
        g_act[0] = (g_hidden * slope[0].astype(F32)).astype(BF16)
        g_gate[0] = (g_hidden * gelu[0].astype(F32)).astype(BF16)
        add_up(total, g_act, weight, slice(0, ff))
        total[...] += nn(g_gate[0], joined_rows(weight, 0, slice(ff, 2 * ff)))

    @pl.when(pl.program_id(0) >= GROUPS)
    def _():
        gradient = total[step_rows(), :]
        unit, inverse = norm(mixed[...].astype(F32))
        add_gain(gain_part, gradient * unit)
        made = cot[step_rows(), :].astype(F32) + norm_back(gradient, unit, inverse, gain[...])
        branch = made.astype(BF16)
        g_branch[...] = branch
        for p in range(GROUPS):
            lanes = slice(p * GROUP, (p + 1) * GROUP)
            g_attended[:, lanes] = nt(branch, joined_rows(outward, p)).astype(BF16)


def feed_back(cots, slope, gelu, mixed, gain, weight, heads):
    _, tokens, ff = slope.shape
    return call(
        feed_back_kernel,
        (GROUPS + tokens // TILE,),
        [resident(cots.shape)]
        + [units_of(tokens, ff)] * 2
        + [later_rows(WIDTH), resident((1, WIDTH))]
        + weight_rows(3 * ff)
        + out_weight(),
        [units_of(tokens, ff)] * 2 + [later_rows(WIDTH)] * 2 + [resident((8, WIDTH))],
        [struct((GROUPS, tokens, ff), BF16)] * 2
        + [struct((tokens, WIDTH), BF16)] * 2
        + [struct((8, WIDTH), F32)],
        [pltpu.VMEM((tokens, WIDTH), BF16), pltpu.VMEM((tokens, WIDTH), F32)],
        2 * tokens * WIDTH * (3 * GROUPS * ff + WIDTH),
        8 * tokens * WIDTH + 6 * GROUPS * ff * (tokens + WIDTH),
        "feed_back",
    )(cots, slope, gelu, mixed, gain, weight, weight, heads, heads)


def unproject_kernel(*refs):
    xs, gq, gk, gv, g_branch, gain, low, high, early, late, gain_part, held, total = refs
    @pl.when(pl.program_id(0) < GROUPS)
    def _():
        own = pl.ds(REACH, gq.shape[0])
        held[0] = jnp.concatenate([gq[...], gk[own, :], gv[own, :]], axis=1)
        add_up(total, held, (low, high))

    @pl.when(pl.program_id(0) >= GROUPS)
    def _():
        gradient = total[step_rows(), :]
        unit, inverse = norm(whole_rows(xs, between_rows()).astype(F32))
        add_gain(gain_part, gradient * unit)
        made = g_branch[...].astype(F32) + norm_back(gradient, unit, inverse, gain[...])
        pl.when(pl.program_id(0) == GROUPS)(lambda: put_rows(early, made))
        pl.when(pl.program_id(0) > GROUPS)(lambda: put_rows(late, made))


def unproject(xs, gq, gk, gv, g_branch, gain, weight):
    tokens = gq.shape[0]
    return call(
        unproject_kernel,
        (GROUPS + tokens // TILE,),
        [resident(xs.shape)]
        + [
            pl.BlockSpec((value.shape[0], GROUP), lambda i: (0, group_of(i)))
            for value in (gq, gk, gv)
        ]
        + [later_rows(WIDTH), resident((1, WIDTH))]
        + weight_rows(3 * GROUP),
        [
            resident((SLOTS, TILE, 256)),
            pl.BlockSpec((SLOTS, TILE, 256), lambda i: (0, jnp.maximum(i - GROUPS - 1, 0), 0)),
            resident((8, WIDTH)),
        ],
        [
            struct((SLOTS, TILE, 256), BF16),
            struct((SLOTS, tokens - TILE, 256), BF16),
            struct((8, WIDTH), F32),
        ],
        [pltpu.VMEM((1, tokens, 3 * GROUP), BF16), pltpu.VMEM((tokens, WIDTH), F32)],
        2 * tokens * WIDTH * 3 * WIDTH,
        12 * tokens * WIDTH + 6 * WIDTH * WIDTH,
        "unproject",
    )(xs, gq, gk, gv, g_branch, gain, weight, weight)


def outer_kernel(count, tokens, *refs):
    inner, outer, out = refs[:count], refs[count : 2 * count], refs[-1]

    def own_rows(value):
        return value[pl.ds((value.shape[0] - tokens) // 2, tokens), :]

    def make(left, right):
        left = left[0] if len(left.shape) == 3 else own_rows(left)
        right = whole_rows(right) if len(right.shape) == 3 else own_rows(right)
        made = tn(left, right)
        for a in range(2):
            for o in range(SLOTS):
                at = o * 256 + a * LANES
                out[a, 0, o] = made[:, at : at + LANES].astype(BF16)

    for t in range(count):
        pl.when(pl.program_id(0) % count == t)(functools.partial(make, inner[t], outer[t]))


def outer_product(tokens, inner, outer, places, kinds, base=None):
    count = len(inner)
    width = inner[0].shape[2] if inner[0].ndim == 3 else GROUP
    stride = places[-1] - places[0]

    def inner_block(value):
        if value.ndim == 3:
            return pl.BlockSpec((1, tokens, width), lambda i: (i // count, 0, 0))
        return pl.BlockSpec((value.shape[0], GROUP), lambda i: (0, i // count))

    more = [] if base is None else [base]
    moved = 8 * count * width * (tokens + WIDTH) + 2 * tokens * WIDTH
    return pl.pallas_call(
        functools.partial(outer_kernel, count, tokens),
        grid=(GROUPS * count,),
        in_specs=[inner_block(value) for value in inner]
        + [resident(value.shape) for value in outer]
        + [pl.BlockSpec(memory_space=pl.ANY) for _ in more],
        out_specs=pl.BlockSpec(
            (2, 1, SLOTS, width, LANES),
            lambda i: (0, i // count, 0, places[0] + i % count * stride, 0),
        ),
        out_shape=struct((2, GROUPS, SLOTS, kinds * width, LANES), BF16),
        input_output_aliases={2 * count: 0} if more else {},
        compiler_params=pltpu.CompilerParams(
            vmem_limit_bytes=VMEM, dimension_semantics=("arbitrary",)
        ),
        cost_estimate=pl.CostEstimate(
            flops=2 * tokens * GROUPS * count * width * WIDTH,
            bytes_accessed=moved,
            transcendentals=0,
        ),
        name="outer_product",
    )(*inner, *outer, *more)


def over_dp(value):
    return lax.ppermute(value, "dp", [(0, 1), (1, 0)])


def over_chip(value):
    return lax.ppermute(value, "col", [(i, i ^ 2) for i in range(4)])


def over_core(value):
    return lax.ppermute(value, "col", [(i, i ^ 1) for i in range(4)])


def exchange(value):
    return lax.all_to_all(value, "row", 0, 0)


def after(value, *earlier):
    return lax.optimization_barrier((value,) + earlier)[0]


def own_half(shard):
    return lax.dynamic_slice_in_dim(shard, lax.axis_index("dp") * LANES, LANES, 1)


def gather_rows(half):
    return exchange(jnp.broadcast_to(half, (SLOTS,) + half.shape))


def gather_groups(own):
    return lax.all_gather(own, ("dp", "col"), axis=0, tiled=False)


def reduce_groups(parts):
    parts = parts.reshape((2 * GROUPS,) + parts.shape[2:])
    return lax.psum_scatter(parts, ("dp", "col"), scatter_dimension=0, tiled=False)


def sum_rows(parts):
    half = jnp.sum(parts.astype(F32), axis=0).astype(BF16)
    other = over_dp(half)
    first = lax.axis_index("dp") == 0
    return jnp.where(first, half, other), jnp.where(first, other, half)


def finish_kernel(kinds, width, low, high, *outs):
    for t, (kind, out) in enumerate(zip(kinds, outs, strict=True)):
        rows = slice(t * width, (t + 1) * width)
        value = jnp.concatenate([low[rows, :], high[rows, :]], axis=1).astype(F32)
        if kind not in "qkv":
            out[...] = value
            continue
        if kind in "qk":
            cuts = [value[at * 32 : (at + 1) * 32] for at in (0, 4, 1, 5, 2, 6, 3, 7)]
            value = jnp.concatenate(cuts, axis=0)
        out[...] = value.T


def finish(halves, kinds, width):
    return pl.pallas_call(
        functools.partial(finish_kernel, kinds, width),
        out_shape=[struct((256, width) if kind in "qkv" else (width, 256), F32) for kind in kinds],
        compiler_params=pltpu.CompilerParams(vmem_limit_bytes=VMEM),
        cost_estimate=pl.CostEstimate(flops=1, bytes_accessed=2**21, transcendentals=0),
        name="finish",
    )(*halves)


def sum_gains(parts):
    both = parts + over_dp(parts)
    both = both + over_chip(both)
    both = both + over_core(both)
    for bit in (1, 2):
        both = both + lax.ppermute(both, "row", [(i, i ^ bit) for i in range(SLOTS)])
    return lax.dynamic_slice_in_dim(both, lax.axis_index("row") * 256, 256, 1)


def groups_of(whole):
    rows = whole.shape[0] // GROUPS
    cut = whole.reshape(GROUPS, rows, SLOTS, 2, LANES).transpose(3, 0, 2, 1, 4)
    return cut.reshape(2 * GROUPS, SLOTS, rows, LANES)


def whole_of(parts, types):
    cut = parts.transpose(1, 3, 2, 0, 4).reshape(GROUPS, types, -1, WIDTH)
    return [cut[:, t].reshape(-1, WIDTH) for t in range(types)]


def split_heads(rows):
    return rows.reshape(-1, 4, 2, 32, rows.shape[1]).swapaxes(1, 2).reshape(rows.shape)


def join_heads(rows):
    return rows.reshape(-1, 2, 4, 32, rows.shape[1]).swapaxes(1, 2).reshape(rows.shape)


def positions_and_masks(segments, valid, first, tokens):
    length = segments.shape[0]
    index = first - REACH + jnp.arange(tokens + 2 * REACH, dtype=jnp.int32)
    pads = (REACH, REACH)
    near = lax.dynamic_slice_in_dim(jnp.pad(segments, pads), first, tokens + 2 * REACH, 0)
    ids = jnp.arange(64, dtype=jnp.int32)
    before = jnp.sum((segments[None, :] < ids[:, None]).astype(jnp.int32), axis=1)
    begin = jnp.sum(jnp.where(near[:, None] == ids[None, :], before[None, :], 0), axis=1)
    where_in = (index - begin).astype(F32)
    frequency = ROPE_THETA ** (-((jnp.arange(LANES) % 32).astype(F32) * 2.0) / HEAD)
    angles = where_in[:, None] * frequency[None, :]
    code = jnp.pad(jnp.where(valid == 1, segments, -1), pads, constant_values=-1)
    code = lax.dynamic_slice_in_dim(code, first, tokens + 2 * REACH, 0)
    span = QUERY + 2 * REACH
    keys = jnp.stack([code[i : i + span] for i in range(0, tokens, QUERY)])[:, None, :]
    queries = near[REACH:-REACH].reshape(-1, QUERY, 1)
    shape = (tokens // QUERY, QUERY, span)
    offset = (
        lax.broadcasted_iota(jnp.int32, shape, 2)
        - lax.broadcasted_iota(jnp.int32, shape, 1)
        - REACH
    )
    allowed = (jnp.abs(offset) <= REACH) & ((queries == keys) | (offset == 0))
    return jnp.cos(angles), jnp.sin(angles), jnp.where(allowed, 0.0, MASKED_SCORE).astype(F32)


def body(
    dp,
    rows,
    cols,
    tokens_in,
    w_query,
    w_key,
    w_value,
    w_out,
    w_act,
    w_gate,
    w_down,
    gain_attn,
    gain_ffn,
    cotangent,
    segment_ids,
    valid_mask,
):
    tokens = tokens_in.shape[0] // rows
    length = segment_ids.shape[1]
    own_slice = (dp, rows, cols) == (2, 4, 4) and rows * tokens == length
    gains = jnp.stack([gain_attn, gain_ffn])
    at = (lax.axis_index("col") * rows + lax.axis_index("row")) * tokens
    sequence, first = at // length, at % length
    count = rows * cols
    joins = [i for i in range(count - 1) if ((i + 1) * tokens) % length]
    upward, downward = [(i, i + 1) for i in joins], [(i + 1, i) for i in joins]

    def shift(value, perm):
        place_of = [(i % rows) * cols + i // rows for i in range(count)]
        return lax.ppermute(value, ("row", "col"), [(place_of[i], place_of[j]) for i, j in perm])

    if own_slice:
        marks = jnp.concatenate([segment_ids, valid_mask]).astype(BF16).reshape(-1, LANES)
        heads_half = jnp.concatenate(
            [
                split_heads(own_half(w_query.T)),
                split_heads(own_half(w_key.T)),
                own_half(w_value.T),
                own_half(w_out),
                marks,
                gains.reshape(4, LANES),
                jnp.zeros((12, LANES), BF16),
            ],
            axis=0,
        )
        feed_half = jnp.concatenate(
            [own_half(w_act.T), own_half(w_gate.T), own_half(w_down)], axis=0
        )
        padded = jnp.pad(tokens_in, ((REACH, REACH), (0, 0)))
        spans = [padded[j * tokens : (j + 1) * tokens + 2 * REACH] for j in range(rows)]
        heads_own = gather_rows(heads_half)
        heads_w = gather_groups(heads_own[:, :WIDTH])
        feed_own = gather_rows(after(feed_half, heads_own))
        feed_w = gather_groups(feed_own)
        last = WIDTH + marks.shape[0]
        marks = heads_own[:, WIDTH:last].reshape(rows, 2, length)
        marks = lax.dynamic_index_in_dim(marks, sequence, 0, False).astype(jnp.int32)
        gain_slots = heads_own[:, last : last + 4].reshape(SLOTS, 2, 256)
        tables = positions_and_masks(*marks, first, tokens)
        xs = exchange(after(jnp.stack(spans), feed_own))
        cots = exchange(after(cotangent.reshape(rows, tokens, 256), xs))
    else:
        xs = exchange(tokens_in.reshape(rows, tokens, 256))
        below, above = shift(xs[:, -REACH:], upward), shift(xs[:, :REACH], downward)
        xs = jnp.concatenate([below, xs, above], axis=1)
        cots = exchange(cotangent.reshape(rows, tokens, 256))
        gain_slots = exchange(jnp.broadcast_to(gains, (rows, 2, 256)))
        marks = lax.all_gather(jnp.stack([segment_ids, valid_mask]), "row", axis=1, tiled=True)
        marks = lax.dynamic_index_in_dim(marks, sequence, 1, False)
        tables = positions_and_masks(*marks, first, tokens)

        def full(value, inner_first):
            first, second = ("col", "row") if inner_first else ("row", "col")
            value = lax.all_gather(value, first, axis=0, tiled=True)
            value = lax.all_gather(value, second, axis=1, tiled=True)
            return value if inner_first else value.T

        def joined(*parts):
            return jnp.concatenate([groups_of(part) for part in parts], axis=2)

        heads_w = joined(
            split_heads(full(w_query, False)),
            split_heads(full(w_key, False)),
            full(w_value, False),
            full(w_out, True),
        )
        feed_w = joined(full(w_act, False), full(w_gate, False), full(w_down, True))
    gain_rows = gain_slots.swapaxes(0, 1).reshape(2, 1, WIDTH).astype(F32)
    cosine, sine, bias = tables

    q, k, v, normed_attn = project(xs, gain_rows[0], cosine, sine, heads_w)
    attended, weights, mixed, normed_ffn = attend(q, k, v, bias, xs, gain_rows[1], heads_w)
    hidden, slope, gelu, early, late = feed(normed_ffn, mixed, feed_w)
    early = exchange(after(early, cots))
    down_parts = outer_product(tokens, [hidden], [cots], (0,), 1)
    g_act, g_gate, g_branch, g_attended, gain_part_ffn = feed_back(
        cots, after(slope, down_parts), gelu, mixed, gain_rows[1], feed_w, heads_w
    )
    up_parts = outer_product(tokens, [after(g_act, early), g_gate], [normed_ffn] * 2, (0, 1), 2)
    if own_slice:
        down_own, up_own = reduce_groups(down_parts), reduce_groups(up_parts)
        g_attended = after(g_attended, up_parts, down_own)
    gq, gk, gv, to_low, to_high, edges = attend_back(
        q, g_attended, weights, k, v, cosine, sine
    )
    from_low, from_high = shift(to_high, upward), shift(to_low, downward)
    if own_slice:
        rest = down_own.reshape(rows, -1, 256)
        late, rest = jnp.split(
            exchange(jnp.concatenate([after(late, early), rest], axis=1)), [TILE], axis=1
        )
        down_sum = rest.reshape(down_own.shape)
    else:
        late = exchange(late)
    layer_out = jnp.concatenate([early, late], axis=1)
    gk, gv = add_edges(gk, gv, edges, from_low, from_high, cosine, sine)
    first_tokens, other_tokens, gain_part_attn = unproject(
        xs, gq, gk, gv, g_branch, gain_rows[0], heads_w
    )
    attended = after(attended, first_tokens, *([late, down_sum] if own_slice else []))
    heads_parts = outer_product(tokens, [gq, attended], [normed_attn, g_branch], (0, 3), 4)
    first_tokens = exchange(after(first_tokens, late))
    gk = after(gk, heads_parts, first_tokens)
    heads_parts = outer_product(tokens, [gk, gv], [normed_attn] * 2, (1, 2), 4, heads_parts)
    other_tokens = exchange(after(other_tokens, first_tokens))
    token_gradient = jnp.concatenate([first_tokens, other_tokens], axis=1)

    gain_parts = jnp.stack([jnp.sum(gain_part_attn, axis=0), jnp.sum(gain_part_ffn, axis=0)])
    if own_slice:
        up_sum = exchange(after(up_own, other_tokens))
        gain_grads = sum_gains(gain_parts)
        heads_sum = exchange(after(reduce_groups(heads_parts), up_sum, gain_grads))
        ff = w_act.shape[1]
        grads = (
            *finish(sum_rows(heads_sum), "qkvo", GROUP),
            *(value.T for value in finish(sum_rows(up_sum), "ag", ff)),
            *finish(sum_rows(down_sum), "d", ff),
        )
    else:

        def share(value, inner_first):
            first, second = ("col", "row") if inner_first else ("row", "col")
            value = value if inner_first else value.T
            value = lax.psum_scatter(value, first, scatter_dimension=0, tiled=True)
            value = lax.psum_scatter(value, second, scatter_dimension=1, tiled=True)
            return lax.psum(value, "dp").astype(F32)

        (down_whole,) = whole_of(down_parts, 1)
        act_whole, gate_whole = whole_of(up_parts, 2)
        query_whole, key_whole, value_whole, out_whole = whole_of(heads_parts, 4)
        grads = (
            share(join_heads(query_whole), False),
            share(join_heads(key_whole), False),
            share(value_whole, False),
            share(out_whole, True),
            share(act_whole, False),
            share(gate_whole, False),
            share(down_whole, True),
        )
        totals = lax.psum(gain_parts, ("dp", "row", "col")).reshape(2, SLOTS, 256)
        gain_grads = lax.dynamic_index_in_dim(totals, lax.axis_index("row"), 1, False)
    layer_out = layer_out.reshape(-1, 256)
    token_gradient = token_gradient.reshape(-1, 256).astype(F32)
    return (layer_out, token_gradient) + grads + (gain_grads[0], gain_grads[1])


def solution(mesh):
    sizes = tuple(mesh.shape[axis] for axis in ("dp", "row", "col"))
    in_specs = (
        P(("dp", "col"), "row"),
        P("row", "col"),
        P("row", "col"),
        P("row", "col"),
        P("col", "row"),
        P("row", "col"),
        P("row", "col"),
        P("col", "row"),
        P("row"),
        P("row"),
        P(("dp", "col"), "row"),
        P(("dp", "row"), None),
        P(("dp", "row"), None),
    )
    out_specs = (
        P(("dp", "col"), "row"),
        P(("dp", "col"), "row"),
        P("row", "col"),
        P("row", "col"),
        P("row", "col"),
        P("col", "row"),
        P("row", "col"),
        P("row", "col"),
        P("col", "row"),
        P("row"),
        P("row"),
    )
    return jax.shard_map(
        functools.partial(body, *sizes),
        mesh=mesh,
        in_specs=in_specs,
        out_specs=out_specs,
        check_vma=False,
    )
```

```python
import functools
import math

import jax
import jax.numpy as jnp
from jax import lax
from jax.experimental import pallas as pl
from jax.experimental.pallas import tpu as pltpu
from jax.sharding import PartitionSpec as P

WIDTH = 1024
HEAD = 64
REACH = 64
EPSILON = 1e-05
ROPE_THETA = 10000.0
MASKED_SCORE = -1e30
LANES = 128
SLOTS = 4
GROUPS = 4
GROUP = 256
TILE = 256
QUERY = 128
VMEM = 60 * 1024 * 1024
F32 = jnp.float32
BF16 = jnp.bfloat16


def nt(left, right):
    return lax.dot_general(left, right, (((1,), (1,)), ((), ())), preferred_element_type=F32)


def nn(left, right):
    return lax.dot_general(left, right, (((1,), (0,)), ((), ())), preferred_element_type=F32)


def tn(left, right):
    return lax.dot_general(left, right, (((0,), (0,)), ((), ())), preferred_element_type=F32)


def call(kernel, grid, in_specs, out_specs, out_shape, scratch, flops, moved, name):
    return pl.pallas_call(
        kernel,
        grid=grid,
        in_specs=in_specs,
        out_specs=out_specs,
        out_shape=out_shape,
        scratch_shapes=scratch,
        compiler_params=pltpu.CompilerParams(
            vmem_limit_bytes=VMEM, dimension_semantics=("arbitrary",)
        ),
        cost_estimate=pl.CostEstimate(flops=flops, bytes_accessed=moved, transcendentals=0),
        name=name,
    )


def resident(shape):
    zeros = (0,) * len(shape)
    return pl.BlockSpec(shape, lambda i: zeros, pipeline_mode=pl.Buffered(1))


def rows_of(width, tile=TILE):
    return pl.BlockSpec((tile, width), lambda i: (i, 0))


BLOCKS = pl.BlockSpec((SLOTS, TILE, 256), lambda i: (0, i, 0))


def later_rows(width):
    return pl.BlockSpec((TILE, width), lambda i: (jnp.maximum(i - GROUPS, 0), 0))


LATER_BLOCKS = pl.BlockSpec((SLOTS, TILE, 256), lambda i: (0, jnp.maximum(i - GROUPS, 0), 0))


def group_of(i):
    return jnp.minimum(i, GROUPS - 1)


def weight_rows(rows, at=0):
    return [
        pl.BlockSpec(
            (1, SLOTS, rows, LANES), lambda i, a=a: (a * GROUPS + group_of(i), 0, at, 0)
        )
        for a in range(2)
    ]


def joined_rows(halves, p=0, rows=slice(None)):
    return jnp.concatenate([w[p, o, rows, :] for o in range(SLOTS) for w in halves], axis=1)


def at_first(run):
    pl.when(pl.program_id(0) == 0)(run)


def add_up(total, inner, weight, rows=slice(None)):
    @at_first
    def _():
        total[...] = nn(inner[0], joined_rows(weight, 0, rows))

    @pl.when(pl.program_id(0) > 0)
    def _():
        total[...] += nn(inner[0], joined_rows(weight, 0, rows))


def struct(shape, dtype):
    return jax.ShapeDtypeStruct(shape, dtype)


def whole_rows(slots, rows=slice(None)):
    return jnp.concatenate([slots[o, rows, :] for o in range(SLOTS)], axis=1)


def put_rows(slots, total):
    for o in range(SLOTS):
        slots[o] = total[:, o * 256 : (o + 1) * 256].astype(slots.dtype)


def norm(values):
    average = jnp.mean(values, axis=1, keepdims=True)
    centered = values - average
    variance = jnp.mean(centered * centered, axis=1, keepdims=True)
    inverse = lax.rsqrt(variance + EPSILON)
    return centered * inverse, inverse


def norm_back(gradient, unit, inverse, gain):
    scaled = gradient * gain
    average = jnp.mean(scaled, axis=1, keepdims=True)
    crossed = jnp.mean(scaled * unit, axis=1, keepdims=True)
    return inverse * (scaled - average - unit * crossed)


def add_gain(gain_part, products):
    @pl.when(pl.program_id(0) == GROUPS)
    def _():
        gain_part[...] = jnp.zeros_like(gain_part)

    gain_part[...] += jnp.sum(products.reshape(-1, 8, WIDTH), axis=0)


def project_kernel(xs, gain, cosine, sine, low, high, q, k, v, normed, rows):
    @at_first
    def _():
        for at in range(0, rows.shape[0], QUERY):
            cut = slice(at, at + QUERY)
            values = jnp.concatenate([xs[o, cut, :] for o in range(SLOTS)], axis=1)
            made = (norm(values.astype(F32))[0] * gain[...]).astype(BF16)
            rows[cut, :] = made
            normed[cut, :] = made

    made = nt(rows[...], joined_rows((low, high)))
    c, s = cosine[...], sine[...]
    for t, out, scale in ((0, q, HEAD**-0.5), (1, k, 1.0)):
        first = made[:, t * GROUP : t * GROUP + LANES] * scale
        second = made[:, t * GROUP + LANES : (t + 1) * GROUP] * scale
        out[:, :LANES] = (first * c - second * s).astype(BF16)
        out[:, LANES:] = (second * c + first * s).astype(BF16)
    v[...] = made[:, 2 * GROUP :].astype(BF16)


def project(xs, gain, cosine, sine, weight):
    tokens = cosine.shape[0]
    return call(
        project_kernel,
        (GROUPS,),
        [resident(xs.shape), resident((1, WIDTH))]
        + [resident((tokens, LANES))] * 2
        + weight_rows(3 * GROUP),
        [pl.BlockSpec((tokens, GROUP), lambda i: (0, i))] * 3 + [resident((tokens, WIDTH))],
        [struct((tokens, WIDTH), BF16)] * 4,
        [pltpu.VMEM((tokens, WIDTH), BF16)],
        2 * tokens * WIDTH * 3 * WIDTH,
        10 * tokens * WIDTH + 6 * WIDTH * WIDTH,
        "project",
    )(xs, gain, cosine, sine, weight, weight)


def head_masks():
    lane = lax.broadcasted_iota(jnp.int32, (1, GROUP), 1)
    halves = [((lane % LANES) // 32 == h) for h in range(4)]
    wholes = [(lane // HEAD == h) for h in range(4)]
    return halves, wholes


def spread(rows, masks):
    return jnp.concatenate([rows * m.astype(BF16) for m in masks], axis=0)


def collect(stacked, masks):
    total = jnp.where(masks[0], stacked[0:QUERY], 0.0)
    for h in range(1, 4):
        total = jnp.where(masks[h], stacked[h * QUERY : (h + 1) * QUERY], total)
    return total


def pair(refs, lanes=slice(None)):
    return jnp.concatenate([ref[:, lanes] for ref in refs], axis=0)


def pair_of(shape):
    lead = len(shape) - 2
    return [
        pl.BlockSpec(
            shape[:lead] + (QUERY, shape[-1]),
            lambda i, more=more: (0,) * lead + (i + more, 0),
        )
        for more in range(2)
    ]


MIDDLE = slice(REACH, REACH + QUERY)


def attend_kernel(*refs):
    q, k, v, xs = (refs[2 * t : 2 * t + 2] for t in range(4))
    bias, gain, low, high = refs[8:12]
    attended, probability, mixed, normed, held = refs[12:]

    @at_first
    def _():
        for p in range(GROUPS):
            held[pl.ds(p * GROUP, GROUP), :] = joined_rows((low, high), p)

    halves, wholes = head_masks()
    masked = bias[0]
    for p in range(GROUPS):
        lanes = slice(p * GROUP, (p + 1) * GROUP)
        scores = nt(spread(pair(q, lanes)[MIDDLE], halves), pair(k, lanes))
        for h in range(4):
            rows = slice(h * QUERY, (h + 1) * QUERY)
            score = scores[rows] + masked
            exponent = jnp.exp(score - jnp.max(score, axis=1, keepdims=True))
            share = 1.0 / jnp.sum(exponent, axis=1, keepdims=True)
            probability[0, p, rows, :] = (exponent * share).astype(BF16)
        made = collect(nn(probability[0, p], pair(v, lanes)), wholes)
        attended[:, lanes] = made.astype(BF16)
    values = [jnp.concatenate([ref[o] for ref in xs], axis=0)[MIDDLE] for o in range(SLOTS)]
    total = jnp.concatenate(values, axis=1).astype(F32) + nn(attended[...], held[...])
    mixed[...] = total.astype(BF16)
    normed[...] = (norm(total)[0] * gain[...]).astype(BF16)


def out_weight():
    return [
        pl.BlockSpec(
            (GROUPS, SLOTS, GROUP, LANES), lambda i, a=a: (a, 0, 3, 0), pipeline_mode=pl.Buffered(1)
        )
        for a in range(2)
    ]


def attend(q, k, v, bias, xs, gain, heads):
    blocks, _, span = bias.shape
    tokens = blocks * QUERY
    return call(
        attend_kernel,
        (blocks,),
        pair_of((QUERY, WIDTH)) * 3
        + pair_of((SLOTS, QUERY, 256))
        + [pl.BlockSpec((1, QUERY, span), lambda i: (i, 0, 0)), resident((1, WIDTH))]
        + out_weight(),
        [
            rows_of(WIDTH, QUERY),
            pl.BlockSpec((1, GROUPS, 4 * QUERY, span), lambda i: (i, 0, 0, 0)),
            rows_of(WIDTH, QUERY),
            rows_of(WIDTH, QUERY),
        ],
        [
            struct((tokens, WIDTH), BF16),
            struct((blocks, GROUPS, 4 * QUERY, span), BF16),
            struct((tokens, WIDTH), BF16),
            struct((tokens, WIDTH), BF16),
        ],
        [pltpu.VMEM((WIDTH, WIDTH), BF16)],
        blocks * GROUPS * 2 * 2 * 4 * QUERY * span * GROUP + 2 * tokens * WIDTH * WIDTH,
        14 * tokens * WIDTH + blocks * GROUPS * 8 * QUERY * span,
        "attend",
    )(q, q, k, k, v, v, xs, xs, bias, gain, heads, heads)


def attend_back_kernel(*refs):
    q, k, v, table_c, table_s = (refs[2 * t : 2 * t + 2] for t in range(5))
    grad, weights = refs[10:12]
    gq, gk, gv, to_low, to_high, edges, sum_k, sum_v = refs[12:]
    step, last = pl.program_id(0), pl.num_programs(0) - 1

    @at_first
    def _():
        sum_k[...] = jnp.zeros_like(sum_k)
        sum_v[...] = jnp.zeros_like(sum_v)

    @pl.when(step < last)
    def _():
        halves, wholes = head_masks()
        c, s = pair(table_c)[MIDDLE], pair(table_s)[MIDDLE]
        for p in range(GROUPS):
            lanes = slice(p * GROUP, (p + 1) * GROUP)
            queries = spread(pair(q, lanes)[MIDDLE], halves)
            grads = spread(grad[:, lanes], wholes)
            d_weights = nt(grads, pair(v, lanes))
            parts = []
            for h in range(4):
                rows = slice(h * QUERY, (h + 1) * QUERY)
                wide, d_weight = weights[0, p, rows, :].astype(F32), d_weights[rows]
                mean = jnp.sum(wide * d_weight, axis=1, keepdims=True)
                parts.append((wide * (d_weight - mean)).astype(BF16))
            g_score = jnp.concatenate(parts, axis=0)
            made = collect(nn(g_score, pair(k, lanes)), halves) * HEAD**-0.5
            first, second = made[:, :LANES], made[:, LANES:]
            gq[:, p * GROUP : p * GROUP + LANES] = (first * c + second * s).astype(BF16)
            gq[:, p * GROUP + LANES : (p + 1) * GROUP] = (second * c - first * s).astype(BF16)
            for total, made in (
                (sum_k, tn(g_score, queries)),
                (sum_v, tn(weights[0, p], grads)),
            ):
                total[0:QUERY, lanes] = total[QUERY:, lanes] + made[0:QUERY]
                total[QUERY:, lanes] = made[QUERY:]

    @pl.when(step == last)
    def _():
        for total in (sum_k, sum_v):
            total[0:QUERY, :] = total[QUERY:, :]

    c, s = table_c[0][...], table_s[0][...]
    for p in range(GROUPS):
        one, two = slice(p * GROUP, p * GROUP + LANES), slice(p * GROUP + LANES, (p + 1) * GROUP)
        first, second = sum_k[0:QUERY, one], sum_k[0:QUERY, two]
        gk[:, one] = (first * c + second * s).astype(BF16)
        gk[:, two] = (second * c - first * s).astype(BF16)
    gv[...] = sum_v[0:QUERY, :].astype(BF16)

    @at_first
    def _():
        for t, total in ((0, sum_k), (1, sum_v)):
            lanes = slice(t * WIDTH, (t + 1) * WIDTH)
            to_low[:, lanes] = total[0:REACH, :].astype(BF16)
            edges[0, :, lanes] = total[REACH:QUERY, :]

    @pl.when(step == last)
    def _():
        for t, total in ((0, sum_k), (1, sum_v)):
            lanes = slice(t * WIDTH, (t + 1) * WIDTH)
            edges[1, :, lanes] = total[0:REACH, :]
            to_high[:, lanes] = total[REACH:QUERY, :].astype(BF16)


def attend_back(q, grad, weights, k, v, cosine, sine):
    tokens = grad.shape[0]
    blocks = tokens // QUERY
    span = QUERY + 2 * REACH
    edge = (REACH, 2 * WIDTH)

    def own(i):
        return jnp.minimum(i, blocks - 1)

    def pairs(width):
        return [
            pl.BlockSpec((QUERY, width), lambda i: (i, 0)),
            pl.BlockSpec((QUERY, width), lambda i: (own(i) + 1, 0)),
        ]

    return call(
        attend_back_kernel,
        (blocks + 1,),
        pairs(WIDTH) * 3
        + pairs(LANES) * 2
        + [
            pl.BlockSpec((QUERY, WIDTH), lambda i: (own(i), 0)),
            pl.BlockSpec((1, GROUPS, 4 * QUERY, span), lambda i: (own(i), 0, 0, 0)),
        ],
        [pl.BlockSpec((QUERY, WIDTH), lambda i: (own(i), 0))]
        + [rows_of(WIDTH, QUERY)] * 2
        + [resident(edge), resident(edge), resident((2,) + edge)],
        [struct((tokens, WIDTH), BF16)]
        + [struct(q.shape, BF16)] * 2
        + [struct(edge, BF16)] * 2
        + [struct((2,) + edge, F32)],
        [pltpu.VMEM((span, WIDTH), F32)] * 2,
        blocks * GROUPS * 2 * 4 * 4 * QUERY * span * GROUP,
        14 * tokens * WIDTH + blocks * GROUPS * 8 * QUERY * span,
        "attend_back",
    )(q, q, k, k, v, v, cosine, cosine, sine, sine, grad, weights)


def edge_kernel(*refs):
    edges, from_low, from_high, cosine, sine = refs[2:7]
    gk, gv = refs[7:]

    def finish(came):
        c, s = cosine[...], sine[...]
        for p in range(GROUPS):
            one = slice(p * GROUP, p * GROUP + LANES)
            two = slice(p * GROUP + LANES, (p + 1) * GROUP)
            first = edges[0, :, one] + came[:, one].astype(F32)
            second = edges[0, :, two] + came[:, two].astype(F32)
            gk[:, one] = (first * c + second * s).astype(BF16)
            gk[:, two] = (second * c - first * s).astype(BF16)
        gv[...] = (edges[0, :, WIDTH:] + came[:, WIDTH:].astype(F32)).astype(BF16)

    pl.when(pl.program_id(0) == 0)(lambda: finish(from_low))
    pl.when(pl.program_id(0) == 1)(lambda: finish(from_high))


def add_edges(gk, gv, edges, from_low, from_high, cosine, sine):
    far = gk.shape[0] // REACH - 3
    rows = pl.BlockSpec((REACH, WIDTH), lambda i: (1 + i * far, 0))
    table = pl.BlockSpec((REACH, LANES), lambda i: (1 + i * far, 0))
    came = resident(from_low.shape)
    return pl.pallas_call(
        edge_kernel,
        grid=(2,),
        in_specs=[pl.BlockSpec(memory_space=pl.ANY)] * 2
        + [pl.BlockSpec((1, REACH, 2 * WIDTH), lambda i: (i, 0, 0)), came, came, table, table],
        out_specs=[rows] * 2,
        out_shape=[struct(gk.shape, BF16)] * 2,
        input_output_aliases={0: 0, 1: 1},
        compiler_params=pltpu.CompilerParams(
            vmem_limit_bytes=VMEM, dimension_semantics=("arbitrary",)
        ),
        cost_estimate=pl.CostEstimate(flops=1, bytes_accessed=2**21, transcendentals=0),
        name="add_edges",
    )(gk, gv, edges, from_low, from_high, cosine, sine)


def step_rows():
    return pl.ds(pl.multiple_of((pl.program_id(0) - GROUPS) * TILE, TILE), TILE)


def between_rows():
    at = (pl.program_id(0) - GROUPS) * TILE + REACH
    return pl.ds(pl.multiple_of(at, REACH), TILE)


def feed_kernel(*refs):
    normed, mixed, weight = refs[0], refs[1], refs[2:4]
    hidden, slope, gelu, early, late, total = refs[4:]
    ff = hidden.shape[2]
    half = GROUPS + total.shape[0] // TILE - 1
    step = pl.program_id(0)

    @pl.when(step < GROUPS)
    def _():
        act = nt(normed[...], joined_rows(weight, 0, slice(0, ff)))
        gate = nt(normed[...], joined_rows(weight, 0, slice(ff, 2 * ff)))
        spread_to = 0.5 * (1.0 + lax.erf(act * math.sqrt(0.5)))
        curve = act * spread_to
        density = jnp.exp(act * act * -0.5) * (1.0 / math.sqrt(2.0 * math.pi))
        slope[0] = (gate * (spread_to + act * density)).astype(BF16)
        gelu[0] = curve.astype(BF16)
        hidden[0] = (curve * gate).astype(BF16)
        add_up(total, hidden, weight, slice(2 * ff, 3 * ff))

    @pl.when((step >= GROUPS) & (step < half))
    def _():
        put_rows(early, mixed[...].astype(F32) + total[step_rows(), :])

    @pl.when(step >= half)
    def _():
        put_rows(late, mixed[...].astype(F32) + total[step_rows(), :])


def units_of(tokens, ff):
    return pl.BlockSpec((1, tokens, ff), lambda i: (group_of(i), 0, 0))


def feed(normed, mixed, weight):
    tokens, ff = normed.shape[0], weight.shape[2] // 3
    last = tokens // TILE - 1
    return call(
        feed_kernel,
        (GROUPS + tokens // TILE,),
        [resident((tokens, WIDTH)), later_rows(WIDTH)] + weight_rows(3 * ff),
        [units_of(tokens, ff)] * 3
        + [
            pl.BlockSpec(
                (SLOTS, TILE, 256), lambda i: (0, jnp.clip(i - GROUPS, 0, last - 1), 0)
            ),
            resident((SLOTS, TILE, 256)),
        ],
        [struct((GROUPS, tokens, ff), BF16)] * 3
        + [struct((SLOTS, tokens - TILE, 256), BF16), struct((SLOTS, TILE, 256), BF16)],
        [pltpu.VMEM((tokens, WIDTH), F32)],
        2 * tokens * WIDTH * 3 * GROUPS * ff,
        6 * tokens * WIDTH + 6 * GROUPS * ff * (tokens + WIDTH),
        "feed",
    )(normed, mixed, weight, weight)


def feed_back_kernel(*refs):
    cots, slope, gelu, mixed, gain = refs[:5]
    weight, outward = refs[5:7], refs[7:9]
    g_act, g_gate, g_branch, g_attended, gain_part, cot, total = refs[9:]
    ff = g_act.shape[2]

    @at_first
    def _():
        cot[...] = whole_rows(cots)

    @pl.when(pl.program_id(0) < GROUPS)
    def _():
        g_hidden = nt(cot[...], joined_rows(weight, 0, slice(2 * ff, 3 * ff)))
        g_act[0] = (g_hidden * slope[0].astype(F32)).astype(BF16)
        g_gate[0] = (g_hidden * gelu[0].astype(F32)).astype(BF16)
        add_up(total, g_act, weight, slice(0, ff))
        total[...] += nn(g_gate[0], joined_rows(weight, 0, slice(ff, 2 * ff)))

    @pl.when(pl.program_id(0) >= GROUPS)
    def _():
        gradient = total[step_rows(), :]
        unit, inverse = norm(mixed[...].astype(F32))
        add_gain(gain_part, gradient * unit)
        made = cot[step_rows(), :].astype(F32) + norm_back(gradient, unit, inverse, gain[...])
        branch = made.astype(BF16)
        g_branch[...] = branch
        for p in range(GROUPS):
            lanes = slice(p * GROUP, (p + 1) * GROUP)
            g_attended[:, lanes] = nt(branch, joined_rows(outward, p)).astype(BF16)


def feed_back(cots, slope, gelu, mixed, gain, weight, heads):
    _, tokens, ff = slope.shape
    return call(
        feed_back_kernel,
        (GROUPS + tokens // TILE,),
        [resident(cots.shape)]
        + [units_of(tokens, ff)] * 2
        + [later_rows(WIDTH), resident((1, WIDTH))]
        + weight_rows(3 * ff)
        + out_weight(),
        [units_of(tokens, ff)] * 2 + [later_rows(WIDTH)] * 2 + [resident((8, WIDTH))],
        [struct((GROUPS, tokens, ff), BF16)] * 2
        + [struct((tokens, WIDTH), BF16)] * 2
        + [struct((8, WIDTH), F32)],
        [pltpu.VMEM((tokens, WIDTH), BF16), pltpu.VMEM((tokens, WIDTH), F32)],
        2 * tokens * WIDTH * (3 * GROUPS * ff + WIDTH),
        8 * tokens * WIDTH + 6 * GROUPS * ff * (tokens + WIDTH),
        "feed_back",
    )(cots, slope, gelu, mixed, gain, weight, weight, heads, heads)


def unproject_kernel(*refs):
    xs, gq, gk, gv, g_branch, gain, low, high, outs, gain_part, held, total = refs
    @pl.when(pl.program_id(0) < GROUPS)
    def _():
        own = pl.ds(REACH, gq.shape[0])
        held[0] = jnp.concatenate([gq[...], gk[own, :], gv[own, :]], axis=1)
        add_up(total, held, (low, high))

    @pl.when(pl.program_id(0) >= GROUPS)
    def _():
        gradient = total[step_rows(), :]
        unit, inverse = norm(whole_rows(xs, between_rows()).astype(F32))
        add_gain(gain_part, gradient * unit)
        made = g_branch[...].astype(F32) + norm_back(gradient, unit, inverse, gain[...])
        put_rows(outs, made)


def unproject(xs, gq, gk, gv, g_branch, gain, weight):
    tokens = gq.shape[0]
    return call(
        unproject_kernel,
        (GROUPS + tokens // TILE,),
        [resident(xs.shape)]
        + [
            pl.BlockSpec((value.shape[0], GROUP), lambda i: (0, group_of(i)))
            for value in (gq, gk, gv)
        ]
        + [later_rows(WIDTH), resident((1, WIDTH))]
        + weight_rows(3 * GROUP),
        [LATER_BLOCKS, resident((8, WIDTH))],
        [struct((SLOTS, tokens, 256), BF16), struct((8, WIDTH), F32)],
        [pltpu.VMEM((1, tokens, 3 * GROUP), BF16), pltpu.VMEM((tokens, WIDTH), F32)],
        2 * tokens * WIDTH * 3 * WIDTH,
        12 * tokens * WIDTH + 6 * WIDTH * WIDTH,
        "unproject",
    )(xs, gq, gk, gv, g_branch, gain, weight, weight)


def outer_kernel(count, tokens, *refs):
    inner, outer, out = refs[:count], refs[count : 2 * count], refs[-1]

    def own_rows(value):
        return value[pl.ds((value.shape[0] - tokens) // 2, tokens), :]

    def make(left, right):
        left = left[0] if len(left.shape) == 3 else own_rows(left)
        right = whole_rows(right) if len(right.shape) == 3 else own_rows(right)
        made = tn(left, right)
        many, width = out.shape[1], out.shape[3]
        for j in range(many):
            rows = slice(j * width, (j + 1) * width)
            for a in range(2):
                for o in range(SLOTS):
                    at = o * 256 + a * LANES
                    out[a, j, o] = made[rows, at : at + LANES].astype(BF16)

    for t in range(count):
        pl.when(pl.program_id(0) % count == t)(functools.partial(make, inner[t], outer[t]))


def outer_product(tokens, inner, outer, places, kinds, base=None):
    count = len(inner)
    width = inner[0].shape[2] if inner[0].ndim == 3 else GROUP
    stride = places[-1] - places[0]
    many = 1 if inner[0].ndim == 3 else 2

    def inner_block(value):
        if value.ndim == 3:
            return pl.BlockSpec((1, tokens, width), lambda i: (i // count, 0, 0))
        return pl.BlockSpec((value.shape[0], many * GROUP), lambda i: (0, i // count))

    more = [] if base is None else [base]
    moved = 8 * count * width * (tokens + WIDTH) + 2 * tokens * WIDTH
    return pl.pallas_call(
        functools.partial(outer_kernel, count, tokens),
        grid=(GROUPS // many * count,),
        in_specs=[inner_block(value) for value in inner]
        + [resident(value.shape) for value in outer]
        + [pl.BlockSpec(memory_space=pl.ANY) for _ in more],
        out_specs=pl.BlockSpec(
            (2, many, SLOTS, width, LANES),
            lambda i: (0, i // count, 0, places[0] + i % count * stride, 0),
        ),
        out_shape=struct((2, GROUPS, SLOTS, kinds * width, LANES), BF16),
        input_output_aliases={2 * count: 0} if more else {},
        compiler_params=pltpu.CompilerParams(
            vmem_limit_bytes=VMEM, dimension_semantics=("arbitrary",)
        ),
        cost_estimate=pl.CostEstimate(
            flops=2 * tokens * GROUPS * count * width * WIDTH,
            bytes_accessed=moved,
            transcendentals=0,
        ),
        name="outer_product",
    )(*inner, *outer, *more)


def over_dp(value):
    return lax.ppermute(value, "dp", [(0, 1), (1, 0)])


def over_chip(value):
    return lax.ppermute(value, "col", [(i, i ^ 2) for i in range(4)])


def over_core(value):
    return lax.ppermute(value, "col", [(i, i ^ 1) for i in range(4)])


def exchange(value):
    return lax.all_to_all(value, "row", 0, 0)


def after(value, *earlier):
    return lax.optimization_barrier((value,) + earlier)[0]


def own_half(shard):
    return lax.dynamic_slice_in_dim(shard, lax.axis_index("dp") * LANES, LANES, 1)


def gather_rows(half):
    return exchange(jnp.broadcast_to(half, (SLOTS,) + half.shape))


def gather_groups(own):
    return lax.all_gather(own, ("dp", "col"), axis=0, tiled=False)


def reduce_groups(parts):
    parts = parts.reshape((2 * GROUPS,) + parts.shape[2:])
    return lax.psum_scatter(parts, ("dp", "col"), scatter_dimension=0, tiled=False)


def sum_rows(parts):
    half = jnp.sum(parts.astype(F32), axis=0).astype(BF16)
    other = over_dp(half)
    first = lax.axis_index("dp") == 0
    return jnp.where(first, half, other), jnp.where(first, other, half)


def finish_kernel(kinds, width, low, high, *outs):
    for t, (kind, out) in enumerate(zip(kinds, outs, strict=True)):
        rows = slice(t * width, (t + 1) * width)
        value = jnp.concatenate([low[rows, :], high[rows, :]], axis=1).astype(F32)
        if kind not in "qkv":
            out[...] = value
            continue
        if kind in "qk":
            cuts = [value[at * 32 : (at + 1) * 32] for at in (0, 4, 1, 5, 2, 6, 3, 7)]
            value = jnp.concatenate(cuts, axis=0)
        out[...] = value.T


def finish(halves, kinds, width):
    return pl.pallas_call(
        functools.partial(finish_kernel, kinds, width),
        out_shape=[struct((256, width) if kind in "qkv" else (width, 256), F32) for kind in kinds],
        compiler_params=pltpu.CompilerParams(vmem_limit_bytes=VMEM),
        cost_estimate=pl.CostEstimate(flops=1, bytes_accessed=2**21, transcendentals=0),
        name="finish",
    )(*halves)


def sum_gains(parts):
    both = parts + over_dp(parts)
    both = both + over_chip(both)
    both = both + over_core(both)
    for bit in (1, 2):
        both = both + lax.ppermute(both, "row", [(i, i ^ bit) for i in range(SLOTS)])
    return lax.dynamic_slice_in_dim(both, lax.axis_index("row") * 256, 256, 1)


def groups_of(whole):
    rows = whole.shape[0] // GROUPS
    cut = whole.reshape(GROUPS, rows, SLOTS, 2, LANES).transpose(3, 0, 2, 1, 4)
    return cut.reshape(2 * GROUPS, SLOTS, rows, LANES)


def whole_of(parts, types):
    cut = parts.transpose(1, 3, 2, 0, 4).reshape(GROUPS, types, -1, WIDTH)
    return [cut[:, t].reshape(-1, WIDTH) for t in range(types)]


def split_heads(rows):
    return rows.reshape(-1, 4, 2, 32, rows.shape[1]).swapaxes(1, 2).reshape(rows.shape)


def join_heads(rows):
    return rows.reshape(-1, 2, 4, 32, rows.shape[1]).swapaxes(1, 2).reshape(rows.shape)


def positions_and_masks(segments, valid, first, tokens):
    length = segments.shape[0]
    index = first - REACH + jnp.arange(tokens + 2 * REACH, dtype=jnp.int32)
    pads = (REACH, REACH)
    near = lax.dynamic_slice_in_dim(jnp.pad(segments, pads), first, tokens + 2 * REACH, 0)
    ids = jnp.arange(64, dtype=jnp.int32)
    before = jnp.sum((segments[None, :] < ids[:, None]).astype(jnp.int32), axis=1)
    begin = jnp.sum(jnp.where(near[:, None] == ids[None, :], before[None, :], 0), axis=1)
    where_in = (index - begin).astype(F32)
    frequency = ROPE_THETA ** (-((jnp.arange(LANES) % 32).astype(F32) * 2.0) / HEAD)
    angles = where_in[:, None] * frequency[None, :]
    code = jnp.pad(jnp.where(valid == 1, segments, -1), pads, constant_values=-1)
    code = lax.dynamic_slice_in_dim(code, first, tokens + 2 * REACH, 0)
    span = QUERY + 2 * REACH
    keys = jnp.stack([code[i : i + span] for i in range(0, tokens, QUERY)])[:, None, :]
    queries = near[REACH:-REACH].reshape(-1, QUERY, 1)
    shape = (tokens // QUERY, QUERY, span)
    offset = (
        lax.broadcasted_iota(jnp.int32, shape, 2)
        - lax.broadcasted_iota(jnp.int32, shape, 1)
        - REACH
    )
    allowed = (jnp.abs(offset) <= REACH) & ((queries == keys) | (offset == 0))
    return jnp.cos(angles), jnp.sin(angles), jnp.where(allowed, 0.0, MASKED_SCORE).astype(F32)


def body(
    dp,
    rows,
    cols,
    tokens_in,
    w_query,
    w_key,
    w_value,
    w_out,
    w_act,
    w_gate,
    w_down,
    gain_attn,
    gain_ffn,
    cotangent,
    segment_ids,
    valid_mask,
):
    tokens = tokens_in.shape[0] // rows
    length = segment_ids.shape[1]
    own_slice = (dp, rows, cols) == (2, 4, 4) and rows * tokens == length
    gains = jnp.stack([gain_attn, gain_ffn])
    at = (lax.axis_index("col") * rows + lax.axis_index("row")) * tokens
    sequence, first = at // length, at % length
    count = rows * cols
    joins = [i for i in range(count - 1) if ((i + 1) * tokens) % length]
    upward, downward = [(i, i + 1) for i in joins], [(i + 1, i) for i in joins]

    def shift(value, perm):
        place_of = [(i % rows) * cols + i // rows for i in range(count)]
        return lax.ppermute(value, ("row", "col"), [(place_of[i], place_of[j]) for i, j in perm])

    if own_slice:
        marks = jnp.concatenate([segment_ids, valid_mask]).astype(BF16).reshape(-1, LANES)
        heads_half = jnp.concatenate(
            [
                split_heads(own_half(w_query.T)),
                split_heads(own_half(w_key.T)),
                own_half(w_value.T),
                own_half(w_out),
                marks,
                gains.reshape(4, LANES),
                jnp.zeros((12, LANES), BF16),
            ],
            axis=0,
        )
        feed_half = jnp.concatenate(
            [own_half(w_act.T), own_half(w_gate.T), own_half(w_down)], axis=0
        )
        padded = jnp.pad(tokens_in, ((REACH, REACH), (0, 0)))
        spans = [padded[j * tokens : (j + 1) * tokens + 2 * REACH] for j in range(rows)]
        heads_own = gather_rows(heads_half)
        heads_w = gather_groups(heads_own[:, :WIDTH])
        feed_own = gather_rows(after(feed_half, heads_own))
        feed_w = gather_groups(feed_own)
        last = WIDTH + marks.shape[0]
        marks = heads_own[:, WIDTH:last].reshape(rows, 2, length)
        marks = lax.dynamic_index_in_dim(marks, sequence, 0, False).astype(jnp.int32)
        gain_slots = heads_own[:, last : last + 4].reshape(SLOTS, 2, 256)
        tables = positions_and_masks(*marks, first, tokens)
        xs = exchange(after(jnp.stack(spans), feed_own))
        cots = exchange(after(cotangent.reshape(rows, tokens, 256), xs))
    else:
        xs = exchange(tokens_in.reshape(rows, tokens, 256))
        below, above = shift(xs[:, -REACH:], upward), shift(xs[:, :REACH], downward)
        xs = jnp.concatenate([below, xs, above], axis=1)
        cots = exchange(cotangent.reshape(rows, tokens, 256))
        gain_slots = exchange(jnp.broadcast_to(gains, (rows, 2, 256)))
        marks = lax.all_gather(jnp.stack([segment_ids, valid_mask]), "row", axis=1, tiled=True)
        marks = lax.dynamic_index_in_dim(marks, sequence, 1, False)
        tables = positions_and_masks(*marks, first, tokens)

        def full(value, inner_first):
            first, second = ("col", "row") if inner_first else ("row", "col")
            value = lax.all_gather(value, first, axis=0, tiled=True)
            value = lax.all_gather(value, second, axis=1, tiled=True)
            return value if inner_first else value.T

        def joined(*parts):
            return jnp.concatenate([groups_of(part) for part in parts], axis=2)

        heads_w = joined(
            split_heads(full(w_query, False)),
            split_heads(full(w_key, False)),
            full(w_value, False),
            full(w_out, True),
        )
        feed_w = joined(full(w_act, False), full(w_gate, False), full(w_down, True))
    gain_rows = gain_slots.swapaxes(0, 1).reshape(2, 1, WIDTH).astype(F32)
    cosine, sine, bias = tables

    q, k, v, normed_attn = project(xs, gain_rows[0], cosine, sine, heads_w)
    attended, weights, mixed, normed_ffn = attend(q, k, v, bias, xs, gain_rows[1], heads_w)
    hidden, slope, gelu, early, late = feed(normed_ffn, mixed, feed_w)
    early = exchange(after(early, cots))
    down_parts = outer_product(tokens, [hidden], [cots], (0,), 1)
    g_act, g_gate, g_branch, g_attended, gain_part_ffn = feed_back(
        cots, after(slope, down_parts), gelu, mixed, gain_rows[1], feed_w, heads_w
    )
    up_parts = outer_product(tokens, [after(g_act, early), g_gate], [normed_ffn] * 2, (0, 1), 2)
    if own_slice:
        down_own, up_own = reduce_groups(down_parts), reduce_groups(up_parts)
        g_attended = after(g_attended, up_parts, down_own)
    gq, gk, gv, to_low, to_high, edges = attend_back(
        q, g_attended, weights, k, v, cosine, sine
    )
    from_low, from_high = shift(to_high, upward), shift(to_low, downward)
    if own_slice:
        rest = down_own.reshape(rows, -1, 256)
        late, rest = jnp.split(
            exchange(jnp.concatenate([after(late, early), rest], axis=1)), [TILE], axis=1
        )
        down_sum = rest.reshape(down_own.shape)
    else:
        late = exchange(late)
    layer_out = jnp.concatenate([early, late], axis=1)
    heads_parts = outer_product(tokens, [gq, attended], [normed_attn, g_branch], (0, 3), 4)
    from_low = after(from_low, heads_parts)
    if own_slice:
        from_low = after(from_low, late, down_sum)
    gk, gv = add_edges(gk, gv, edges, from_low, from_high, cosine, sine)
    grad_slots, gain_part_attn = unproject(
        xs, gq, gk, gv, g_branch, gain_rows[0], heads_w
    )
    heads_parts = outer_product(
        tokens, [after(gk, grad_slots), gv], [normed_attn] * 2, (1, 2), 4, heads_parts
    )
    token_gradient = exchange(after(grad_slots, late))

    gain_parts = jnp.stack([jnp.sum(gain_part_attn, axis=0), jnp.sum(gain_part_ffn, axis=0)])
    if own_slice:
        up_sum = exchange(after(up_own, token_gradient))
        gain_grads = sum_gains(gain_parts)
        heads_sum = exchange(after(reduce_groups(heads_parts), up_sum, gain_grads))
        ff = w_act.shape[1]
        grads = (
            *finish(sum_rows(heads_sum), "qkvo", GROUP),
            *(value.T for value in finish(sum_rows(up_sum), "ag", ff)),
            *finish(sum_rows(down_sum), "d", ff),
        )
    else:

        def share(value, inner_first):
            first, second = ("col", "row") if inner_first else ("row", "col")
            value = value if inner_first else value.T
            value = lax.psum_scatter(value, first, scatter_dimension=0, tiled=True)
            value = lax.psum_scatter(value, second, scatter_dimension=1, tiled=True)
            return lax.psum(value, "dp").astype(F32)

        (down_whole,) = whole_of(down_parts, 1)
        act_whole, gate_whole = whole_of(up_parts, 2)
        query_whole, key_whole, value_whole, out_whole = whole_of(heads_parts, 4)
        grads = (
            share(join_heads(query_whole), False),
            share(join_heads(key_whole), False),
            share(value_whole, False),
            share(out_whole, True),
            share(act_whole, False),
            share(gate_whole, False),
            share(down_whole, True),
        )
        totals = lax.psum(gain_parts, ("dp", "row", "col")).reshape(2, SLOTS, 256)
        gain_grads = lax.dynamic_index_in_dim(totals, lax.axis_index("row"), 1, False)
    layer_out = layer_out.reshape(-1, 256)
    token_gradient = token_gradient.reshape(-1, 256).astype(F32)
    return (layer_out, token_gradient) + grads + (gain_grads[0], gain_grads[1])


def solution(mesh):
    sizes = tuple(mesh.shape[axis] for axis in ("dp", "row", "col"))
    in_specs = (
        P(("dp", "col"), "row"),
        P("row", "col"),
        P("row", "col"),
        P("row", "col"),
        P("col", "row"),
        P("row", "col"),
        P("row", "col"),
        P("col", "row"),
        P("row"),
        P("row"),
        P(("dp", "col"), "row"),
        P(("dp", "row"), None),
        P(("dp", "row"), None),
    )
    out_specs = (
        P(("dp", "col"), "row"),
        P(("dp", "col"), "row"),
        P("row", "col"),
        P("row", "col"),
        P("row", "col"),
        P("col", "row"),
        P("row", "col"),
        P("row", "col"),
        P("col", "row"),
        P("row"),
        P("row"),
    )
    return jax.shard_map(
        functools.partial(body, *sizes),
        mesh=mesh,
        in_specs=in_specs,
        out_specs=out_specs,
        check_vma=False,
    )
```

```python
import functools
import math

import jax
import jax.numpy as jnp
from jax import lax
from jax.experimental import pallas as pl
from jax.experimental.pallas import tpu as pltpu
from jax.sharding import PartitionSpec as P

WIDTH = 1024
HEAD = 64
REACH = 64
EPSILON = 1e-05
ROPE_THETA = 10000.0
MASKED_SCORE = -1e30
LANES = 128
SLOTS = 4
GROUPS = 4
GROUP = 256
TILE = 256
QUERY = 128
VMEM = 60 * 1024 * 1024
F32 = jnp.float32
BF16 = jnp.bfloat16


def nt(left, right):
    return lax.dot_general(left, right, (((1,), (1,)), ((), ())), preferred_element_type=F32)


def nn(left, right):
    return lax.dot_general(left, right, (((1,), (0,)), ((), ())), preferred_element_type=F32)


def tn(left, right):
    return lax.dot_general(left, right, (((0,), (0,)), ((), ())), preferred_element_type=F32)


def call(kernel, grid, in_specs, out_specs, out_shape, scratch, flops, moved, name):
    return pl.pallas_call(
        kernel,
        grid=grid,
        in_specs=in_specs,
        out_specs=out_specs,
        out_shape=out_shape,
        scratch_shapes=scratch,
        compiler_params=pltpu.CompilerParams(
            vmem_limit_bytes=VMEM, dimension_semantics=("arbitrary",)
        ),
        cost_estimate=pl.CostEstimate(flops=flops, bytes_accessed=moved, transcendentals=0),
        name=name,
    )


def resident(shape):
    zeros = (0,) * len(shape)
    return pl.BlockSpec(shape, lambda i: zeros, pipeline_mode=pl.Buffered(1))


def rows_of(width, tile=TILE):
    return pl.BlockSpec((tile, width), lambda i: (i, 0))


BLOCKS = pl.BlockSpec((SLOTS, TILE, 256), lambda i: (0, i, 0))


def later_rows(width):
    return pl.BlockSpec((TILE, width), lambda i: (jnp.maximum(i - GROUPS, 0), 0))


LATER_BLOCKS = pl.BlockSpec((SLOTS, TILE, 256), lambda i: (0, jnp.maximum(i - GROUPS, 0), 0))


def group_of(i):
    return jnp.minimum(i, GROUPS - 1)


def weight_rows(rows, at=0):
    return [
        pl.BlockSpec(
            (1, SLOTS, rows, LANES), lambda i, a=a: (a * GROUPS + group_of(i), 0, at, 0)
        )
        for a in range(2)
    ]


def joined_rows(halves, p=0, rows=slice(None)):
    return jnp.concatenate([w[p, o, rows, :] for o in range(SLOTS) for w in halves], axis=1)


def at_first(run):
    pl.when(pl.program_id(0) == 0)(run)


def add_up(total, inner, weight, rows=slice(None)):
    @at_first
    def _():
        total[...] = nn(inner[0], joined_rows(weight, 0, rows))

    @pl.when(pl.program_id(0) > 0)
    def _():
        total[...] += nn(inner[0], joined_rows(weight, 0, rows))


def struct(shape, dtype):
    return jax.ShapeDtypeStruct(shape, dtype)


def whole_rows(slots, rows=slice(None)):
    return jnp.concatenate([slots[o, rows, :] for o in range(SLOTS)], axis=1)


def put_rows(slots, total):
    for o in range(SLOTS):
        slots[o] = total[:, o * 256 : (o + 1) * 256].astype(slots.dtype)


def norm(values):
    average = jnp.mean(values, axis=1, keepdims=True)
    centered = values - average
    variance = jnp.mean(centered * centered, axis=1, keepdims=True)
    inverse = lax.rsqrt(variance + EPSILON)
    return centered * inverse, inverse


def norm_back(gradient, unit, inverse, gain):
    scaled = gradient * gain
    average = jnp.mean(scaled, axis=1, keepdims=True)
    crossed = jnp.mean(scaled * unit, axis=1, keepdims=True)
    return inverse * (scaled - average - unit * crossed)


def add_gain(gain_part, products):
    @pl.when(pl.program_id(0) == GROUPS)
    def _():
        gain_part[...] = jnp.zeros_like(gain_part)

    gain_part[...] += jnp.sum(products.reshape(-1, 8, WIDTH), axis=0)


def project_kernel(xs, gain, cosine, sine, low, high, q, k, v, normed, rows):
    @at_first
    def _():
        for at in range(0, rows.shape[0], QUERY):
            cut = slice(at, at + QUERY)
            values = jnp.concatenate([xs[o, cut, :] for o in range(SLOTS)], axis=1)
            made = (norm(values.astype(F32))[0] * gain[...]).astype(BF16)
            rows[cut, :] = made
            normed[cut, :] = made

    made = nt(rows[...], joined_rows((low, high)))
    c, s = cosine[...], sine[...]
    for t, out, scale in ((0, q, HEAD**-0.5), (1, k, 1.0)):
        first = made[:, t * GROUP : t * GROUP + LANES] * scale
        second = made[:, t * GROUP + LANES : (t + 1) * GROUP] * scale
        out[:, :LANES] = (first * c - second * s).astype(BF16)
        out[:, LANES:] = (second * c + first * s).astype(BF16)
    v[...] = made[:, 2 * GROUP :].astype(BF16)


def project(xs, gain, cosine, sine, weight):
    tokens = cosine.shape[0]
    return call(
        project_kernel,
        (GROUPS,),
        [resident(xs.shape), resident((1, WIDTH))]
        + [resident((tokens, LANES))] * 2
        + weight_rows(3 * GROUP),
        [pl.BlockSpec((tokens, GROUP), lambda i: (0, i))] * 3 + [resident((tokens, WIDTH))],
        [struct((tokens, WIDTH), BF16)] * 4,
        [pltpu.VMEM((tokens, WIDTH), BF16)],
        2 * tokens * WIDTH * 3 * WIDTH,
        10 * tokens * WIDTH + 6 * WIDTH * WIDTH,
        "project",
    )(xs, gain, cosine, sine, weight, weight)


def head_masks():
    lane = lax.broadcasted_iota(jnp.int32, (1, GROUP), 1)
    halves = [((lane % LANES) // 32 == h) for h in range(4)]
    wholes = [(lane // HEAD == h) for h in range(4)]
    return halves, wholes


def spread(rows, masks):
    return jnp.concatenate([rows * m.astype(BF16) for m in masks], axis=0)


def collect(stacked, masks):
    total = jnp.where(masks[0], stacked[0:QUERY], 0.0)
    for h in range(1, 4):
        total = jnp.where(masks[h], stacked[h * QUERY : (h + 1) * QUERY], total)
    return total


def pair(refs, lanes=slice(None)):
    return jnp.concatenate([ref[:, lanes] for ref in refs], axis=0)


def pair_of(shape):
    lead = len(shape) - 2
    return [
        pl.BlockSpec(
            shape[:lead] + (QUERY, shape[-1]),
            lambda i, more=more: (0,) * lead + (i + more, 0),
        )
        for more in range(2)
    ]


MIDDLE = slice(REACH, REACH + QUERY)


def attend_kernel(*refs):
    q, k, v, xs = (refs[2 * t : 2 * t + 2] for t in range(4))
    bias, gain, low, high = refs[8:12]
    attended, probability, mixed, normed, held = refs[12:]

    @at_first
    def _():
        for p in range(GROUPS):
            held[pl.ds(p * GROUP, GROUP), :] = joined_rows((low, high), p)

    halves, wholes = head_masks()
    masked = bias[0]
    for p in range(GROUPS):
        lanes = slice(p * GROUP, (p + 1) * GROUP)
        scores = nt(spread(pair(q, lanes)[MIDDLE], halves), pair(k, lanes))
        for h in range(4):
            rows = slice(h * QUERY, (h + 1) * QUERY)
            score = scores[rows] + masked
            exponent = jnp.exp(score - jnp.max(score, axis=1, keepdims=True))
            share = 1.0 / jnp.sum(exponent, axis=1, keepdims=True)
            probability[0, p, rows, :] = (exponent * share).astype(BF16)
        made = collect(nn(probability[0, p], pair(v, lanes)), wholes)
        attended[:, lanes] = made.astype(BF16)
    values = [jnp.concatenate([ref[o] for ref in xs], axis=0)[MIDDLE] for o in range(SLOTS)]
    total = jnp.concatenate(values, axis=1).astype(F32) + nn(attended[...], held[...])
    mixed[...] = total.astype(BF16)
    normed[...] = (norm(total)[0] * gain[...]).astype(BF16)


def out_weight():
    return [
        pl.BlockSpec(
            (GROUPS, SLOTS, GROUP, LANES), lambda i, a=a: (a, 0, 3, 0), pipeline_mode=pl.Buffered(1)
        )
        for a in range(2)
    ]


def attend(q, k, v, bias, xs, gain, heads):
    blocks, _, span = bias.shape
    tokens = blocks * QUERY
    return call(
        attend_kernel,
        (blocks,),
        pair_of((QUERY, WIDTH)) * 3
        + pair_of((SLOTS, QUERY, 256))
        + [pl.BlockSpec((1, QUERY, span), lambda i: (i, 0, 0)), resident((1, WIDTH))]
        + out_weight(),
        [
            rows_of(WIDTH, QUERY),
            pl.BlockSpec((1, GROUPS, 4 * QUERY, span), lambda i: (i, 0, 0, 0)),
            rows_of(WIDTH, QUERY),
            rows_of(WIDTH, QUERY),
        ],
        [
            struct((tokens, WIDTH), BF16),
            struct((blocks, GROUPS, 4 * QUERY, span), BF16),
            struct((tokens, WIDTH), BF16),
            struct((tokens, WIDTH), BF16),
        ],
        [pltpu.VMEM((WIDTH, WIDTH), BF16)],
        blocks * GROUPS * 2 * 2 * 4 * QUERY * span * GROUP + 2 * tokens * WIDTH * WIDTH,
        14 * tokens * WIDTH + blocks * GROUPS * 8 * QUERY * span,
        "attend",
    )(q, q, k, k, v, v, xs, xs, bias, gain, heads, heads)


def attend_back_kernel(*refs):
    q, k, v, table_c, table_s = (refs[2 * t : 2 * t + 2] for t in range(5))
    grad, weights = refs[10:12]
    gq, gk, gv, to_low, to_high, edges, sum_k, sum_v = refs[12:]
    step, last = pl.program_id(0), pl.num_programs(0) - 1

    @at_first
    def _():
        sum_k[...] = jnp.zeros_like(sum_k)
        sum_v[...] = jnp.zeros_like(sum_v)

    @pl.when(step < last)
    def _():
        halves, wholes = head_masks()
        c, s = pair(table_c)[MIDDLE], pair(table_s)[MIDDLE]
        for p in range(GROUPS):
            lanes = slice(p * GROUP, (p + 1) * GROUP)
            queries = spread(pair(q, lanes)[MIDDLE], halves)
            grads = spread(grad[:, lanes], wholes)
            d_weights = nt(grads, pair(v, lanes))
            parts = []
            for h in range(4):
                rows = slice(h * QUERY, (h + 1) * QUERY)
                wide, d_weight = weights[0, p, rows, :].astype(F32), d_weights[rows]
                mean = jnp.sum(wide * d_weight, axis=1, keepdims=True)
                parts.append((wide * (d_weight - mean)).astype(BF16))
            g_score = jnp.concatenate(parts, axis=0)
            made = collect(nn(g_score, pair(k, lanes)), halves) * HEAD**-0.5
            first, second = made[:, :LANES], made[:, LANES:]
            gq[:, p * GROUP : p * GROUP + LANES] = (first * c + second * s).astype(BF16)
            gq[:, p * GROUP + LANES : (p + 1) * GROUP] = (second * c - first * s).astype(BF16)
            for total, made in (
                (sum_k, tn(g_score, queries)),
                (sum_v, tn(weights[0, p], grads)),
            ):
                total[0:QUERY, lanes] = total[QUERY:, lanes] + made[0:QUERY]
                total[QUERY:, lanes] = made[QUERY:]

    @pl.when(step == last)
    def _():
        for total in (sum_k, sum_v):
            total[0:QUERY, :] = total[QUERY:, :]

    c, s = table_c[0][...], table_s[0][...]
    for p in range(GROUPS):
        one, two = slice(p * GROUP, p * GROUP + LANES), slice(p * GROUP + LANES, (p + 1) * GROUP)
        first, second = sum_k[0:QUERY, one], sum_k[0:QUERY, two]
        gk[:, one] = (first * c + second * s).astype(BF16)
        gk[:, two] = (second * c - first * s).astype(BF16)
    gv[...] = sum_v[0:QUERY, :].astype(BF16)

    @at_first
    def _():
        for t, total in ((0, sum_k), (1, sum_v)):
            lanes = slice(t * WIDTH, (t + 1) * WIDTH)
            to_low[:, lanes] = total[0:REACH, :].astype(BF16)
            edges[0, :, lanes] = total[REACH:QUERY, :]

    @pl.when(step == last)
    def _():
        for t, total in ((0, sum_k), (1, sum_v)):
            lanes = slice(t * WIDTH, (t + 1) * WIDTH)
            edges[1, :, lanes] = total[0:REACH, :]
            to_high[:, lanes] = total[REACH:QUERY, :].astype(BF16)


def attend_back(q, grad, weights, k, v, cosine, sine):
    tokens = grad.shape[0]
    blocks = tokens // QUERY
    span = QUERY + 2 * REACH
    edge = (REACH, 2 * WIDTH)

    def own(i):
        return jnp.minimum(i, blocks - 1)

    def pairs(width):
        return [
            pl.BlockSpec((QUERY, width), lambda i: (i, 0)),
            pl.BlockSpec((QUERY, width), lambda i: (own(i) + 1, 0)),
        ]

    return call(
        attend_back_kernel,
        (blocks + 1,),
        pairs(WIDTH) * 3
        + pairs(LANES) * 2
        + [
            pl.BlockSpec((QUERY, WIDTH), lambda i: (own(i), 0)),
            pl.BlockSpec((1, GROUPS, 4 * QUERY, span), lambda i: (own(i), 0, 0, 0)),
        ],
        [pl.BlockSpec((QUERY, WIDTH), lambda i: (own(i), 0))]
        + [rows_of(WIDTH, QUERY)] * 2
        + [resident(edge), resident(edge), resident((2,) + edge)],
        [struct((tokens, WIDTH), BF16)]
        + [struct(q.shape, BF16)] * 2
        + [struct(edge, BF16)] * 2
        + [struct((2,) + edge, F32)],
        [pltpu.VMEM((span, WIDTH), F32)] * 2,
        blocks * GROUPS * 2 * 4 * 4 * QUERY * span * GROUP,
        14 * tokens * WIDTH + blocks * GROUPS * 8 * QUERY * span,
        "attend_back",
    )(q, q, k, k, v, v, cosine, cosine, sine, sine, grad, weights)


def edge_kernel(*refs):
    edges, from_low, from_high, cosine, sine = refs[2:7]
    gk, gv = refs[7:]

    def finish(came):
        c, s = cosine[...], sine[...]
        for p in range(GROUPS):
            one = slice(p * GROUP, p * GROUP + LANES)
            two = slice(p * GROUP + LANES, (p + 1) * GROUP)
            first = edges[0, :, one] + came[:, one].astype(F32)
            second = edges[0, :, two] + came[:, two].astype(F32)
            gk[:, one] = (first * c + second * s).astype(BF16)
            gk[:, two] = (second * c - first * s).astype(BF16)
        gv[...] = (edges[0, :, WIDTH:] + came[:, WIDTH:].astype(F32)).astype(BF16)

    pl.when(pl.program_id(0) == 0)(lambda: finish(from_low))
    pl.when(pl.program_id(0) == 1)(lambda: finish(from_high))


def add_edges(gk, gv, edges, from_low, from_high, cosine, sine):
    far = gk.shape[0] // REACH - 3
    rows = pl.BlockSpec((REACH, WIDTH), lambda i: (1 + i * far, 0))
    table = pl.BlockSpec((REACH, LANES), lambda i: (1 + i * far, 0))
    came = resident(from_low.shape)
    return pl.pallas_call(
        edge_kernel,
        grid=(2,),
        in_specs=[pl.BlockSpec(memory_space=pl.ANY)] * 2
        + [pl.BlockSpec((1, REACH, 2 * WIDTH), lambda i: (i, 0, 0)), came, came, table, table],
        out_specs=[rows] * 2,
        out_shape=[struct(gk.shape, BF16)] * 2,
        input_output_aliases={0: 0, 1: 1},
        compiler_params=pltpu.CompilerParams(
            vmem_limit_bytes=VMEM, dimension_semantics=("arbitrary",)
        ),
        cost_estimate=pl.CostEstimate(flops=1, bytes_accessed=2**21, transcendentals=0),
        name="add_edges",
    )(gk, gv, edges, from_low, from_high, cosine, sine)


def step_rows():
    return pl.ds(pl.multiple_of((pl.program_id(0) - GROUPS) * TILE, TILE), TILE)


def between_rows():
    at = (pl.program_id(0) - GROUPS) * TILE + REACH
    return pl.ds(pl.multiple_of(at, REACH), TILE)


def feed_kernel(*refs):
    normed, mixed, weight = refs[0], refs[1], refs[2:4]
    hidden, slope, gelu, early, late, total = refs[4:]
    ff = hidden.shape[2]
    half = GROUPS + total.shape[0] // TILE - 1
    step = pl.program_id(0)

    @pl.when(step < GROUPS)
    def _():
        act = nt(normed[...], joined_rows(weight, 0, slice(0, ff)))
        gate = nt(normed[...], joined_rows(weight, 0, slice(ff, 2 * ff)))
        spread_to = 0.5 * (1.0 + lax.erf(act * math.sqrt(0.5)))
        curve = act * spread_to
        density = jnp.exp(act * act * -0.5) * (1.0 / math.sqrt(2.0 * math.pi))
        slope[0] = (gate * (spread_to + act * density)).astype(BF16)
        gelu[0] = curve.astype(BF16)
        hidden[0] = (curve * gate).astype(BF16)
        add_up(total, hidden, weight, slice(2 * ff, 3 * ff))

    @pl.when((step >= GROUPS) & (step < half))
    def _():
        put_rows(early, mixed[...].astype(F32) + total[step_rows(), :])

    @pl.when(step >= half)
    def _():
        put_rows(late, mixed[...].astype(F32) + total[step_rows(), :])


def units_of(tokens, ff):
    return pl.BlockSpec((1, tokens, ff), lambda i: (group_of(i), 0, 0))


def feed(normed, mixed, weight):
    tokens, ff = normed.shape[0], weight.shape[2] // 3
    last = tokens // TILE - 1
    return call(
        feed_kernel,
        (GROUPS + tokens // TILE,),
        [resident((tokens, WIDTH)), later_rows(WIDTH)] + weight_rows(3 * ff),
        [units_of(tokens, ff)] * 3
        + [
            pl.BlockSpec(
                (SLOTS, TILE, 256), lambda i: (0, jnp.clip(i - GROUPS, 0, last - 1), 0)
            ),
            resident((SLOTS, TILE, 256)),
        ],
        [struct((GROUPS, tokens, ff), BF16)] * 3
        + [struct((SLOTS, tokens - TILE, 256), BF16), struct((SLOTS, TILE, 256), BF16)],
        [pltpu.VMEM((tokens, WIDTH), F32)],
        2 * tokens * WIDTH * 3 * GROUPS * ff,
        6 * tokens * WIDTH + 6 * GROUPS * ff * (tokens + WIDTH),
        "feed",
    )(normed, mixed, weight, weight)


def feed_back_kernel(*refs):
    cots, slope, gelu, mixed, gain = refs[:5]
    weight, outward = refs[5:7], refs[7:9]
    g_act, g_gate, g_branch, g_attended, gain_part, cot, total = refs[9:]
    ff = g_act.shape[2]

    @at_first
    def _():
        cot[...] = whole_rows(cots)

    @pl.when(pl.program_id(0) < GROUPS)
    def _():
        g_hidden = nt(cot[...], joined_rows(weight, 0, slice(2 * ff, 3 * ff)))
        g_act[0] = (g_hidden * slope[0].astype(F32)).astype(BF16)
        g_gate[0] = (g_hidden * gelu[0].astype(F32)).astype(BF16)
        add_up(total, g_act, weight, slice(0, ff))
        total[...] += nn(g_gate[0], joined_rows(weight, 0, slice(ff, 2 * ff)))

    @pl.when(pl.program_id(0) >= GROUPS)
    def _():
        gradient = total[step_rows(), :]
        unit, inverse = norm(mixed[...].astype(F32))
        add_gain(gain_part, gradient * unit)
        made = cot[step_rows(), :].astype(F32) + norm_back(gradient, unit, inverse, gain[...])
        branch = made.astype(BF16)
        g_branch[...] = branch
        for p in range(GROUPS):
            lanes = slice(p * GROUP, (p + 1) * GROUP)
            g_attended[:, lanes] = nt(branch, joined_rows(outward, p)).astype(BF16)


def feed_back(cots, slope, gelu, mixed, gain, weight, heads):
    _, tokens, ff = slope.shape
    return call(
        feed_back_kernel,
        (GROUPS + tokens // TILE,),
        [resident(cots.shape)]
        + [units_of(tokens, ff)] * 2
        + [later_rows(WIDTH), resident((1, WIDTH))]
        + weight_rows(3 * ff)
        + out_weight(),
        [units_of(tokens, ff)] * 2 + [later_rows(WIDTH)] * 2 + [resident((8, WIDTH))],
        [struct((GROUPS, tokens, ff), BF16)] * 2
        + [struct((tokens, WIDTH), BF16)] * 2
        + [struct((8, WIDTH), F32)],
        [pltpu.VMEM((tokens, WIDTH), BF16), pltpu.VMEM((tokens, WIDTH), F32)],
        2 * tokens * WIDTH * (3 * GROUPS * ff + WIDTH),
        8 * tokens * WIDTH + 6 * GROUPS * ff * (tokens + WIDTH),
        "feed_back",
    )(cots, slope, gelu, mixed, gain, weight, weight, heads, heads)


def unproject_kernel(*refs):
    xs, gq, gk, gv, g_branch, gain, low, high, outs, gain_part, held, total = refs
    @pl.when(pl.program_id(0) < GROUPS)
    def _():
        own = pl.ds(REACH, gq.shape[0])
        held[0] = jnp.concatenate([gq[...], gk[own, :], gv[own, :]], axis=1)
        add_up(total, held, (low, high))

    @pl.when(pl.program_id(0) >= GROUPS)
    def _():
        gradient = total[step_rows(), :]
        unit, inverse = norm(whole_rows(xs, between_rows()).astype(F32))
        add_gain(gain_part, gradient * unit)
        made = g_branch[...].astype(F32) + norm_back(gradient, unit, inverse, gain[...])
        put_rows(outs, made)


def unproject(xs, gq, gk, gv, g_branch, gain, weight):
    tokens = gq.shape[0]
    return call(
        unproject_kernel,
        (GROUPS + tokens // TILE,),
        [resident(xs.shape)]
        + [
            pl.BlockSpec((value.shape[0], GROUP), lambda i: (0, group_of(i)))
            for value in (gq, gk, gv)
        ]
        + [later_rows(WIDTH), resident((1, WIDTH))]
        + weight_rows(3 * GROUP),
        [LATER_BLOCKS, resident((8, WIDTH))],
        [struct((SLOTS, tokens, 256), BF16), struct((8, WIDTH), F32)],
        [pltpu.VMEM((1, tokens, 3 * GROUP), BF16), pltpu.VMEM((tokens, WIDTH), F32)],
        2 * tokens * WIDTH * 3 * WIDTH,
        12 * tokens * WIDTH + 6 * WIDTH * WIDTH,
        "unproject",
    )(xs, gq, gk, gv, g_branch, gain, weight, weight)


def outer_kernel(count, tokens, *refs):
    inner, outer, out = refs[:count], refs[count : 2 * count], refs[-1]

    def own_rows(value):
        return value[pl.ds((value.shape[0] - tokens) // 2, tokens), :]

    def make(left, right):
        left = left[0] if len(left.shape) == 3 else own_rows(left)
        right = whole_rows(right) if len(right.shape) == 3 else own_rows(right)
        made = tn(left, right)
        many, width = out.shape[1], out.shape[3]
        for j in range(many):
            rows = slice(j * width, (j + 1) * width)
            for a in range(2):
                for o in range(SLOTS):
                    at = o * 256 + a * LANES
                    out[a, j, o] = made[rows, at : at + LANES].astype(BF16)

    for t in range(count):
        pl.when(pl.program_id(0) % count == t)(functools.partial(make, inner[t], outer[t]))


def outer_product(tokens, inner, outer, places, kinds, base=None):
    count = len(inner)
    width = inner[0].shape[2] if inner[0].ndim == 3 else GROUP
    stride = places[-1] - places[0]
    many = 1 if inner[0].ndim == 3 else 2

    def inner_block(value):
        if value.ndim == 3:
            return pl.BlockSpec((1, tokens, width), lambda i: (i // count, 0, 0))
        return pl.BlockSpec((value.shape[0], many * GROUP), lambda i: (0, i // count))

    more = [] if base is None else [base]
    moved = 8 * count * width * (tokens + WIDTH) + 2 * tokens * WIDTH
    return pl.pallas_call(
        functools.partial(outer_kernel, count, tokens),
        grid=(GROUPS // many * count,),
        in_specs=[inner_block(value) for value in inner]
        + [resident(value.shape) for value in outer]
        + [pl.BlockSpec(memory_space=pl.ANY) for _ in more],
        out_specs=pl.BlockSpec(
            (2, many, SLOTS, width, LANES),
            lambda i: (0, i // count, 0, places[0] + i % count * stride, 0),
        ),
        out_shape=struct((2, GROUPS, SLOTS, kinds * width, LANES), BF16),
        input_output_aliases={2 * count: 0} if more else {},
        compiler_params=pltpu.CompilerParams(
            vmem_limit_bytes=VMEM, dimension_semantics=("arbitrary",)
        ),
        cost_estimate=pl.CostEstimate(
            flops=2 * tokens * GROUPS * count * width * WIDTH,
            bytes_accessed=moved,
            transcendentals=0,
        ),
        name="outer_product",
    )(*inner, *outer, *more)


def over_dp(value):
    return lax.ppermute(value, "dp", [(0, 1), (1, 0)])


def over_chip(value):
    return lax.ppermute(value, "col", [(i, i ^ 2) for i in range(4)])


def over_core(value):
    return lax.ppermute(value, "col", [(i, i ^ 1) for i in range(4)])


def exchange(value):
    return lax.all_to_all(value, "row", 0, 0)


def after(value, *earlier):
    return lax.optimization_barrier((value,) + earlier)[0]


def own_half(shard):
    return lax.dynamic_slice_in_dim(shard, lax.axis_index("dp") * LANES, LANES, 1)


def gather_rows(half):
    return exchange(jnp.broadcast_to(half, (SLOTS,) + half.shape))


def gather_groups(own):
    return lax.all_gather(own, ("dp", "col"), axis=0, tiled=False)


def reduce_groups(parts):
    parts = parts.reshape((2 * GROUPS,) + parts.shape[2:])
    return lax.psum_scatter(parts, ("dp", "col"), scatter_dimension=0, tiled=False)


def sum_rows(parts):
    half = jnp.sum(parts.astype(F32), axis=0).astype(BF16)
    return lax.axis_index("dp").reshape(1), half, over_dp(half)


def finish_kernel(kinds, width, which, mine, other, *outs):
    low_is_mine = jnp.full((width, LANES), which[0]) == 0
    for t, (kind, out) in enumerate(zip(kinds, outs, strict=True)):
        rows = slice(t * width, (t + 1) * width)
        one, two = mine[rows, :].astype(F32), other[rows, :].astype(F32)
        value = jnp.concatenate(
            [jnp.where(low_is_mine, one, two), jnp.where(low_is_mine, two, one)], axis=1
        )
        if kind not in "qkv":
            out[...] = value
            continue
        if kind in "qk":
            cuts = [value[at * 32 : (at + 1) * 32] for at in (0, 4, 1, 5, 2, 6, 3, 7)]
            value = jnp.concatenate(cuts, axis=0)
        out[...] = value.T


def finish(halves, kinds, width):
    return pl.pallas_call(
        functools.partial(finish_kernel, kinds, width),
        in_specs=[
            pl.BlockSpec(memory_space=space) for space in (pltpu.SMEM, pltpu.VMEM, pltpu.VMEM)
        ],
        out_shape=[struct((256, width) if kind in "qkv" else (width, 256), F32) for kind in kinds],
        compiler_params=pltpu.CompilerParams(vmem_limit_bytes=VMEM),
        cost_estimate=pl.CostEstimate(flops=1, bytes_accessed=2**21, transcendentals=0),
        name="finish",
    )(*halves)


def sum_gains(parts):
    both = parts + over_dp(parts)
    both = both + over_chip(both)
    both = both + over_core(both)
    for bit in (1, 2):
        both = both + lax.ppermute(both, "row", [(i, i ^ bit) for i in range(SLOTS)])
    return lax.dynamic_slice_in_dim(both, lax.axis_index("row") * 256, 256, 1)


def groups_of(whole):
    rows = whole.shape[0] // GROUPS
    cut = whole.reshape(GROUPS, rows, SLOTS, 2, LANES).transpose(3, 0, 2, 1, 4)
    return cut.reshape(2 * GROUPS, SLOTS, rows, LANES)


def whole_of(parts, types):
    cut = parts.transpose(1, 3, 2, 0, 4).reshape(GROUPS, types, -1, WIDTH)
    return [cut[:, t].reshape(-1, WIDTH) for t in range(types)]


def split_heads(rows):
    return rows.reshape(-1, 4, 2, 32, rows.shape[1]).swapaxes(1, 2).reshape(rows.shape)


def join_heads(rows):
    return rows.reshape(-1, 2, 4, 32, rows.shape[1]).swapaxes(1, 2).reshape(rows.shape)


def positions_and_masks(segments, valid, first, tokens):
    length = segments.shape[0]
    index = first - REACH + jnp.arange(tokens + 2 * REACH, dtype=jnp.int32)
    pads = (REACH, REACH)
    near = lax.dynamic_slice_in_dim(jnp.pad(segments, pads), first, tokens + 2 * REACH, 0)
    ids = jnp.arange(64, dtype=jnp.int32)
    before = jnp.sum((segments[None, :] < ids[:, None]).astype(jnp.int32), axis=1)
    begin = jnp.sum(jnp.where(near[:, None] == ids[None, :], before[None, :], 0), axis=1)
    where_in = (index - begin).astype(F32)
    frequency = ROPE_THETA ** (-((jnp.arange(LANES) % 32).astype(F32) * 2.0) / HEAD)
    angles = where_in[:, None] * frequency[None, :]
    code = jnp.pad(jnp.where(valid == 1, segments, -1), pads, constant_values=-1)
    code = lax.dynamic_slice_in_dim(code, first, tokens + 2 * REACH, 0)
    span = QUERY + 2 * REACH
    keys = jnp.stack([code[i : i + span] for i in range(0, tokens, QUERY)])[:, None, :]
    queries = near[REACH:-REACH].reshape(-1, QUERY, 1)
    shape = (tokens // QUERY, QUERY, span)
    offset = (
        lax.broadcasted_iota(jnp.int32, shape, 2)
        - lax.broadcasted_iota(jnp.int32, shape, 1)
        - REACH
    )
    allowed = (jnp.abs(offset) <= REACH) & ((queries == keys) | (offset == 0))
    return jnp.cos(angles), jnp.sin(angles), jnp.where(allowed, 0.0, MASKED_SCORE).astype(F32)


def body(
    dp,
    rows,
    cols,
    tokens_in,
    w_query,
    w_key,
    w_value,
    w_out,
    w_act,
    w_gate,
    w_down,
    gain_attn,
    gain_ffn,
    cotangent,
    segment_ids,
    valid_mask,
):
    tokens = tokens_in.shape[0] // rows
    length = segment_ids.shape[1]
    own_slice = (dp, rows, cols) == (2, 4, 4) and rows * tokens == length
    gains = jnp.stack([gain_attn, gain_ffn])
    at = (lax.axis_index("col") * rows + lax.axis_index("row")) * tokens
    sequence, first = at // length, at % length
    count = rows * cols
    joins = [i for i in range(count - 1) if ((i + 1) * tokens) % length]
    upward, downward = [(i, i + 1) for i in joins], [(i + 1, i) for i in joins]

    def shift(value, perm):
        place_of = [(i % rows) * cols + i // rows for i in range(count)]
        return lax.ppermute(value, ("row", "col"), [(place_of[i], place_of[j]) for i, j in perm])

    if own_slice:
        marks = jnp.concatenate([segment_ids, valid_mask]).astype(BF16).reshape(-1, LANES)
        heads_half = jnp.concatenate(
            [
                split_heads(own_half(w_query.T)),
                split_heads(own_half(w_key.T)),
                own_half(w_value.T),
                own_half(w_out),
                marks,
                gains.reshape(4, LANES),
                jnp.zeros((12, LANES), BF16),
            ],
            axis=0,
        )
        feed_half = jnp.concatenate(
            [own_half(w_act.T), own_half(w_gate.T), own_half(w_down)], axis=0
        )
        padded = jnp.pad(tokens_in, ((REACH, REACH), (0, 0)))
        spans = [padded[j * tokens : (j + 1) * tokens + 2 * REACH] for j in range(rows)]
        heads_own = gather_rows(heads_half)
        heads_w = gather_groups(heads_own[:, :WIDTH])
        spans = jnp.stack(spans)
        feed_own = gather_rows(after(feed_half, heads_own, spans))
        feed_w = gather_groups(feed_own)
        last = WIDTH + marks.shape[0]
        marks = heads_own[:, WIDTH:last].reshape(rows, 2, length)
        marks = lax.dynamic_index_in_dim(marks, sequence, 0, False).astype(jnp.int32)
        gain_slots = heads_own[:, last : last + 4].reshape(SLOTS, 2, 256)
        tables = positions_and_masks(*marks, first, tokens)
        xs = exchange(after(spans, feed_own))
        cots = exchange(after(cotangent.reshape(rows, tokens, 256), xs))
    else:
        xs = exchange(tokens_in.reshape(rows, tokens, 256))
        below, above = shift(xs[:, -REACH:], upward), shift(xs[:, :REACH], downward)
        xs = jnp.concatenate([below, xs, above], axis=1)
        cots = exchange(cotangent.reshape(rows, tokens, 256))
        gain_slots = exchange(jnp.broadcast_to(gains, (rows, 2, 256)))
        marks = lax.all_gather(jnp.stack([segment_ids, valid_mask]), "row", axis=1, tiled=True)
        marks = lax.dynamic_index_in_dim(marks, sequence, 1, False)
        tables = positions_and_masks(*marks, first, tokens)

        def full(value, inner_first):
            first, second = ("col", "row") if inner_first else ("row", "col")
            value = lax.all_gather(value, first, axis=0, tiled=True)
            value = lax.all_gather(value, second, axis=1, tiled=True)
            return value if inner_first else value.T

        def joined(*parts):
            return jnp.concatenate([groups_of(part) for part in parts], axis=2)

        heads_w = joined(
            split_heads(full(w_query, False)),
            split_heads(full(w_key, False)),
            full(w_value, False),
            full(w_out, True),
        )
        feed_w = joined(full(w_act, False), full(w_gate, False), full(w_down, True))
    gain_rows = gain_slots.swapaxes(0, 1).reshape(2, 1, WIDTH).astype(F32)
    cosine, sine, bias = tables

    q, k, v, normed_attn = project(xs, gain_rows[0], cosine, sine, heads_w)
    attended, weights, mixed, normed_ffn = attend(q, k, v, bias, xs, gain_rows[1], heads_w)
    hidden, slope, gelu, early, late = feed(normed_ffn, mixed, feed_w)
    early = exchange(after(early, cots))
    down_parts = outer_product(tokens, [hidden], [cots], (0,), 1)
    g_act, g_gate, g_branch, g_attended, gain_part_ffn = feed_back(
        cots, after(slope, down_parts), gelu, mixed, gain_rows[1], feed_w, heads_w
    )
    up_parts = outer_product(tokens, [after(g_act, early), g_gate], [normed_ffn] * 2, (0, 1), 2)
    if own_slice:
        down_own, up_own = reduce_groups(down_parts), reduce_groups(up_parts)
        g_attended = after(g_attended, up_parts, down_own)
    gq, gk, gv, to_low, to_high, edges = attend_back(
        q, g_attended, weights, k, v, cosine, sine
    )
    from_low, from_high = shift(to_high, upward), shift(to_low, downward)
    if own_slice:
        rest = down_own.reshape(rows, -1, 256)
        late, rest = jnp.split(
            exchange(jnp.concatenate([after(late, early), rest], axis=1)), [TILE], axis=1
        )
        down_sum = rest.reshape(down_own.shape)
    else:
        late = exchange(late)
    layer_out = jnp.concatenate([early, late], axis=1)
    heads_parts = outer_product(tokens, [gq, attended], [normed_attn, g_branch], (0, 3), 4)
    from_low = after(from_low, heads_parts)
    if own_slice:
        from_low = after(from_low, late, down_sum)
    gk, gv = add_edges(gk, gv, edges, from_low, from_high, cosine, sine)
    grad_slots, gain_part_attn = unproject(
        xs, gq, gk, gv, g_branch, gain_rows[0], heads_w
    )
    heads_parts = outer_product(
        tokens, [after(gk, grad_slots), gv], [normed_attn] * 2, (1, 2), 4, heads_parts
    )
    token_gradient = exchange(after(grad_slots, late))

    gain_parts = jnp.stack([jnp.sum(gain_part_attn, axis=0), jnp.sum(gain_part_ffn, axis=0)])
    if own_slice:
        up_sum = exchange(after(up_own, token_gradient))
        gain_grads = sum_gains(gain_parts)
        heads_sum = exchange(after(reduce_groups(heads_parts), up_sum, gain_grads))
        ff = w_act.shape[1]
        grads = (
            *finish(sum_rows(heads_sum), "qkvo", GROUP),
            *(value.T for value in finish(sum_rows(up_sum), "ag", ff)),
            *finish(sum_rows(down_sum), "d", ff),
        )
    else:

        def share(value, inner_first):
            first, second = ("col", "row") if inner_first else ("row", "col")
            value = value if inner_first else value.T
            value = lax.psum_scatter(value, first, scatter_dimension=0, tiled=True)
            value = lax.psum_scatter(value, second, scatter_dimension=1, tiled=True)
            return lax.psum(value, "dp").astype(F32)

        (down_whole,) = whole_of(down_parts, 1)
        act_whole, gate_whole = whole_of(up_parts, 2)
        query_whole, key_whole, value_whole, out_whole = whole_of(heads_parts, 4)
        grads = (
            share(join_heads(query_whole), False),
            share(join_heads(key_whole), False),
            share(value_whole, False),
            share(out_whole, True),
            share(act_whole, False),
            share(gate_whole, False),
            share(down_whole, True),
        )
        totals = lax.psum(gain_parts, ("dp", "row", "col")).reshape(2, SLOTS, 256)
        gain_grads = lax.dynamic_index_in_dim(totals, lax.axis_index("row"), 1, False)
    layer_out = layer_out.reshape(-1, 256)
    token_gradient = token_gradient.reshape(-1, 256).astype(F32)
    return (layer_out, token_gradient) + grads + (gain_grads[0], gain_grads[1])


def solution(mesh):
    sizes = tuple(mesh.shape[axis] for axis in ("dp", "row", "col"))
    in_specs = (
        P(("dp", "col"), "row"),
        P("row", "col"),
        P("row", "col"),
        P("row", "col"),
        P("col", "row"),
        P("row", "col"),
        P("row", "col"),
        P("col", "row"),
        P("row"),
        P("row"),
        P(("dp", "col"), "row"),
        P(("dp", "row"), None),
        P(("dp", "row"), None),
    )
    out_specs = (
        P(("dp", "col"), "row"),
        P(("dp", "col"), "row"),
        P("row", "col"),
        P("row", "col"),
        P("row", "col"),
        P("col", "row"),
        P("row", "col"),
        P("row", "col"),
        P("col", "row"),
        P("row"),
        P("row"),
    )
    return jax.shard_map(
        functools.partial(body, *sizes),
        mesh=mesh,
        in_specs=in_specs,
        out_specs=out_specs,
        check_vma=False,
    )
```
